32 devices in a mesh: groups: 2 (over y), boxes: 4 (over z), sub: 2 (over x), pair: 2 (over core).
Axes of the slice: x: 2, y: 2, z: 4, core: 2. Of those that a mesh axis runs over, the one named last changes fastest.
Arguments:
- phase: float32 [256, 128, 256], P(('groups', 'boxes'), 'sub', 'pair'), parts along dimension 0, may hold values from 0 to 1
- target_mask: int32 [256, 128, 256], P(('groups', 'boxes'), 'sub', 'pair'), parts along dimension 0, may hold values 0 or 1
- deviation: float32 [256, 128, 256], P(('groups', 'boxes'), 'sub', 'pair'), parts along dimension 0, may hold values from -12 to 12
Outputs:
- adjoint_field: float32 [256, 128, 256], P(('groups', 'boxes'), 'sub', 'pair'), parts along dimension 0
- residual: float32 [256, 128, 256], P(('groups', 'boxes'), 'sub', 'pair'), parts along dimension 0
The draws below stay inside these ranges and needn't reach their ends.
There are 2 independent parts, one for each index of `groups`. The reference program is written for one: setup_inputs(seed, part) draws one part's arguments, and reference() takes and returns one part's arrays. A program takes and returns all parts, laid end to end along the dimension named above; each array names one. Nothing has to cross between parts.
All inputs are finite; a program needn't handle non-finite values. No bound on the sum of `target_mask` on one device may be relied on, other than what follows from the above.
Results may differ from the reference program's by a relative error of at most 0.00011.
Values sent between devices are 32-bit elements; how exact they have to be, the bound alone decides.
No kernel may reach another device: no remote copies, remote signals or barrier semaphores. Data moves between devices by JAX's collectives and lax.ppermute only.
A program may use at most 320 MiB of HBM per device.

```python
import jax
import jax.numpy as jnp

SWEEPS = 2
BOTTOM_SWEEPS = 8
NX = 128
NY = 128
NZ = 256


def draw_deviation(key, part):
    key = jax.random.fold_in(key, 7)
    rough = jax.random.normal(key, (NX, NY, NZ), jnp.float32)
    return 3.0 * jnp.clip(rough, -4.0, 4.0)


def touch_ends(drawn, own_key, least, high):
    shape = drawn.shape
    place = [jax.random.randint(jax.random.fold_in(own_key, axis), (), 0, shape[axis]) for axis in range(len(shape))]
    drawn = drawn.at[tuple(place)].set(least)
    longest = shape.index(max(shape))
    place[longest] = (place[longest] + 1) % shape[longest]
    return drawn.at[tuple(place)].set(high)


def steps_of(stream_key, shape, cuts, low, largest):
    def one(dim, shards_of):
        steps = jax.random.uniform(jax.random.fold_in(jax.random.fold_in(stream_key, 6), dim), (shards_of,), jnp.float32, low / len(cuts), largest / len(cuts))
        return jnp.repeat(jnp.exp(steps), shape[dim] // shards_of).reshape((-1,) + (1,) * (len(shape) - dim - 1))

    loudness = one(*cuts[0])
    for cut in cuts[1:]:
        loudness = loudness * one(*cut)
    return loudness


def setup_inputs(seed: int = 0, part: int = 0) -> dict:
    seeds = jax.random.split(jax.random.key(seed), 4)
    part_splits = jax.random.split(jax.random.fold_in(seeds[3], part), 4)
    return {
        "phase": jnp.clip(1.0 * jax.random.uniform(part_splits[0], (NX, NY, NZ), jnp.float32) ** steps_of(part_splits[0], (NX, NY, NZ), ((0, 4), (1, 2), (2, 2)), -0.2, 0.2), 0.0, 1.0),
        "target_mask": touch_ends((jax.random.randint(part_splits[1], (NX, NY, NZ), 0, 2) < 1).astype(jnp.int32), jax.random.fold_in(part_splits[1], 1), 0, 1),
        "deviation": draw_deviation(jax.random.fold_in(jax.random.fold_in(seeds[3], part), 71), part),
    }


floor_conduct = 0.1
relax_weight = 0.8


def conduct(phase):
    return floor_conduct + (1.0 - floor_conduct) * (phase * phase * phase)


def coarsen(field):
    size_a, size_b, size_c = field.shape
    blocks = field.reshape(size_a // 2, 2, size_b // 2, 2, size_c // 2, 2)
    return jnp.mean(blocks, axis=(1, 3, 5))


def refine(field):
    return jnp.repeat(jnp.repeat(jnp.repeat(field, 2, axis=0), 2, axis=1), 2, axis=2)


def neighbours(padded):
    return [padded[2:, 1:-1, 1:-1], padded[:-2, 1:-1, 1:-1],
            padded[1:-1, 2:, 1:-1], padded[1:-1, :-2, 1:-1],
            padded[1:-1, 1:-1, 2:], padded[1:-1, 1:-1, :-2]]


def face_terms(loop):
    center = loop[1:-1, 1:-1, 1:-1]
    return [0.5 * (center + other) for other in neighbours(loop)]


def diagonal_of(faces, scale):
    total = faces[0]
    for other in faces[1:]:
        total = total + other
    return total * scale


def operate(padded, faces, scale):
    center = padded[1:-1, 1:-1, 1:-1]
    others = neighbours(padded)
    total = faces[0] * (center - others[0])
    for index in range(1, 6):
        total = total + faces[index] * (center - others[index])
    return total * scale


def relax_sweep(field, source, faces, diagonal, scale):
    padded = jnp.pad(field, 1)
    return field + relax_weight * (source - operate(padded, faces, scale)) / diagonal


def smooth(field, source, faces, diagonal, scale, count):
    for repeat in range(count):
        field = relax_sweep(field, source, faces, diagonal, scale)
    return field


def reference(phase, target_mask, deviation):
    cond0 = conduct(phase)
    cond1 = coarsen(cond0)
    cond2 = coarsen(cond1)
    faces0 = face_terms(jnp.pad(cond0, 1))
    faces1 = face_terms(jnp.pad(cond1, 1))
    faces2 = face_terms(jnp.pad(cond2, 1))
    diag0 = diagonal_of(faces0, 1.0)
    diag1 = diagonal_of(faces1, 0.25)
    diag2 = diagonal_of(faces2, 0.0625)
    source = target_mask.astype(jnp.float32) * deviation
    field0 = relax_weight * source / diag0
    field0 = smooth(field0, source, faces0, diag0, 1.0, SWEEPS - 1)
    rest0 = source - operate(jnp.pad(field0, 1), faces0, 1.0)
    source1 = coarsen(rest0)
    field1 = relax_weight * source1 / diag1
    field1 = smooth(field1, source1, faces1, diag1, 0.25, SWEEPS - 1)
    rest1 = source1 - operate(jnp.pad(field1, 1), faces1, 0.25)
    source2 = coarsen(rest1)
    field2 = relax_weight * source2 / diag2
    field2 = smooth(field2, source2, faces2, diag2, 0.0625, BOTTOM_SWEEPS - 1)
    field1 = field1 + refine(field2)
    field1 = smooth(field1, source1, faces1, diag1, 0.25, SWEEPS)
    field0 = field0 + refine(field1)
    field0 = smooth(field0, source, faces0, diag0, 1.0, SWEEPS)
    residual = source - operate(jnp.pad(field0, 1), faces0, 1.0)
    return field0, residual
```

```python
import jax
import jax.numpy as jnp
from jax import lax
from jax.experimental import pallas as pl
from jax.experimental.pallas import tpu as pltpu
from jax.sharding import PartitionSpec as P

SWEEPS = 2
BOTTOM_SWEEPS = 8

floor_conduct = 0.1
relax_weight = 0.8

XH = 8
YH = 16
GX = 6
DC, DG = 6, 5
ZW = 16
L2X = 10
HI = lax.Precision.HIGHEST
F32 = jnp.float32
MIB = 1 << 20


def exchanges(count, step=1):
    swaps = []
    for e in range(2):
        pairs = []
        for i in range(count):
            if (i // step + e) % 2 == 0 and i + step < count:
                pairs += [(i, i + step), (i + step, i)]
        if pairs:
            swaps.append(pairs)
    return swaps


def upward(index, e, step=1):
    return ((index // step) + e) % 2 == 0


def spec(shape):
    return jax.ShapeDtypeStruct(shape, F32)


def in_vmem(shape):
    return pltpu.VMEM(shape, F32)


def held(x):
    return pltpu.with_memory_space_constraint(x, pltpu.VMEM)


def params(mib):
    return pltpu.CompilerParams(vmem_limit_bytes=mib * MIB)


def roll_up(v, axis):
    return pltpu.roll(v, v.shape[axis] - 1, axis)


def roll_down(v, axis):
    return pltpu.roll(v, 1, axis)


def loop(low, high, body, init=None):
    if init is None:

        def plain(i, carry):
            body(i)
            return carry

        lax.fori_loop(low, high, plain, 0)
        return None
    return lax.fori_loop(low, high, body, init)


def coefficients(c, kx, ky, kz, rd, low, high, scale):
    half = 0.5 * scale

    def faces(x):
        cx = c[x]
        fx = half * (cx + c[x + 1])
        fy = half * (cx + roll_up(cx, 0))
        fz = half * (cx + roll_up(cx, 1))
        kx[x] = fx
        ky[x] = fy
        kz[x] = fz
        return cx, fx, fy, fz

    _, first, _, _ = faces(low - 1)

    def body(x, before):
        cx, fx, fy, fz = faces(x)
        diagonal = fx + before + fy + roll_down(fy, 0) + fz + roll_down(fz, 1)
        inside = cx > 0.0
        rd[x] = jnp.where(inside, relax_weight / jnp.where(inside, diagonal, 1.0), 0.0)
        return fx

    loop(low, high, body, first)


def operate(v, kx, ky, kz, low, high, use):
    def body(x, before):
        vx = v[x]
        fx = kx[x] * (vx - v[x + 1])
        fy = ky[x] * (vx - roll_up(vx, 0))
        fz = kz[x] * (vx - roll_up(vx, 1))
        use(x, vx, (fx - before) + (fy - roll_down(fy, 0)) + (fz - roll_down(fz, 1)))
        return fx

    loop(low, high, body, kx[low - 1] * (v[low - 1] - v[low]))


def sweep(v, out, g, kx, ky, kz, rd, low, high):
    def use(x, vx, av):
        out[x] = vx + rd[x] * (g[x] - av)

    operate(v, kx, ky, kz, low, high, use)


def iota2(shape, dim):
    return lax.broadcasted_iota(jnp.int32, shape, dim)


def send_kernel(nx, ny, phase, mask, dev, c_out, g_out, *outs):
    ox, oy, _ = phase.shape

    def body(x):
        p = phase[x]
        c_out[x] = floor_conduct + (1.0 - floor_conduct) * (p * p * p)
        g_out[x] = mask[x].astype(F32) * dev[x]

    loop(0, ox, body)
    bx = lax.axis_index("boxes")
    sy = lax.axis_index("sub")
    place = 0
    rows = [pl.ds(pl.multiple_of(jnp.where(upward(sy, f), oy - YH, 0), 8), YH) for f in range(ny)]
    for e in range(nx):
        up = upward(bx, e)
        face = outs[place]
        place += 1
        face[0:XH] = c_out[pl.ds(jnp.where(up, ox - XH, 0), XH)]
        face[XH:XH + GX] = g_out[pl.ds(jnp.where(up, ox - GX, 0), GX)]
    for f in range(ny):
        face = outs[place]
        place += 1
        face[0] = c_out[:, rows[f], :]
        face[1] = g_out[:, rows[f], :]
    for e in range(nx):
        up = upward(bx, e)
        for f in range(ny):
            face = outs[place]
            place += 1
            face[0:DC] = c_out[pl.ds(jnp.where(up, ox - DC, 0), DC), rows[f], :]
            face[DC:DC + DG] = g_out[pl.ds(jnp.where(up, ox - DG, 0), DG), rows[f], :]


def halo_rows(ny, f, oy, up):
    if ny == 1:
        return oy
    return jnp.where(up, oy, oy + YH)


def extend_kernel(nx, ny, c, g, *refs):
    count = nx + ny + nx * ny
    got, (c_out, g_out, strip) = refs[:count], refs[count:]
    ox, oy, oz = c.shape
    bx = lax.axis_index("boxes")
    sy = lax.axis_index("sub")
    pz = lax.axis_index("pair")
    c_out[...] = jnp.zeros_like(c_out)
    g_out[...] = jnp.zeros_like(g_out)
    c_out[XH:XH + ox, 0:oy, :] = c[...]
    g_out[XH:XH + ox, 0:oy, :] = g[...]
    place = 0
    row = iota2((YH, oz), 0)

    def trim(values, up):
        if ny > 1:
            return values
        return jnp.where(lax.div(row, 2) == jnp.where(up, YH // 2 - 1, 0), 0.0, values)

    def below(up, planes):
        return jnp.where(up, XH + ox, XH - planes)

    for e in range(nx):
        up = upward(bx, e)
        face = got[place]
        place += 1
        c_out[pl.ds(below(up, XH), XH), 0:oy, :] = face[0:XH]
        g_out[pl.ds(below(up, GX), GX), 0:oy, :] = face[XH:XH + GX]
    for f in range(ny):
        up = upward(sy, f)
        face = got[place]
        place += 1
        rows = pl.ds(pl.multiple_of(halo_rows(ny, f, oy, up), 8), YH)

        def copy(x, face=face, rows=rows, up=up):
            c_out[XH + x, rows, :] = trim(face[0, x], up)
            g_out[XH + x, rows, :] = trim(face[1, x], up)

        loop(0, ox, copy)
    for e in range(nx):
        ux = upward(bx, e)
        for f in range(ny):
            up = upward(sy, f)
            face = got[place]
            place += 1
            rows = pl.ds(pl.multiple_of(halo_rows(ny, f, oy, up), 8), YH)
            for x in range(DC):
                c_out[below(ux, DC) + x, rows, :] = trim(face[x], up)
            for x in range(DG):
                g_out[below(ux, DG) + x, rows, :] = trim(face[DC + x], up)
    group = oz // ZW
    nrows = c_out.shape[1]
    lane = iota2((nrows, oz), 1)
    start = jnp.where(pz == 0, oz - ZW, 0)
    packed = c_out.shape[0] // group

    def pack(a):
        for which, source in enumerate((c_out, g_out)):
            total = None
            for b in range(group):
                moved = pltpu.roll(source[group * a + b], lax.rem(ZW * b + oz - start, oz), 1)
                total = moved if total is None else jnp.where(lane >= ZW * b, moved, total)
            strip[which * packed + a] = total

    loop(0, packed, pack)


def pool(source, low, high, out, matrix, work, rows, first):
    half = rows // 2

    def body(j):
        work[...] = jnp.dot(source(2 * j) + source(2 * j + 1), matrix, precision=HI, preferred_element_type=F32)
        out[j - first] = work[pl.ds(0, half, stride=2), :] + work[pl.ds(1, half, stride=2), :]

    loop(low, high, body)


def pool_matrix(size_in, size_out, limit, shift, weight):
    i, j = iota2((size_in, size_out), 0), iota2((size_in, size_out), 1)
    return jnp.where((i < limit) & (j == shift + lax.div(i, 2)), weight, 0.0).astype(F32)


def down_kernel(nx, cpad, gpad, strip, *refs):
    kx, ky, kz, rd, g, u0, kx1, ky1, kz1, rd1, c1, f1, u1, f2 = refs[:14]
    faces = refs[14:14 + nx]
    c, first, v1, work, work1 = refs[14 + nx:]
    planes, rows, oz = cpad.shape
    pz = lax.axis_index("pair")
    bx = lax.axis_index("boxes")
    group = oz // ZW
    packed = planes // group
    lane = iota2((rows, oz), 1)
    start = jnp.where(pz == 0, 0, oz - ZW)
    near = (lane >= start) & (lane < start + ZW)

    def unpack(a):
        cs, gs = strip[a], strip[packed + a]
        for b in range(group):
            x = group * a + b
            turn = lax.rem(start + oz - ZW * b, oz)
            c[x, :, 0:oz] = cpad[x]
            g[x, :, 0:oz] = gpad[x]
            c[x, :, oz:] = jnp.where(near, pltpu.roll(cs, turn, 1), 0.0)
            g[x, :, oz:] = jnp.where(near, pltpu.roll(gs, turn, 1), 0.0)

    loop(0, packed, unpack)
    edge = XH - GX
    coefficients(c, kx, ky, kz, rd, edge, planes - edge, 1.0)

    def start_sweep(x):
        first[x] = g[x] * rd[x]

    loop(edge, planes - edge, start_sweep)
    sweep(first, u0, g, kx, ky, kz, rd, edge + 1, planes - edge - 1)
    rest = first

    def use(x, vx, av):
        rest[x] = g[x] - av

    operate(u0, kx, ky, kz, edge + 2, planes - edge - 2, use)
    matrix = pool_matrix(2 * oz, oz, 2 * oz, 0, 0.125)
    planes1 = planes // 2
    pool(lambda x: c[x], 0, planes1, c1, matrix, work, rows, 0)
    f1[...] = jnp.zeros_like(f1)
    low1 = (edge + 2) // 2
    high1 = planes1 - low1
    pool(lambda x: rest[x], low1, high1, f1, matrix, work, rows, 0)
    coefficients(c1, kx1, ky1, kz1, rd1, 1, planes1 - 1, 0.25)

    def start_sweep1(x):
        v1[x] = f1[x] * rd1[x]

    loop(low1, high1, start_sweep1)
    u1[...] = jnp.zeros_like(u1)
    sweep(v1, u1, f1, kx1, ky1, kz1, rd1, low1 + 1, high1 - 1)
    h1 = XH // 2
    o1 = planes1 - XH

    def use1(x, vx, av):
        v1[x] = f1[x] - av

    operate(u1, kx1, ky1, kz1, h1, planes1 - h1, use1)
    half = oz // 2
    matrix1 = pool_matrix(oz, oz, half, jnp.where(pz == 0, 0, half // 2), 0.125)
    own1 = 2 * f2.shape[1]
    pool(lambda x: v1[x, 0:own1, :], h1 // 2, (planes1 - h1) // 2, f2, matrix1, work1, own1, h1 // 2)
    for e in range(nx):
        up = upward(bx, e)
        faces[e][0:h1] = u1[pl.ds(jnp.where(up, o1, h1), h1)]
        faces[e][h1:2 * h1 - 1] = f1[pl.ds(jnp.where(up, o1 + 1, h1), h1 - 1)]


def c2_kernel(c, c2, work):
    ox, oy, oz = c.shape
    pz = lax.axis_index("pair")
    quarter = oz // 4
    i, j = iota2((oz, oz), 0), iota2((oz, oz), 1)
    matrix = jnp.where(j == pz * quarter + lax.div(i, 4), 1.0 / 64.0, 0.0).astype(F32)

    def body(x):
        total = (c[4 * x] + c[4 * x + 1]) + (c[4 * x + 2] + c[4 * x + 3])
        work[...] = jnp.dot(total, matrix, precision=HI, preferred_element_type=F32)
        part = [work[pl.ds(k, oy // 4, stride=4), :] for k in range(4)]
        c2[x] = (part[0] + part[1]) + (part[2] + part[3])

    loop(0, ox // 4, body)


def up_kernel(nx, ny, nfar, *refs):
    kx, ky, kz, rd, g, u0, kx1, ky1, kz1, rd1, c1, f1, u1 = refs[:13]
    at = 13
    faces = refs[at:at + nx]
    at += nx
    pieces = 1 + nx + nfar
    got_f = refs[at:at + pieces]
    at += pieces
    got_c = refs[at:at + pieces]
    at += pieces
    field, residual = refs[at:at + 2]
    at += 2
    ua, ub, v1, w1, g1, c2, f2, kx2, ky2, kz2, rd2, v2, w2, work, wide = refs[at:]
    planes, rows, lanes = u0.shape
    planes1, rows1, oz = u1.shape
    planes2, rows2, _ = c2.shape
    ox, oy, _ = field.shape
    bx = lax.axis_index("boxes")
    sy = lax.axis_index("sub")
    pz = lax.axis_index("pair")
    o2x, o2y = ox // 4, oy // 4

    c2[...] = jnp.zeros_like(c2)
    f2[...] = jnp.zeros_like(f2)
    for out, got in ((c2, got_c), (f2, got_f)):
        places = [(L2X, o2x)]
        for e in range(nx):
            places.append((jnp.where(upward(bx, e), L2X + o2x, L2X - o2x), o2x))
        for e in range(nfar):
            places.append((jnp.where(upward(bx, e, 2), L2X + 2 * o2x, 0), L2X - o2x))
        for (x0, count), piece in zip(places, got):
            for f in range(ny + 1):
                if f == 0:
                    y0 = 0
                elif ny == 1:
                    y0 = pl.multiple_of(jnp.where(upward(sy, 0), o2y, rows2 - o2y), 8)
                else:
                    y0 = pl.multiple_of(jnp.where(upward(sy, f - 1), o2y, rows2 - o2y), 8)
                for x in range(count):
                    out[x0 + x, pl.ds(y0, o2y), :] = piece[f, x]
    coefficients(c2, kx2, ky2, kz2, rd2, 1, planes2 - 1, 0.0625)

    def start_sweep2(x):
        v2[x] = f2[x] * rd2[x]

    loop(1, planes2 - 1, start_sweep2)
    old, new = v2, w2
    for k in range(2, BOTTOM_SWEEPS + 1):
        sweep(old, new, f2, kx2, ky2, kz2, rd2, k, planes2 - k)
        old, new = new, old

    h1 = XH // 2
    o1 = planes1 - XH
    for x in range(planes1):
        g1[x] = f1[x]
        v1[x] = u1[x]
    for e in range(nx):
        up = upward(bx, e)
        v1[pl.ds(jnp.where(up, planes1 - h1, 0), h1)] = faces[e][0:h1]
        g1[pl.ds(jnp.where(up, planes1 - h1, 1), h1 - 1)] = faces[e][h1:2 * h1 - 1]
    i, j = iota2((oz, oz), 0), iota2((oz, oz), 1)
    spread_z = jnp.where(i == lax.div(lax.rem(pz * (oz // 2) + j, oz), 2), 1.0, 0.0).astype(F32)
    i, j = iota2((rows1, rows2), 0), iota2((rows1, rows2), 1)
    own1 = oy // 2
    if ny == 1:
        low_rows = (i >= own1) & jnp.logical_not(upward(sy, 0))
    else:
        low_rows = i >= own1 + YH // 2
    spread_y = jnp.where(j == lax.div(i, 2) + jnp.where(low_rows, rows2 - rows1 // 2, 0), 1.0, 0.0).astype(F32)
    base = L2X - h1 // 2

    def spread(x):
        moved = jnp.dot(old[base + x], spread_z, precision=HI, preferred_element_type=F32)
        moved = jnp.dot(spread_y, moved, precision=HI, preferred_element_type=F32)
        for k in range(2):
            y = 2 * x + k
            v1[y] = jnp.where(c1[y] > 0.0, v1[y] + moved, 0.0)

    loop(0, planes1 // 2, spread)
    sweep(v1, w1, g1, kx1, ky1, kz1, rd1, 1, planes1 - 1)
    sweep(w1, v1, g1, kx1, ky1, kz1, rd1, 2, planes1 - 2)

    i, j = iota2((oz, lanes), 0), iota2((oz, lanes), 1)
    spread_z0 = jnp.where(i == lax.div(j, 2), 1.0, 0.0).astype(F32)

    def spread0(x):
        work[...] = jnp.dot(v1[x], spread_z0, precision=HI, preferred_element_type=F32)
        for h in range(lanes // 128):
            values = work[:, 128 * h:128 * h + 128]
            wide[h, pl.ds(0, rows1, stride=2), :] = values
            wide[h, pl.ds(1, rows1, stride=2), :] = values
        for k in range(2):
            y = 2 * x + k
            for h in range(lanes // 128):
                cols = slice(128 * h, 128 * h + 128)
                ua[y, :, cols] = jnp.where(rd[y, :, cols] > 0.0, u0[y, :, cols] + wide[h], 0.0)

    loop(2, planes1 - 2, spread0)
    sweep(ua, ub, g, kx, ky, kz, rd, XH - 2, planes - XH + 2)
    sweep(ub, ua, g, kx, ky, kz, rd, XH - 1, planes - XH + 1)

    def use(x, vx, av):
        field[x - XH] = vx[0:oy, 0:oz]
        residual[x - XH] = g[x, 0:oy, 0:oz] - av[0:oy, 0:oz]

    operate(ua, kx, ky, kz, XH, planes - XH, use)


def call(kernel, outs, scratch=(), mib=60):
    return pl.pallas_call(
        kernel,
        out_shape=tuple(outs),
        scratch_shapes=tuple(pltpu.VMEM(s, F32) for s in scratch),
        compiler_params=params(mib),
    )


def per_device(phase, target_mask, deviation):
    ox, oy, oz = phase.shape
    nbox, nsub = lax.axis_size("boxes"), lax.axis_size("sub")
    swap_x, swap_y, far_x = exchanges(nbox), exchanges(nsub), exchanges(nbox, 2)
    nx, ny, nfar = len(swap_x), len(swap_y), len(far_x)
    pair_swap = [(0, 1), (1, 0)]

    def both(px, py):
        return [(a * nsub + c, b * nsub + d) for a, b in px for c, d in py]

    def traded(faces):
        out = []
        for e in range(nx):
            out.append(lax.ppermute(faces[e], "boxes", swap_x[e]))
        for f in range(ny):
            out.append(lax.ppermute(faces[nx + f], "sub", swap_y[f]))
        for e in range(nx):
            for f in range(ny):
                out.append(lax.ppermute(faces[nx + ny + e * ny + f], ("boxes", "sub"), both(swap_x[e], swap_y[f])))
        return out

    def gathered(own):
        line = own + lax.ppermute(own, "pair", pair_swap)
        sheet = jnp.stack([line] + [lax.ppermute(line, "sub", p) for p in swap_y])
        out = [sheet]
        for p in swap_x:
            out.append(lax.ppermute(sheet, "boxes", p))
        for e, p in enumerate(far_x):
            count = L2X - ox // 4
            at = jnp.where(upward(lax.axis_index("boxes"), e, 2), ox // 4 - count, 0)
            out.append(lax.ppermute(lax.dynamic_slice_in_dim(sheet, at, count, axis=1), "boxes", p))
        return out

    planes, rows = ox + 2 * XH, oy + YH * ny
    planes1, rows1 = planes // 2, rows // 2
    o2x, o2y = ox // 4, oy // 4
    planes2 = o2x + 2 * L2X
    rows2 = o2y * (ny + 1) + (8 if ny == 1 else 0)

    box = spec((ox, oy, oz))
    faces = [spec((XH + GX, oy, oz))] * nx + [spec((2, ox, YH, oz))] * ny + [spec((DC + DG, YH, oz))] * (nx * ny)
    c, g, *faces = call(lambda *r: send_kernel(nx, ny, *r), [box, box] + faces)(phase, target_mask, deviation)
    got = traded(faces)
    (c2,) = call(c2_kernel, [spec((o2x, o2y, oz))], [(oy, oz)])(c)
    got_c = gathered(c2)
    packed = 2 * planes // (oz // ZW)
    cpad, gpad, strip = call(
        lambda *r: extend_kernel(nx, ny, *r),
        [spec((planes, rows, oz)), spec((planes, rows, oz)), spec((packed, rows, oz))],
    )(c, g, *got)
    strip = lax.ppermute(strip, "pair", pair_swap)
    fine = (planes, rows, 2 * oz)
    middle = (planes1, rows1, oz)
    down = call(
        lambda *r: down_kernel(nx, *r),
        [in_vmem(fine)] * 6 + [in_vmem(middle)] * 7 + [spec((o2x, o2y, oz))] + [spec((XH - 1, rows1, oz))] * nx,
        [fine, fine, middle, (rows, oz), (oy // 2, oz)],
        mib=24,
    )(cpad, gpad, strip)
    kept, f2, sides = down[:13], down[13], down[14:]
    sides = [lax.ppermute(s, "boxes", p) for s, p in zip(sides, swap_x)]
    got_f = gathered(f2)
    lowest = (planes2, rows2, oz)
    return tuple(call(
        lambda *r: up_kernel(nx, ny, nfar, *r),
        [box, box],
        [fine, fine, middle, middle, middle] + [lowest] * 8 + [(rows1, 2 * oz), (2, rows, oz)],
        mib=24,
    )(*[held(x) for x in kept], *sides, *got_f, *got_c))


def solution(mesh):
    where = P(("groups", "boxes"), "sub", "pair")
    return jax.shard_map(
        per_device,
        mesh=mesh,
        in_specs=(where, where, where),
        out_specs=(where, where),
        check_vma=False,
    )
```

```python
import jax
import jax.numpy as jnp
from jax import lax
from jax.experimental import pallas as pl
from jax.experimental.pallas import tpu as pltpu
from jax.sharding import PartitionSpec as P

SWEEPS = 2
BOTTOM_SWEEPS = 8

floor_conduct = 0.1
relax_weight = 0.8

XH = 8
YH = 16
GX = 6
DC, DG = 6, 5
ZW = 16
L2X = 10
HI = lax.Precision.HIGHEST
F32 = jnp.float32
MIB = 1 << 20


def exchanges(count, step=1):
    swaps = []
    for e in range(2):
        pairs = []
        for i in range(count):
            if (i // step + e) % 2 == 0 and i + step < count:
                pairs += [(i, i + step), (i + step, i)]
        if pairs:
            swaps.append(pairs)
    return swaps


def upward(index, e, step=1):
    return ((index // step) + e) % 2 == 0


def spec(shape):
    return jax.ShapeDtypeStruct(shape, F32)


def in_vmem(shape):
    return pltpu.VMEM(shape, F32)


def held(x):
    return pltpu.with_memory_space_constraint(x, pltpu.VMEM)


def params(mib):
    return pltpu.CompilerParams(vmem_limit_bytes=mib * MIB)


def roll_up(v, axis):
    return pltpu.roll(v, v.shape[axis] - 1, axis)


def roll_down(v, axis):
    return pltpu.roll(v, 1, axis)


def loop(low, high, body, init=None, unroll=1):
    def step(i, carry):
        if init is None:
            body(i)
            return carry
        return body(i, carry)

    carry = 0 if init is None else init
    whole = (high - low) // unroll
    if whole > 1:

        def several(k, carry):
            for j in range(unroll):
                carry = step(low + k * unroll + j, carry)
            return carry

        carry = lax.fori_loop(0, whole, several, carry)
        low += whole * unroll
    for i in range(low, high):
        carry = step(i, carry)
    return carry


def unrolling(ref):
    return UNROLL.get(ref.shape[1] * ref.shape[2] // 1024, 4)


UNROLL = {20: 4, 5: 8}


def coefficients(c, kx, ky, kz, rd, low, high, scale):
    half = 0.5 * scale

    def faces(x):
        cx = c[x]
        fx = half * (cx + c[x + 1])
        fy = half * (cx + roll_up(cx, 0))
        fz = half * (cx + roll_up(cx, 1))
        kx[x] = fx
        ky[x] = fy
        kz[x] = fz
        return cx, fx, fy, fz

    _, first, _, _ = faces(low - 1)

    def body(x, before):
        cx, fx, fy, fz = faces(x)
        diagonal = fx + before + fy + roll_down(fy, 0) + fz + roll_down(fz, 1)
        inside = cx > 0.0
        rd[x] = jnp.where(inside, relax_weight / jnp.where(inside, diagonal, 1.0), 0.0)
        return fx

    loop(low, high, body, first, unrolling(rd))


def operate(v, kx, ky, kz, low, high, use):
    def body(x, before):
        vx = v[x]
        fx = kx[x] * (vx - v[x + 1])
        fy = ky[x] * (vx - roll_up(vx, 0))
        fz = kz[x] * (vx - roll_up(vx, 1))
        use(x, vx, (fx - before) + (fy - roll_down(fy, 0)) + (fz - roll_down(fz, 1)))
        return fx

    loop(low, high, body, kx[low - 1] * (v[low - 1] - v[low]), unrolling(v))


def sweep(v, out, g, kx, ky, kz, rd, low, high):
    def use(x, vx, av):
        out[x] = vx + rd[x] * (g[x] - av)

    operate(v, kx, ky, kz, low, high, use)


def iota2(shape, dim):
    return lax.broadcasted_iota(jnp.int32, shape, dim)


def send_kernel(nx, ny, phase, mask, dev, c_out, g_out, *outs):
    ox, oy, _ = phase.shape

    def body(x):
        p = phase[x]
        c_out[x] = floor_conduct + (1.0 - floor_conduct) * (p * p * p)
        g_out[x] = mask[x].astype(F32) * dev[x]

    loop(0, ox, body)
    bx = lax.axis_index("boxes")
    sy = lax.axis_index("sub")
    place = 0
    rows = [pl.ds(pl.multiple_of(jnp.where(upward(sy, f), oy - YH, 0), 8), YH) for f in range(ny)]
    for e in range(nx):
        up = upward(bx, e)
        face = outs[place]
        place += 1
        face[0:XH] = c_out[pl.ds(jnp.where(up, ox - XH, 0), XH)]
        face[XH:XH + GX] = g_out[pl.ds(jnp.where(up, ox - GX, 0), GX)]
    for f in range(ny):
        face = outs[place]
        place += 1
        face[0] = c_out[:, rows[f], :]
        face[1] = g_out[:, rows[f], :]
    for e in range(nx):
        up = upward(bx, e)
        for f in range(ny):
            face = outs[place]
            place += 1
            face[0:DC] = c_out[pl.ds(jnp.where(up, ox - DC, 0), DC), rows[f], :]
            face[DC:DC + DG] = g_out[pl.ds(jnp.where(up, ox - DG, 0), DG), rows[f], :]


def halo_rows(ny, f, oy, up):
    if ny == 1:
        return oy
    return jnp.where(up, oy, oy + YH)


def extend_kernel(nx, ny, c, g, *refs):
    count = nx + ny + nx * ny
    got, (c_out, g_out, strip) = refs[:count], refs[count:]
    ox, oy, oz = c.shape
    bx = lax.axis_index("boxes")
    sy = lax.axis_index("sub")
    pz = lax.axis_index("pair")
    c_out[...] = jnp.zeros_like(c_out)
    g_out[...] = jnp.zeros_like(g_out)
    c_out[XH:XH + ox, 0:oy, :] = c[...]
    g_out[XH:XH + ox, 0:oy, :] = g[...]
    place = 0
    row = iota2((YH, oz), 0)

    def trim(values, up):
        if ny > 1:
            return values
        return jnp.where(lax.div(row, 2) == jnp.where(up, YH // 2 - 1, 0), 0.0, values)

    def below(up, planes):
        return jnp.where(up, XH + ox, XH - planes)

    for e in range(nx):
        up = upward(bx, e)
        face = got[place]
        place += 1
        c_out[pl.ds(below(up, XH), XH), 0:oy, :] = face[0:XH]
        g_out[pl.ds(below(up, GX), GX), 0:oy, :] = face[XH:XH + GX]
    for f in range(ny):
        up = upward(sy, f)
        face = got[place]
        place += 1
        rows = pl.ds(pl.multiple_of(halo_rows(ny, f, oy, up), 8), YH)

        def copy(x, face=face, rows=rows, up=up):
            c_out[XH + x, rows, :] = trim(face[0, x], up)
            g_out[XH + x, rows, :] = trim(face[1, x], up)

        loop(0, ox, copy)
    for e in range(nx):
        ux = upward(bx, e)
        for f in range(ny):
            up = upward(sy, f)
            face = got[place]
            place += 1
            rows = pl.ds(pl.multiple_of(halo_rows(ny, f, oy, up), 8), YH)
            for x in range(DC):
                c_out[below(ux, DC) + x, rows, :] = trim(face[x], up)
            for x in range(DG):
                g_out[below(ux, DG) + x, rows, :] = trim(face[DC + x], up)
    group = oz // ZW
    nrows = c_out.shape[1]
    lane = iota2((nrows, oz), 1)
    start = jnp.where(pz == 0, oz - ZW, 0)
    packed = c_out.shape[0] // group

    def pack(a):
        for which, source in enumerate((c_out, g_out)):
            total = None
            for b in range(group):
                moved = pltpu.roll(source[group * a + b], lax.rem(ZW * b + oz - start, oz), 1)
                total = moved if total is None else jnp.where(lane >= ZW * b, moved, total)
            strip[which * packed + a] = total

    loop(0, packed, pack)


def pool(source, low, high, out, matrix, work, rows, first):
    half = rows // 2

    def body(j):
        work[...] = jnp.dot(source(2 * j) + source(2 * j + 1), matrix, precision=HI, preferred_element_type=F32)
        out[j - first] = work[pl.ds(0, half, stride=2), :] + work[pl.ds(1, half, stride=2), :]

    loop(low, high, body, unroll=4)


def pool_matrix(size_in, size_out, limit, shift, weight):
    i, j = iota2((size_in, size_out), 0), iota2((size_in, size_out), 1)
    return jnp.where((i < limit) & (j == shift + lax.div(i, 2)), weight, 0.0).astype(F32)


def down_kernel(nx, cpad, gpad, strip, *refs):
    kx, ky, kz, rd, g, u0, kx1, ky1, kz1, rd1, c1, f1, u1, f2 = refs[:14]
    faces = refs[14:14 + nx]
    c, first, v1, work, work1 = refs[14 + nx:]
    planes, rows, oz = cpad.shape
    pz = lax.axis_index("pair")
    bx = lax.axis_index("boxes")
    group = oz // ZW
    packed = planes // group
    lane = iota2((rows, oz), 1)
    start = jnp.where(pz == 0, 0, oz - ZW)
    near = (lane >= start) & (lane < start + ZW)

    def unpack(a):
        cs, gs = strip[a], strip[packed + a]
        for b in range(group):
            x = group * a + b
            turn = lax.rem(start + oz - ZW * b, oz)
            c[x, :, 0:oz] = cpad[x]
            g[x, :, 0:oz] = gpad[x]
            c[x, :, oz:] = jnp.where(near, pltpu.roll(cs, turn, 1), 0.0)
            g[x, :, oz:] = jnp.where(near, pltpu.roll(gs, turn, 1), 0.0)

    loop(0, packed, unpack)
    edge = XH - GX
    coefficients(c, kx, ky, kz, rd, edge, planes - edge, 1.0)

    def start_sweep(x):
        first[x] = g[x] * rd[x]

    loop(edge, planes - edge, start_sweep)
    sweep(first, u0, g, kx, ky, kz, rd, edge + 1, planes - edge - 1)
    rest = first

    def use(x, vx, av):
        rest[x] = g[x] - av

    operate(u0, kx, ky, kz, edge + 2, planes - edge - 2, use)
    matrix = pool_matrix(2 * oz, oz, 2 * oz, 0, 0.125)
    planes1 = planes // 2
    pool(lambda x: c[x], 0, planes1, c1, matrix, work, rows, 0)
    f1[...] = jnp.zeros_like(f1)
    low1 = (edge + 2) // 2
    high1 = planes1 - low1
    pool(lambda x: rest[x], low1, high1, f1, matrix, work, rows, 0)
    coefficients(c1, kx1, ky1, kz1, rd1, 1, planes1 - 1, 0.25)

    def start_sweep1(x):
        v1[x] = f1[x] * rd1[x]

    loop(low1, high1, start_sweep1)
    u1[...] = jnp.zeros_like(u1)
    sweep(v1, u1, f1, kx1, ky1, kz1, rd1, low1 + 1, high1 - 1)
    h1 = XH // 2
    o1 = planes1 - XH

    def use1(x, vx, av):
        v1[x] = f1[x] - av

    operate(u1, kx1, ky1, kz1, h1, planes1 - h1, use1)
    half = oz // 2
    matrix1 = pool_matrix(oz, oz, half, jnp.where(pz == 0, 0, half // 2), 0.125)
    own1 = 2 * f2.shape[1]
    pool(lambda x: v1[x, 0:own1, :], h1 // 2, (planes1 - h1) // 2, f2, matrix1, work1, own1, h1 // 2)
    for e in range(nx):
        up = upward(bx, e)
        faces[e][0:h1] = u1[pl.ds(jnp.where(up, o1, h1), h1)]
        faces[e][h1:2 * h1 - 1] = f1[pl.ds(jnp.where(up, o1 + 1, h1), h1 - 1)]


def c2_kernel(c, c2, work):
    ox, oy, oz = c.shape
    pz = lax.axis_index("pair")
    quarter = oz // 4
    i, j = iota2((oz, oz), 0), iota2((oz, oz), 1)
    matrix = jnp.where(j == pz * quarter + lax.div(i, 4), 1.0 / 64.0, 0.0).astype(F32)

    def body(x):
        total = (c[4 * x] + c[4 * x + 1]) + (c[4 * x + 2] + c[4 * x + 3])
        work[...] = jnp.dot(total, matrix, precision=HI, preferred_element_type=F32)
        part = [work[pl.ds(k, oy // 4, stride=4), :] for k in range(4)]
        c2[x] = (part[0] + part[1]) + (part[2] + part[3])

    loop(0, ox // 4, body)


def up_kernel(nx, ny, nfar, *refs):
    kx, ky, kz, rd, g, u0, kx1, ky1, kz1, rd1, c1, f1, u1 = refs[:13]
    at = 13
    faces = refs[at:at + nx]
    at += nx
    pieces = 1 + nx + nfar
    got_f = refs[at:at + pieces]
    at += pieces
    got_c = refs[at:at + pieces]
    at += pieces
    field, residual = refs[at:at + 2]
    at += 2
    ua, ub, v1, w1, g1, c2, f2, kx2, ky2, kz2, rd2, v2, w2, work, wide = refs[at:]
    planes, rows, lanes = u0.shape
    planes1, rows1, oz = u1.shape
    planes2, rows2, _ = c2.shape
    ox, oy, _ = field.shape
    bx = lax.axis_index("boxes")
    sy = lax.axis_index("sub")
    pz = lax.axis_index("pair")
    o2x, o2y = ox // 4, oy // 4

    c2[...] = jnp.zeros_like(c2)
    f2[...] = jnp.zeros_like(f2)
    for out, got in ((c2, got_c), (f2, got_f)):
        places = [(L2X, o2x)]
        for e in range(nx):
            places.append((jnp.where(upward(bx, e), L2X + o2x, L2X - o2x), o2x))
        for e in range(nfar):
            places.append((jnp.where(upward(bx, e, 2), L2X + 2 * o2x, 0), L2X - o2x))
        for (x0, count), piece in zip(places, got):
            for f in range(ny + 1):
                if f == 0:
                    y0 = 0
                elif ny == 1:
                    y0 = pl.multiple_of(jnp.where(upward(sy, 0), o2y, rows2 - o2y), 8)
                else:
                    y0 = pl.multiple_of(jnp.where(upward(sy, f - 1), o2y, rows2 - o2y), 8)
                for x in range(count):
                    out[x0 + x, pl.ds(y0, o2y), :] = piece[f, x]
    coefficients(c2, kx2, ky2, kz2, rd2, 1, planes2 - 1, 0.0625)

    def start_sweep2(x):
        v2[x] = f2[x] * rd2[x]

    loop(1, planes2 - 1, start_sweep2)
    old, new = v2, w2
    for k in range(2, BOTTOM_SWEEPS + 1):
        sweep(old, new, f2, kx2, ky2, kz2, rd2, k, planes2 - k)
        old, new = new, old

    h1 = XH // 2
    o1 = planes1 - XH
    for x in range(planes1):
        g1[x] = f1[x]
        v1[x] = u1[x]
    for e in range(nx):
        up = upward(bx, e)
        v1[pl.ds(jnp.where(up, planes1 - h1, 0), h1)] = faces[e][0:h1]
        g1[pl.ds(jnp.where(up, planes1 - h1, 1), h1 - 1)] = faces[e][h1:2 * h1 - 1]
    i, j = iota2((oz, oz), 0), iota2((oz, oz), 1)
    spread_z = jnp.where(i == lax.div(lax.rem(pz * (oz // 2) + j, oz), 2), 1.0, 0.0).astype(F32)
    i, j = iota2((rows1, rows2), 0), iota2((rows1, rows2), 1)
    own1 = oy // 2
    if ny == 1:
        low_rows = (i >= own1) & jnp.logical_not(upward(sy, 0))
    else:
        low_rows = i >= own1 + YH // 2
    spread_y = jnp.where(j == lax.div(i, 2) + jnp.where(low_rows, rows2 - rows1 // 2, 0), 1.0, 0.0).astype(F32)
    base = L2X - h1 // 2

    def spread(x):
        moved = jnp.dot(old[base + x], spread_z, precision=HI, preferred_element_type=F32)
        moved = jnp.dot(spread_y, moved, precision=HI, preferred_element_type=F32)
        for k in range(2):
            y = 2 * x + k
            v1[y] = jnp.where(c1[y] > 0.0, v1[y] + moved, 0.0)

    loop(0, planes1 // 2, spread)
    sweep(v1, w1, g1, kx1, ky1, kz1, rd1, 1, planes1 - 1)
    sweep(w1, v1, g1, kx1, ky1, kz1, rd1, 2, planes1 - 2)

    i, j = iota2((oz, lanes), 0), iota2((oz, lanes), 1)
    spread_z0 = jnp.where(i == lax.div(j, 2), 1.0, 0.0).astype(F32)

    def spread0(x):
        work[...] = jnp.dot(v1[x], spread_z0, precision=HI, preferred_element_type=F32)
        for h in range(lanes // 128):
            values = work[:, 128 * h:128 * h + 128]
            wide[h, pl.ds(0, rows1, stride=2), :] = values
            wide[h, pl.ds(1, rows1, stride=2), :] = values
        for k in range(2):
            y = 2 * x + k
            for h in range(lanes // 128):
                cols = slice(128 * h, 128 * h + 128)
                ua[y, :, cols] = jnp.where(rd[y, :, cols] > 0.0, u0[y, :, cols] + wide[h], 0.0)

    loop(2, planes1 - 2, spread0)
    sweep(ua, ub, g, kx, ky, kz, rd, XH - 2, planes - XH + 2)
    sweep(ub, ua, g, kx, ky, kz, rd, XH - 1, planes - XH + 1)

    def use(x, vx, av):
        field[x - XH] = vx[0:oy, 0:oz]
        residual[x - XH] = g[x, 0:oy, 0:oz] - av[0:oy, 0:oz]

    operate(ua, kx, ky, kz, XH, planes - XH, use)


def call(kernel, outs, scratch=(), mib=60):
    return pl.pallas_call(
        kernel,
        out_shape=tuple(outs),
        scratch_shapes=tuple(pltpu.VMEM(s, F32) for s in scratch),
        compiler_params=params(mib),
    )


def per_device(phase, target_mask, deviation):
    ox, oy, oz = phase.shape
    nbox, nsub = lax.axis_size("boxes"), lax.axis_size("sub")
    swap_x, swap_y, far_x = exchanges(nbox), exchanges(nsub), exchanges(nbox, 2)
    nx, ny, nfar = len(swap_x), len(swap_y), len(far_x)
    pair_swap = [(0, 1), (1, 0)]

    def both(px, py):
        return [(a * nsub + c, b * nsub + d) for a, b in px for c, d in py]

    def traded(faces):
        out = []
        for e in range(nx):
            out.append(lax.ppermute(faces[e], "boxes", swap_x[e]))
        for f in range(ny):
            out.append(lax.ppermute(faces[nx + f], "sub", swap_y[f]))
        for e in range(nx):
            for f in range(ny):
                out.append(lax.ppermute(faces[nx + ny + e * ny + f], ("boxes", "sub"), both(swap_x[e], swap_y[f])))
        return out

    def gathered(own):
        line = own + lax.ppermute(own, "pair", pair_swap)
        sheet = jnp.stack([line] + [lax.ppermute(line, "sub", p) for p in swap_y])
        out = [sheet]
        for p in swap_x:
            out.append(lax.ppermute(sheet, "boxes", p))
        for e, p in enumerate(far_x):
            count = L2X - ox // 4
            at = jnp.where(upward(lax.axis_index("boxes"), e, 2), ox // 4 - count, 0)
            out.append(lax.ppermute(lax.dynamic_slice_in_dim(sheet, at, count, axis=1), "boxes", p))
        return out

    planes, rows = ox + 2 * XH, oy + YH * ny
    planes1, rows1 = planes // 2, rows // 2
    o2x, o2y = ox // 4, oy // 4
    planes2 = o2x + 2 * L2X
    rows2 = o2y * (ny + 1) + (8 if ny == 1 else 0)

    box = spec((ox, oy, oz))
    faces = [spec((XH + GX, oy, oz))] * nx + [spec((2, ox, YH, oz))] * ny + [spec((DC + DG, YH, oz))] * (nx * ny)
    c, g, *faces = call(lambda *r: send_kernel(nx, ny, *r), [box, box] + faces)(phase, target_mask, deviation)
    got = traded(faces)
    (c2,) = call(c2_kernel, [spec((o2x, o2y, oz))], [(oy, oz)])(c)
    got_c = gathered(c2)
    packed = 2 * planes // (oz // ZW)
    cpad, gpad, strip = call(
        lambda *r: extend_kernel(nx, ny, *r),
        [spec((planes, rows, oz)), spec((planes, rows, oz)), spec((packed, rows, oz))],
    )(c, g, *got)
    strip = lax.ppermute(strip, "pair", pair_swap)
    fine = (planes, rows, 2 * oz)
    middle = (planes1, rows1, oz)
    down = call(
        lambda *r: down_kernel(nx, *r),
        [in_vmem(fine)] * 6 + [in_vmem(middle)] * 7 + [spec((o2x, o2y, oz))] + [spec((XH - 1, rows1, oz))] * nx,
        [fine, fine, middle, (rows, oz), (oy // 2, oz)],
        mib=24,
    )(cpad, gpad, strip)
    kept, f2, sides = down[:13], down[13], down[14:]
    sides = [lax.ppermute(s, "boxes", p) for s, p in zip(sides, swap_x)]
    got_f = gathered(f2)
    lowest = (planes2, rows2, oz)
    return tuple(call(
        lambda *r: up_kernel(nx, ny, nfar, *r),
        [box, box],
        [fine, fine, middle, middle, middle] + [lowest] * 8 + [(rows1, 2 * oz), (2, rows, oz)],
        mib=24,
    )(*[held(x) for x in kept], *sides, *got_f, *got_c))


def solution(mesh):
    where = P(("groups", "boxes"), "sub", "pair")
    return jax.shard_map(
        per_device,
        mesh=mesh,
        in_specs=(where, where, where),
        out_specs=(where, where),
        check_vma=False,
    )
```

```python
import jax
import jax.numpy as jnp
from jax import lax
from jax.experimental import pallas as pl
from jax.experimental.pallas import tpu as pltpu
from jax.sharding import PartitionSpec as P

SWEEPS = 2
BOTTOM_SWEEPS = 8

floor_conduct = 0.1
relax_weight = 0.8

XH = 8
YH = 16
GX = 6
DC, DG = 6, 5
ZW = 16
L2X = 10
F32 = jnp.float32
BF16 = jnp.bfloat16
MIB = 1 << 20


def exchanges(count, step=1):
    swaps = []
    for e in range(2):
        pairs = []
        for i in range(count):
            if (i // step + e) % 2 == 0 and i + step < count:
                pairs += [(i, i + step), (i + step, i)]
        if pairs:
            swaps.append(pairs)
    return swaps


def upward(index, e, step=1):
    return ((index // step) + e) % 2 == 0


def spec(shape):
    return jax.ShapeDtypeStruct(shape, F32)


def in_vmem(shape):
    return pltpu.VMEM(shape, F32)


def held(x):
    return pltpu.with_memory_space_constraint(x, pltpu.VMEM)


def params(mib):
    return pltpu.CompilerParams(vmem_limit_bytes=mib * MIB)


def roll_up(v, axis):
    return pltpu.roll(v, v.shape[axis] - 1, axis)


def roll_down(v, axis):
    return pltpu.roll(v, 1, axis)


def loop(low, high, body, init=None, unroll=1):
    def step(i, carry):
        if init is None:
            body(i)
            return carry
        return body(i, carry)

    carry = 0 if init is None else init
    whole = (high - low) // unroll
    if whole > 1:

        def several(k, carry):
            for j in range(unroll):
                carry = step(low + k * unroll + j, carry)
            return carry

        carry = lax.fori_loop(0, whole, several, carry)
        low += whole * unroll
    for i in range(low, high):
        carry = step(i, carry)
    return carry


def unrolling(ref):
    return UNROLL.get(ref.shape[1] * ref.shape[2] // 1024, 4)


UNROLL = {20: 4, 5: 8}


def coefficients(c, kx, ky, kz, rd, low, high, scale):
    half = 0.5 * scale

    def faces(x):
        cx = c[x]
        fx = half * (cx + c[x + 1])
        fy = half * (cx + roll_up(cx, 0))
        fz = half * (cx + roll_up(cx, 1))
        kx[x] = fx
        ky[x] = fy
        kz[x] = fz
        return cx, fx, fy, fz

    _, first, _, _ = faces(low - 1)

    def body(x, before):
        cx, fx, fy, fz = faces(x)
        diagonal = fx + before + fy + roll_down(fy, 0) + fz + roll_down(fz, 1)
        inside = cx > 0.0
        rd[x] = jnp.where(inside, relax_weight / jnp.where(inside, diagonal, 1.0), 0.0)
        return fx

    loop(low, high, body, first, unrolling(rd))


def operate(v, kx, ky, kz, low, high, use):
    def body(x, before):
        vx = v[x]
        fx = kx[x] * (vx - v[x + 1])
        fy = ky[x] * (vx - roll_up(vx, 0))
        fz = kz[x] * (vx - roll_up(vx, 1))
        use(x, vx, (fx - before) + (fy - roll_down(fy, 0)) + (fz - roll_down(fz, 1)))
        return fx

    loop(low, high, body, kx[low - 1] * (v[low - 1] - v[low]), unrolling(v))


def sweep(v, out, g, kx, ky, kz, rd, low, high):
    def use(x, vx, av):
        out[x] = vx + rd[x] * (g[x] - av)

    operate(v, kx, ky, kz, low, high, use)


def iota2(shape, dim):
    return lax.broadcasted_iota(jnp.int32, shape, dim)


def make(phase, mask, dev, x, rows=slice(None)):
    p = phase[x, rows, :]
    return floor_conduct + (1.0 - floor_conduct) * (p * p * p), mask[x, rows, :].astype(F32) * dev[x, rows, :]


def send_kernel(nx, ny, phase, mask, dev, *outs):
    ox, oy, _ = phase.shape
    bx = lax.axis_index("boxes")
    sy = lax.axis_index("sub")
    place = 0
    rows = [pl.ds(pl.multiple_of(jnp.where(upward(sy, f), oy - YH, 0), 8), YH) for f in range(ny)]
    for e in range(nx):
        up = upward(bx, e)
        face = outs[place]
        place += 1
        for x in range(XH):
            p = phase[jnp.where(up, ox - XH, 0) + x]
            face[x] = floor_conduct + (1.0 - floor_conduct) * (p * p * p)
        for x in range(GX):
            at = jnp.where(up, ox - GX, 0) + x
            face[XH + x] = mask[at].astype(F32) * dev[at]
    for f in range(ny):
        face = outs[place]
        place += 1

        def body(x, face=face, f=f):
            face[0, x], face[1, x] = make(phase, mask, dev, x, rows[f])

        loop(0, ox, body, unroll=8)
    for e in range(nx):
        up = upward(bx, e)
        for f in range(ny):
            face = outs[place]
            place += 1
            for x in range(DC):
                face[x] = make(phase, mask, dev, jnp.where(up, ox - DC, 0) + x, rows[f])[0]
            for x in range(DG):
                face[DC + x] = make(phase, mask, dev, jnp.where(up, ox - DG, 0) + x, rows[f])[1]


def pack(planes, turns, lane):
    total = None
    for b, (plane, turn) in enumerate(zip(planes, turns)):
        moved = pltpu.roll(plane, turn, 1)
        total = moved if total is None else jnp.where(lane >= ZW * b, moved, total)
    return total


def strip_turns(oz, start):
    return [lax.rem(ZW * b + oz - start, oz) for b in range(oz // ZW)]


def split(x):
    high = x.astype(BF16)
    rest = x - high.astype(F32)
    middle = rest.astype(BF16)
    low = (rest - middle.astype(F32)).astype(BF16)
    return jnp.concatenate([high, middle, low], axis=-1)


def times(x, matrix):
    return jnp.dot(split(x), matrix, preferred_element_type=F32)


def thrice(matrix):
    return jnp.concatenate([matrix.astype(BF16)] * 3, axis=0)


def own_kernel(phase, mask, dev, c, g, strip, c2, sums, work):
    ox, oy, oz = phase.shape
    pz = lax.axis_index("pair")

    def body(x):
        c[x], g[x] = make(phase, mask, dev, x)

    loop(0, ox, body, unroll=4)
    quarter = oz // 4
    i, j = iota2((oz, oz), 0), iota2((oz, oz), 1)
    matrix = thrice(jnp.where(j == pz * quarter + lax.div(i, 4), 1.0 / 64.0, 0.0))
    for x in range(ox // 4):
        sums[...] = (c[4 * x] + c[4 * x + 1]) + (c[4 * x + 2] + c[4 * x + 3])
        part = [sums[pl.ds(k, oy // 4, stride=4), :] for k in range(4)]
        work[x] = (part[0] + part[1]) + (part[2] + part[3])
    c2[...] = times(work[...].reshape(-1, oz), matrix).reshape(c2.shape)
    group = oz // ZW
    turns = strip_turns(oz, jnp.where(pz == 0, oz - ZW, 0))
    lane = iota2((oy, oz), 1)
    for which, source in enumerate((c, g)):
        for a in range(ox // group):
            strip[which, a] = pack([source[group * a + b] for b in range(group)], turns, lane)


def halo_rows(ny, f, oy, up):
    if ny == 1:
        return oy
    return jnp.where(up, oy, oy + YH)


def extend_kernel(nx, ny, c, g, own, *refs):
    count = nx + ny + nx * ny
    got, (c_out, g_out, strip) = refs[:count], refs[count:]
    ox, oy, oz = c.shape
    planes, nrows, _ = c_out.shape
    bx = lax.axis_index("boxes")
    sy = lax.axis_index("sub")
    pz = lax.axis_index("pair")
    for out, source in ((c_out, c), (g_out, g)):
        for low, high in ((0, XH), (XH + ox, planes)):
            out[low:high] = jnp.zeros((high - low, nrows, oz), F32)
        out[XH:XH + ox, 0:oy, :] = source[...]
    place = 0
    row = iota2((YH, oz), 0)

    def trim(values, up):
        if ny > 1:
            return values
        return jnp.where(lax.div(row, 2) == jnp.where(up, YH // 2 - 1, 0), 0.0, values)

    def below(up, planes):
        return jnp.where(up, XH + ox, XH - planes)

    for e in range(nx):
        up = upward(bx, e)
        face = got[place]
        place += 1
        c_out[pl.ds(below(up, XH), XH), 0:oy, :] = face[0:XH]
        g_out[pl.ds(below(up, GX), GX), 0:oy, :] = face[XH:XH + GX]
    for f in range(ny):
        up = upward(sy, f)
        face = got[place]
        place += 1
        rows = pl.ds(pl.multiple_of(halo_rows(ny, f, oy, up), 8), YH)

        def copy(x, face=face, rows=rows, up=up):
            c_out[XH + x, rows, :] = trim(face[0, x], up)
            g_out[XH + x, rows, :] = trim(face[1, x], up)

        loop(0, ox, copy, unroll=8)
    for e in range(nx):
        ux = upward(bx, e)
        for f in range(ny):
            up = upward(sy, f)
            face = got[place]
            place += 1
            rows = pl.ds(pl.multiple_of(halo_rows(ny, f, oy, up), 8), YH)
            for x in range(DC):
                c_out[below(ux, DC) + x, rows, :] = trim(face[x], up)
            for x in range(DG):
                g_out[below(ux, DG) + x, rows, :] = trim(face[DC + x], up)
    group = oz // ZW
    turns = strip_turns(oz, jnp.where(pz == 0, oz - ZW, 0))
    packed = planes // group
    side = XH // group
    for which, source in enumerate((c_out, g_out)):
        for a in range(packed):
            at = which * packed + a
            if side <= a < packed - side:
                strip[at, 0:oy, :] = own[which, a - side]
                rows = slice(oy, nrows)
            else:
                rows = slice(0, nrows)
            lane = iota2((nrows - (rows.start or 0), oz), 1)
            strip[at, rows, :] = pack([source[group * a + b, rows, :] for b in range(group)], turns, lane)


def pool(source, low, high, out, matrix, work, step):
    tiles, rows, width = work.shape

    def body(k):
        sums = []
        for j in range(step):
            at = 2 * (low + step * k + j)
            total = source(at) + source(at + 1)
            parts = []
            for h in range(tiles // step):
                slot = j * (tiles // step) + h
                work[slot] = total[:, width * h:width * h + width]
                parts.append(work[slot, pl.ds(0, rows // 2, stride=2), :] + work[slot, pl.ds(1, rows // 2, stride=2), :])
            sums.append(jnp.concatenate(parts, axis=1))
        done = times(jnp.concatenate(sums, axis=0), matrix)
        out[pl.ds(step * k, step)] = done.reshape(step, rows // 2, done.shape[1])

    loop(0, (high - low) // step, body)


def pool_matrix(size_in, size_out, limit, shift, weight):
    i, j = iota2((size_in, size_out), 0), iota2((size_in, size_out), 1)
    return thrice(jnp.where((i < limit) & (j == shift + lax.div(i, 2)), weight, 0.0))


def down_kernel(nx, cpad, gpad, strip, *refs):
    kx, ky, kz, rd, g, u0, kx1, ky1, kz1, rd1, c1, f1, u1, f2 = refs[:14]
    faces = refs[14:14 + nx]
    c, first, v1, work, work1 = refs[14 + nx:]
    planes, rows, oz = cpad.shape
    pz = lax.axis_index("pair")
    bx = lax.axis_index("boxes")
    group = oz // ZW
    packed = planes // group
    lane = iota2((rows, oz), 1)
    start = jnp.where(pz == 0, 0, oz - ZW)
    near = (lane >= start) & (lane < start + ZW)

    def unpack(a):
        cs, gs = strip[a], strip[packed + a]
        for b in range(group):
            x = group * a + b
            turn = lax.rem(start + oz - ZW * b, oz)
            c[x, :, 0:oz] = cpad[x]
            g[x, :, 0:oz] = gpad[x]
            c[x, :, oz:] = jnp.where(near, pltpu.roll(cs, turn, 1), 0.0)
            g[x, :, oz:] = jnp.where(near, pltpu.roll(gs, turn, 1), 0.0)

    loop(0, packed, unpack)
    edge = XH - GX
    coefficients(c, kx, ky, kz, rd, edge, planes - edge, 1.0)

    def start_sweep(x):
        first[x] = g[x] * rd[x]

    loop(edge, planes - edge, start_sweep)
    sweep(first, u0, g, kx, ky, kz, rd, edge + 1, planes - edge - 1)
    rest = first

    def use(x, vx, av):
        rest[x] = g[x] - av

    operate(u0, kx, ky, kz, edge + 2, planes - edge - 2, use)
    matrix = pool_matrix(2 * oz, oz, 2 * oz, 0, 0.125)
    planes1 = planes // 2
    pool(lambda x: c[x], 0, planes1, c1, matrix, work, 4)
    f1[...] = jnp.zeros_like(f1)
    low1 = (edge + 2) // 2
    high1 = planes1 - low1
    pool(lambda x: rest[x], low1, high1, f1.at[low1:high1], matrix, work, 4)
    coefficients(c1, kx1, ky1, kz1, rd1, 1, planes1 - 1, 0.25)

    def start_sweep1(x):
        v1[x] = f1[x] * rd1[x]

    loop(low1, high1, start_sweep1)
    u1[...] = jnp.zeros_like(u1)
    sweep(v1, u1, f1, kx1, ky1, kz1, rd1, low1 + 1, high1 - 1)
    h1 = XH // 2
    o1 = planes1 - XH

    def use1(x, vx, av):
        v1[x] = f1[x] - av

    operate(u1, kx1, ky1, kz1, h1, planes1 - h1, use1)
    half = oz // 2
    matrix1 = pool_matrix(oz, oz, half, jnp.where(pz == 0, 0, half // 2), 0.125)
    own1 = 2 * f2.shape[1]
    pool(lambda x: v1[x, 0:own1, :], h1 // 2, (planes1 - h1) // 2, f2, matrix1, work1, f2.shape[0])
    for e in range(nx):
        up = upward(bx, e)
        faces[e][0:h1] = u1[pl.ds(jnp.where(up, o1, h1), h1)]
        faces[e][h1:2 * h1 - 1] = f1[pl.ds(jnp.where(up, o1 + 1, h1), h1 - 1)]


def up_kernel(nx, ny, nfar, *refs):
    kx, ky, kz, rd, g, u0, kx1, ky1, kz1, rd1, c1, f1, u1 = refs[:13]
    at = 13
    faces = refs[at:at + nx]
    at += nx
    pieces = 1 + nx + nfar
    got_f = refs[at:at + pieces]
    at += pieces
    got_c = refs[at:at + pieces]
    at += pieces
    field, residual = refs[at:at + 2]
    at += 2
    ua, ub, v1, w1, g1, c2, f2, kx2, ky2, kz2, rd2, v2, w2, tall, wide = refs[at:]
    planes, rows, lanes = u0.shape
    planes1, rows1, oz = u1.shape
    planes2, rows2, _ = c2.shape
    ox, oy, _ = field.shape
    bx = lax.axis_index("boxes")
    sy = lax.axis_index("sub")
    pz = lax.axis_index("pair")
    o2x, o2y = ox // 4, oy // 4

    c2[...] = jnp.zeros_like(c2)
    f2[...] = jnp.zeros_like(f2)
    for out, got in ((c2, got_c), (f2, got_f)):
        places = [(L2X, o2x)]
        for e in range(nx):
            places.append((jnp.where(upward(bx, e), L2X + o2x, L2X - o2x), o2x))
        for e in range(nfar):
            places.append((jnp.where(upward(bx, e, 2), L2X + 2 * o2x, 0), L2X - o2x))
        for (x0, count), piece in zip(places, got):
            for f in range(ny + 1):
                if f == 0:
                    y0 = 0
                elif ny == 1:
                    y0 = pl.multiple_of(jnp.where(upward(sy, 0), o2y, rows2 - o2y), 8)
                else:
                    y0 = pl.multiple_of(jnp.where(upward(sy, f - 1), o2y, rows2 - o2y), 8)
                for x in range(count):
                    out[x0 + x, pl.ds(y0, o2y), :] = piece[f, x]
    coefficients(c2, kx2, ky2, kz2, rd2, 1, planes2 - 1, 0.0625)

    def start_sweep2(x):
        v2[x] = f2[x] * rd2[x]

    loop(1, planes2 - 1, start_sweep2)
    old, new = v2, w2
    for k in range(2, BOTTOM_SWEEPS + 1):
        sweep(old, new, f2, kx2, ky2, kz2, rd2, k, planes2 - k)
        old, new = new, old

    h1 = XH // 2
    o1 = planes1 - XH
    for x in range(planes1):
        g1[x] = f1[x]
        v1[x] = u1[x]
    for e in range(nx):
        up = upward(bx, e)
        v1[pl.ds(jnp.where(up, planes1 - h1, 0), h1)] = faces[e][0:h1]
        g1[pl.ds(jnp.where(up, planes1 - h1, 1), h1 - 1)] = faces[e][h1:2 * h1 - 1]
    i, j = iota2((oz, oz), 0), iota2((oz, oz), 1)
    spread_z = thrice(jnp.where(i == lax.div(lax.rem(pz * (oz // 2) + j, oz), 2), 1.0, 0.0))
    base = L2X - h1 // 2
    count = planes1 // 2
    moved = times(old[base:base + count].reshape(count * rows2, oz), spread_z)
    row = iota2((8, oz), 0)
    for x in range(count):
        t = moved[x * rows2:x * rows2 + rows2]
        if ny == 1:
            halo = jnp.where(upward(sy, 0), t[o2y:o2y + 8], pltpu.roll(t[rows2 - 8:], 4, 0))
        else:
            halo = jnp.where(row < 4, t[o2y:o2y + 8], t[rows2 - 8:])
        t = jnp.concatenate([t[0:o2y], halo], axis=0)
        tall[x, pl.ds(0, o2y + 8, stride=2), :] = t
        tall[x, pl.ds(1, o2y + 8, stride=2), :] = t
        both = tall[x, 0:rows1, :]
        for k in range(2):
            y = 2 * x + k
            v1[y] = jnp.where(c1[y] > 0.0, v1[y] + both, 0.0)

    sweep(v1, w1, g1, kx1, ky1, kz1, rd1, 1, planes1 - 1)
    sweep(w1, v1, g1, kx1, ky1, kz1, rd1, 2, planes1 - 2)

    i, j = iota2((oz, lanes), 0), iota2((oz, lanes), 1)
    spread_z0 = thrice(jnp.where(i == lax.div(j, 2), 1.0, 0.0))
    step = 4

    def spread0(n):
        low = 2 + step * n
        moved = times(v1[pl.ds(low, step)].reshape(step * rows1, oz), spread_z0)
        for m in range(step):
            for h in range(lanes // oz):
                cols = slice(oz * h, oz * h + oz)
                values = moved[m * rows1:m * rows1 + rows1, cols]
                wide[2 * m + h, pl.ds(0, rows1, stride=2), :] = values
                wide[2 * m + h, pl.ds(1, rows1, stride=2), :] = values
                for k in range(2):
                    y = 2 * (low + m) + k
                    ua[y, :, cols] = jnp.where(rd[y, :, cols] > 0.0, u0[y, :, cols] + wide[2 * m + h], 0.0)

    loop(0, (planes1 - 4) // step, spread0)
    sweep(ua, ub, g, kx, ky, kz, rd, XH - 2, planes - XH + 2)
    sweep(ub, ua, g, kx, ky, kz, rd, XH - 1, planes - XH + 1)

    def use(x, vx, av):
        field[x - XH] = vx[0:oy, 0:oz]
        residual[x - XH] = g[x, 0:oy, 0:oz] - av[0:oy, 0:oz]

    operate(ua, kx, ky, kz, XH, planes - XH, use)


def call(kernel, outs, scratch=(), mib=60):
    return pl.pallas_call(
        kernel,
        out_shape=tuple(outs),
        scratch_shapes=tuple(pltpu.VMEM(s, F32) for s in scratch),
        compiler_params=params(mib),
    )


def per_device(phase, target_mask, deviation):
    ox, oy, oz = phase.shape
    nbox, nsub = lax.axis_size("boxes"), lax.axis_size("sub")
    swap_x, swap_y, far_x = exchanges(nbox), exchanges(nsub), exchanges(nbox, 2)
    nx, ny, nfar = len(swap_x), len(swap_y), len(far_x)
    pair_swap = [(0, 1), (1, 0)]

    def both(px, py):
        return [(a * nsub + c, b * nsub + d) for a, b in px for c, d in py]

    def traded(faces):
        out = []
        for e in range(nx):
            out.append(lax.ppermute(faces[e], "boxes", swap_x[e]))
        for f in range(ny):
            out.append(lax.ppermute(faces[nx + f], "sub", swap_y[f]))
        for e in range(nx):
            for f in range(ny):
                out.append(lax.ppermute(faces[nx + ny + e * ny + f], ("boxes", "sub"), both(swap_x[e], swap_y[f])))
        return out

    def gathered(own):
        line = own + lax.ppermute(own, "pair", pair_swap)
        sheet = jnp.stack([line] + [lax.ppermute(line, "sub", p) for p in swap_y])
        out = [sheet]
        for p in swap_x:
            out.append(lax.ppermute(sheet, "boxes", p))
        for e, p in enumerate(far_x):
            count = L2X - ox // 4
            at = jnp.where(upward(lax.axis_index("boxes"), e, 2), ox // 4 - count, 0)
            out.append(lax.ppermute(lax.dynamic_slice_in_dim(sheet, at, count, axis=1), "boxes", p))
        return out

    planes, rows = ox + 2 * XH, oy + YH * ny
    planes1, rows1 = planes // 2, rows // 2
    o2x, o2y = ox // 4, oy // 4
    planes2 = o2x + 2 * L2X
    rows2 = o2y * (ny + 1) + (8 if ny == 1 else 0)

    box = spec((ox, oy, oz))
    faces = [spec((XH + GX, oy, oz))] * nx + [spec((2, ox, YH, oz))] * ny + [spec((DC + DG, YH, oz))] * (nx * ny)
    faces = call(lambda *r: send_kernel(nx, ny, *r), faces)(phase, target_mask, deviation)
    got = traded(faces)
    phase, target_mask, deviation, _ = lax.optimization_barrier((phase, target_mask, deviation, faces))
    group = oz // ZW
    c, g, own, c2 = call(
        own_kernel,
        [in_vmem((ox, oy, oz)), in_vmem((ox, oy, oz)), in_vmem((2, ox // group, oy, oz)), spec((o2x, o2y, oz))],
        [(oy, oz), (o2x, o2y, oz)],
        mib=24,
    )(phase, target_mask, deviation)
    got_c = gathered(c2)
    got, got_c = lax.optimization_barrier((got, got_c))
    padded = (planes, rows, oz)
    cpad, gpad, strip = call(
        lambda *r: extend_kernel(nx, ny, *r),
        [in_vmem(padded), in_vmem(padded), spec((2 * planes // group, rows, oz))],
        mib=24,
    )(held(c), held(g), held(own), *got)
    strip = lax.ppermute(strip, "pair", pair_swap)
    fine = (planes, rows, 2 * oz)
    middle = (planes1, rows1, oz)
    down = call(
        lambda *r: down_kernel(nx, *r),
        [in_vmem(fine)] * 6 + [in_vmem(middle)] * 7 + [spec((o2x, o2y, oz))] + [spec((XH - 1, rows1, oz))] * nx,
        [fine, fine, middle, (8, rows, oz), (o2x, oy // 2, oz)],
        mib=24,
    )(held(cpad), held(gpad), strip)
    kept, f2, sides = down[:13], down[13], down[14:]
    sides = [lax.ppermute(s, "boxes", p) for s, p in zip(sides, swap_x)]
    got_f = gathered(f2)
    lowest = (planes2, rows2, oz)
    return tuple(call(
        lambda *r: up_kernel(nx, ny, nfar, *r),
        [box, box],
        [fine, fine, middle, middle, middle] + [lowest] * 8 + [(planes1 // 2, 2 * (o2y + 8), oz), (8, rows, oz)],
        mib=24,
    )(*[held(x) for x in kept], *sides, *got_f, *got_c))


def solution(mesh):
    where = P(("groups", "boxes"), "sub", "pair")
    return jax.shard_map(
        per_device,
        mesh=mesh,
        in_specs=(where, where, where),
        out_specs=(where, where),
        check_vma=False,
    )
```

```python
import jax
import jax.numpy as jnp
from jax import lax
from jax.experimental import pallas as pl
from jax.experimental.pallas import tpu as pltpu
from jax.sharding import PartitionSpec as P

SWEEPS = 2
BOTTOM_SWEEPS = 8

floor_conduct = 0.1
relax_weight = 0.8

XH = 8
YH = 16
GX = 6
DC, DG = 6, 5
ZW = 16
L2X = 10
F32 = jnp.float32
BF16 = jnp.bfloat16
MIB = 1 << 20


def exchanges(count, step=1):
    swaps = []
    for e in range(2):
        pairs = []
        for i in range(count):
            if (i // step + e) % 2 == 0 and i + step < count:
                pairs += [(i, i + step), (i + step, i)]
        if pairs:
            swaps.append(pairs)
    return swaps


def upward(index, e, step=1):
    return ((index // step) + e) % 2 == 0


def spec(shape):
    return jax.ShapeDtypeStruct(shape, F32)


def in_vmem(shape):
    return pltpu.VMEM(shape, F32)


def held(x):
    return pltpu.with_memory_space_constraint(x, pltpu.VMEM)


def params(mib):
    return pltpu.CompilerParams(vmem_limit_bytes=mib * MIB)


def roll_up(v, axis):
    return pltpu.roll(v, v.shape[axis] - 1, axis)


def roll_down(v, axis):
    return pltpu.roll(v, 1, axis)


def loop(low, high, body, init=None, unroll=1):
    def step(i, carry):
        if init is None:
            body(i)
            return carry
        return body(i, carry)

    carry = 0 if init is None else init
    whole = (high - low) // unroll
    if whole > 1:

        def several(k, carry):
            for j in range(unroll):
                carry = step(low + k * unroll + j, carry)
            return carry

        carry = lax.fori_loop(0, whole, several, carry)
        low += whole * unroll
    for i in range(low, high):
        carry = step(i, carry)
    return carry


def unrolling(ref):
    return UNROLL.get(ref.shape[1] * ref.shape[2] // 1024, 4)


UNROLL = {20: 4, 5: 8}


def coefficients(c, kx, ky, kz, rd, low, high, scale):
    half = 0.5 * scale

    def faces(x):
        cx = c[x]
        fx = half * (cx + c[x + 1])
        fy = half * (cx + roll_up(cx, 0))
        fz = half * (cx + roll_up(cx, 1))
        kx[x] = fx
        ky[x] = fy
        kz[x] = fz
        return cx, fx, fy, fz

    _, first, _, _ = faces(low - 1)

    def body(x, before):
        cx, fx, fy, fz = faces(x)
        diagonal = fx + before + fy + roll_down(fy, 0) + fz + roll_down(fz, 1)
        inside = cx > 0.0
        rd[x] = jnp.where(inside, relax_weight / jnp.where(inside, diagonal, 1.0), 0.0)
        return fx

    loop(low, high, body, first, unrolling(rd))


def operate(v, kx, ky, kz, low, high, use):
    def body(x, before):
        vx = v[x]
        fx = kx[x] * (vx - v[x + 1])
        fy = ky[x] * (vx - roll_up(vx, 0))
        fz = kz[x] * (vx - roll_up(vx, 1))
        use(x, vx, (fx - before) + (fy - roll_down(fy, 0)) + (fz - roll_down(fz, 1)))
        return fx

    loop(low, high, body, kx[low - 1] * (v[low - 1] - v[low]), unrolling(v))


def sweep(v, out, g, kx, ky, kz, rd, low, high):
    def use(x, vx, av):
        out[x] = vx + rd[x] * (g[x] - av)

    operate(v, kx, ky, kz, low, high, use)


def iota2(shape, dim):
    return lax.broadcasted_iota(jnp.int32, shape, dim)


def make(phase, mask, dev, x, rows=slice(None)):
    p = phase[x, rows, :]
    return floor_conduct + (1.0 - floor_conduct) * (p * p * p), mask[x, rows, :].astype(F32) * dev[x, rows, :]


def send_kernel(nx, ny, phase, mask, dev, *outs):
    ox, oy, _ = phase.shape
    bx = lax.axis_index("boxes")
    sy = lax.axis_index("sub")
    place = 0
    rows = [pl.ds(pl.multiple_of(jnp.where(upward(sy, f), oy - YH, 0), 8), YH) for f in range(ny)]
    for e in range(nx):
        up = upward(bx, e)
        face = outs[place]
        place += 1
        for x in range(XH):
            p = phase[jnp.where(up, ox - XH, 0) + x]
            face[x] = floor_conduct + (1.0 - floor_conduct) * (p * p * p)
        for x in range(GX):
            at = jnp.where(up, ox - GX, 0) + x
            face[XH + x] = mask[at].astype(F32) * dev[at]
    for f in range(ny):
        face = outs[place]
        place += 1

        def body(x, face=face, f=f):
            face[0, x], face[1, x] = make(phase, mask, dev, x, rows[f])

        loop(0, ox, body, unroll=8)
    for e in range(nx):
        up = upward(bx, e)
        for f in range(ny):
            face = outs[place]
            place += 1
            for x in range(DC):
                face[x] = make(phase, mask, dev, jnp.where(up, ox - DC, 0) + x, rows[f])[0]
            for x in range(DG):
                face[DC + x] = make(phase, mask, dev, jnp.where(up, ox - DG, 0) + x, rows[f])[1]


def pack(planes, turns, lane):
    total = None
    for b, (plane, turn) in enumerate(zip(planes, turns)):
        moved = pltpu.roll(plane, turn, 1)
        total = moved if total is None else jnp.where(lane >= ZW * b, moved, total)
    return total


def strip_turns(oz, start):
    return [lax.rem(ZW * b + oz - start, oz) for b in range(oz // ZW)]


def split(x):
    high = x.astype(BF16)
    rest = x - high.astype(F32)
    middle = rest.astype(BF16)
    low = (rest - middle.astype(F32)).astype(BF16)
    return jnp.concatenate([high, middle, low], axis=-1)


def times(x, matrix):
    return jnp.dot(split(x), matrix, preferred_element_type=F32)


def thrice(matrix):
    return jnp.concatenate([matrix.astype(BF16)] * 3, axis=0)


def own_kernel(phase, mask, dev, c, g, strip, c2, sums, work):
    ox, oy, oz = phase.shape
    pz = lax.axis_index("pair")

    def body(x):
        c[x], g[x] = make(phase, mask, dev, x)

    loop(0, ox, body, unroll=4)
    quarter = oz // 4
    i, j = iota2((oz, oz), 0), iota2((oz, oz), 1)
    matrix = thrice(jnp.where(j == oz // 2 + pz * quarter + lax.div(i, 4), 1.0 / 64.0, 0.0))
    for x in range(ox // 4):
        sums[...] = (c[4 * x] + c[4 * x + 1]) + (c[4 * x + 2] + c[4 * x + 3])
        part = [sums[pl.ds(k, oy // 4, stride=4), :] for k in range(4)]
        work[x] = (part[0] + part[1]) + (part[2] + part[3])
    c2[...] = times(work[...].reshape(-1, oz), matrix).reshape(c2.shape)
    group = oz // ZW
    turns = strip_turns(oz, jnp.where(pz == 0, oz - ZW, 0))
    lane = iota2((oy, oz), 1)
    for which, source in enumerate((c, g)):
        for a in range(ox // group):
            strip[which, a] = pack([source[group * a + b] for b in range(group)], turns, lane)


def halo_rows(ny, f, oy, up):
    if ny == 1:
        return oy
    return jnp.where(up, oy, oy + YH)


def extend_kernel(nx, ny, c, g, own, *refs):
    count = nx + ny + nx * ny
    got, (c_out, g_out, strip) = refs[:count], refs[count:]
    ox, oy, oz = c.shape
    planes, nrows, _ = c_out.shape
    bx = lax.axis_index("boxes")
    sy = lax.axis_index("sub")
    pz = lax.axis_index("pair")
    for out, source in ((c_out, c), (g_out, g)):
        for low, high in ((0, XH), (XH + ox, planes)):
            out[low:high] = jnp.zeros((high - low, nrows, oz), F32)
        out[XH:XH + ox, 0:oy, :] = source[...]
    place = 0
    row = iota2((YH, oz), 0)

    def trim(values, up):
        if ny > 1:
            return values
        return jnp.where(lax.div(row, 2) == jnp.where(up, YH // 2 - 1, 0), 0.0, values)

    def below(up, planes):
        return jnp.where(up, XH + ox, XH - planes)

    for e in range(nx):
        up = upward(bx, e)
        face = got[place]
        place += 1
        c_out[pl.ds(below(up, XH), XH), 0:oy, :] = face[0:XH]
        g_out[pl.ds(below(up, GX), GX), 0:oy, :] = face[XH:XH + GX]
    for f in range(ny):
        up = upward(sy, f)
        face = got[place]
        place += 1
        rows = pl.ds(pl.multiple_of(halo_rows(ny, f, oy, up), 8), YH)

        def copy(x, face=face, rows=rows, up=up):
            c_out[XH + x, rows, :] = trim(face[0, x], up)
            g_out[XH + x, rows, :] = trim(face[1, x], up)

        loop(0, ox, copy, unroll=8)
    for e in range(nx):
        ux = upward(bx, e)
        for f in range(ny):
            up = upward(sy, f)
            face = got[place]
            place += 1
            rows = pl.ds(pl.multiple_of(halo_rows(ny, f, oy, up), 8), YH)
            for x in range(DC):
                c_out[below(ux, DC) + x, rows, :] = trim(face[x], up)
            for x in range(DG):
                g_out[below(ux, DG) + x, rows, :] = trim(face[DC + x], up)
    group = oz // ZW
    turns = strip_turns(oz, jnp.where(pz == 0, oz - ZW, 0))
    packed = planes // group
    side = XH // group
    for which, source in enumerate((c_out, g_out)):
        for a in range(packed):
            at = which * packed + a
            if side <= a < packed - side:
                strip[at, 0:oy, :] = own[which, a - side]
                rows = slice(oy, nrows)
            else:
                rows = slice(0, nrows)
            lane = iota2((nrows - (rows.start or 0), oz), 1)
            strip[at, rows, :] = pack([source[group * a + b, rows, :] for b in range(group)], turns, lane)


def pool(source, low, high, out, matrix, work, step):
    tiles, rows, width = work.shape

    def body(k):
        sums = []
        for j in range(step):
            at = 2 * (low + step * k + j)
            total = source(at) + source(at + 1)
            parts = []
            for h in range(tiles // step):
                slot = j * (tiles // step) + h
                work[slot] = total[:, width * h:width * h + width]
                parts.append(work[slot, pl.ds(0, rows // 2, stride=2), :] + work[slot, pl.ds(1, rows // 2, stride=2), :])
            sums.append(jnp.concatenate(parts, axis=1))
        done = times(jnp.concatenate(sums, axis=0), matrix)
        out[pl.ds(step * k, step)] = done.reshape(step, rows // 2, done.shape[1])

    loop(0, (high - low) // step, body)


def pool_matrix(size_in, size_out, limit, shift, weight):
    i, j = iota2((size_in, size_out), 0), iota2((size_in, size_out), 1)
    return thrice(jnp.where((i < limit) & (j == shift + lax.div(i, 2)), weight, 0.0))


def down_kernel(nx, cpad, gpad, strip, c2, *refs):
    kx, ky, kz, rd, g, u0, kx1, ky1, kz1, rd1, c1, f1, u1, f2 = refs[:14]
    faces = refs[14:14 + nx]
    c, first, v1, work, work1 = refs[14 + nx:]
    planes, rows, oz = cpad.shape
    pz = lax.axis_index("pair")
    bx = lax.axis_index("boxes")
    group = oz // ZW
    packed = planes // group
    lane = iota2((rows, oz), 1)
    start = jnp.where(pz == 0, 0, oz - ZW)
    near = (lane >= start) & (lane < start + ZW)

    def unpack(a):
        cs, gs = strip[a], strip[packed + a]
        for b in range(group):
            x = group * a + b
            turn = lax.rem(start + oz - ZW * b, oz)
            c[x, :, 0:oz] = cpad[x]
            g[x, :, 0:oz] = gpad[x]
            c[x, :, oz:] = jnp.where(near, pltpu.roll(cs, turn, 1), 0.0)
            g[x, :, oz:] = jnp.where(near, pltpu.roll(gs, turn, 1), 0.0)

    loop(0, packed, unpack)
    edge = XH - GX
    coefficients(c, kx, ky, kz, rd, edge, planes - edge, 1.0)

    def start_sweep(x):
        first[x] = g[x] * rd[x]

    loop(edge, planes - edge, start_sweep)
    sweep(first, u0, g, kx, ky, kz, rd, edge + 1, planes - edge - 1)
    rest = first

    def use(x, vx, av):
        rest[x] = g[x] - av

    operate(u0, kx, ky, kz, edge + 2, planes - edge - 2, use)
    matrix = pool_matrix(2 * oz, oz, 2 * oz, 0, 0.125)
    planes1 = planes // 2
    pool(lambda x: c[x], 0, planes1, c1, matrix, work, 4)
    f1[...] = jnp.zeros_like(f1)
    low1 = (edge + 2) // 2
    high1 = planes1 - low1
    pool(lambda x: rest[x], low1, high1, f1.at[low1:high1], matrix, work, 4)
    coefficients(c1, kx1, ky1, kz1, rd1, 1, planes1 - 1, 0.25)

    def start_sweep1(x):
        v1[x] = f1[x] * rd1[x]

    loop(low1, high1, start_sweep1)
    u1[...] = jnp.zeros_like(u1)
    sweep(v1, u1, f1, kx1, ky1, kz1, rd1, low1 + 1, high1 - 1)
    h1 = XH // 2
    o1 = planes1 - XH

    def use1(x, vx, av):
        v1[x] = f1[x] - av

    operate(u1, kx1, ky1, kz1, h1, planes1 - h1, use1)
    half = oz // 2
    matrix1 = pool_matrix(oz, oz, half, jnp.where(pz == 0, 0, half // 2), 0.125)
    own1 = 2 * f2.shape[1]
    pool(lambda x: v1[x, 0:own1, :], h1 // 2, (planes1 - h1) // 2, f2, matrix1, work1, f2.shape[0])
    f2[...] = f2[...] + c2[...]
    for e in range(nx):
        up = upward(bx, e)
        faces[e][0:h1] = u1[pl.ds(jnp.where(up, o1, h1), h1)]
        faces[e][h1:2 * h1 - 1] = f1[pl.ds(jnp.where(up, o1 + 1, h1), h1 - 1)]


def up_kernel(nx, ny, nfar, *refs):
    kx, ky, kz, rd, g, u0, kx1, ky1, kz1, rd1, c1, f1, u1 = refs[:13]
    at = 13
    faces = refs[at:at + nx]
    at += nx
    pieces = 1 + nx + nfar
    got = refs[at:at + pieces]
    at += pieces
    field, residual = refs[at:at + 2]
    at += 2
    ua, ub, v1, w1, g1, c2, f2, kx2, ky2, kz2, rd2, v2, w2, tall, wide = refs[at:]
    planes, rows, lanes = u0.shape
    planes1, rows1, oz = u1.shape
    planes2, rows2, _ = c2.shape
    ox, oy, _ = field.shape
    bx = lax.axis_index("boxes")
    sy = lax.axis_index("sub")
    pz = lax.axis_index("pair")
    o2x, o2y = ox // 4, oy // 4

    c2[...] = jnp.zeros_like(c2)
    f2[...] = jnp.zeros_like(f2)
    lower = iota2((o2y, oz), 1) < oz // 2
    places = [(L2X, o2x)]
    for e in range(nx):
        places.append((jnp.where(upward(bx, e), L2X + o2x, L2X - o2x), o2x))
    for e in range(nfar):
        places.append((jnp.where(upward(bx, e, 2), L2X + 2 * o2x, 0), L2X - o2x))
    for (x0, count), piece in zip(places, got):
        for f in range(ny + 1):
            if f == 0:
                y0 = 0
            else:
                y0 = pl.multiple_of(jnp.where(upward(sy, f - 1), o2y, rows2 - o2y), 8)
            for x in range(count):
                values = piece[f, x]
                f2[x0 + x, pl.ds(y0, o2y), :] = jnp.where(lower, values, 0.0)
                c2[x0 + x, pl.ds(y0, o2y), :] = jnp.where(lower, pltpu.roll(values, oz // 2, 1), 0.0)
    coefficients(c2, kx2, ky2, kz2, rd2, 1, planes2 - 1, 0.0625)

    def start_sweep2(x):
        v2[x] = f2[x] * rd2[x]

    loop(1, planes2 - 1, start_sweep2)
    old, new = v2, w2
    for k in range(2, BOTTOM_SWEEPS + 1):
        sweep(old, new, f2, kx2, ky2, kz2, rd2, k, planes2 - k)
        old, new = new, old

    h1 = XH // 2
    o1 = planes1 - XH
    for x in range(planes1):
        g1[x] = f1[x]
        v1[x] = u1[x]
    for e in range(nx):
        up = upward(bx, e)
        v1[pl.ds(jnp.where(up, planes1 - h1, 0), h1)] = faces[e][0:h1]
        g1[pl.ds(jnp.where(up, planes1 - h1, 1), h1 - 1)] = faces[e][h1:2 * h1 - 1]
    i, j = iota2((oz, oz), 0), iota2((oz, oz), 1)
    spread_z = thrice(jnp.where(i == lax.div(lax.rem(pz * (oz // 2) + j, oz), 2), 1.0, 0.0))
    base = L2X - h1 // 2
    count = planes1 // 2
    moved = times(old[base:base + count].reshape(count * rows2, oz), spread_z)
    row = iota2((8, oz), 0)
    for x in range(count):
        t = moved[x * rows2:x * rows2 + rows2]
        if ny == 1:
            halo = jnp.where(upward(sy, 0), t[o2y:o2y + 8], pltpu.roll(t[rows2 - 8:], 4, 0))
        else:
            halo = jnp.where(row < 4, t[o2y:o2y + 8], t[rows2 - 8:])
        t = jnp.concatenate([t[0:o2y], halo], axis=0)
        tall[x, pl.ds(0, o2y + 8, stride=2), :] = t
        tall[x, pl.ds(1, o2y + 8, stride=2), :] = t
        both = tall[x, 0:rows1, :]
        for k in range(2):
            y = 2 * x + k
            v1[y] = jnp.where(c1[y] > 0.0, v1[y] + both, 0.0)

    sweep(v1, w1, g1, kx1, ky1, kz1, rd1, 1, planes1 - 1)
    sweep(w1, v1, g1, kx1, ky1, kz1, rd1, 2, planes1 - 2)

    i, j = iota2((oz, lanes), 0), iota2((oz, lanes), 1)
    spread_z0 = thrice(jnp.where(i == lax.div(j, 2), 1.0, 0.0))
    step = 4

    def spread0(n):
        low = 2 + step * n
        moved = times(v1[pl.ds(low, step)].reshape(step * rows1, oz), spread_z0)
        for m in range(step):
            for h in range(lanes // oz):
                cols = slice(oz * h, oz * h + oz)
                values = moved[m * rows1:m * rows1 + rows1, cols]
                wide[2 * m + h, pl.ds(0, rows1, stride=2), :] = values
                wide[2 * m + h, pl.ds(1, rows1, stride=2), :] = values
                for k in range(2):
                    y = 2 * (low + m) + k
                    ua[y, :, cols] = jnp.where(rd[y, :, cols] > 0.0, u0[y, :, cols] + wide[2 * m + h], 0.0)

    loop(0, (planes1 - 4) // step, spread0)
    sweep(ua, ub, g, kx, ky, kz, rd, XH - 2, planes - XH + 2)
    sweep(ub, ua, g, kx, ky, kz, rd, XH - 1, planes - XH + 1)

    def use(x, vx, av):
        field[x - XH] = vx[0:oy, 0:oz]
        residual[x - XH] = g[x, 0:oy, 0:oz] - av[0:oy, 0:oz]

    operate(ua, kx, ky, kz, XH, planes - XH, use)


def call(kernel, outs, scratch=(), mib=60):
    return pl.pallas_call(
        kernel,
        out_shape=tuple(outs),
        scratch_shapes=tuple(pltpu.VMEM(s, F32) for s in scratch),
        compiler_params=params(mib),
    )


def per_device(phase, target_mask, deviation):
    ox, oy, oz = phase.shape
    nbox, nsub = lax.axis_size("boxes"), lax.axis_size("sub")
    swap_x, swap_y, far_x = exchanges(nbox), exchanges(nsub), exchanges(nbox, 2)
    nx, ny, nfar = len(swap_x), len(swap_y), len(far_x)
    pair_swap = [(0, 1), (1, 0)]

    def both(px, py):
        return [(a * nsub + c, b * nsub + d) for a, b in px for c, d in py]

    def traded(faces):
        out = []
        for e in range(nx):
            out.append(lax.ppermute(faces[e], "boxes", swap_x[e]))
        for f in range(ny):
            out.append(lax.ppermute(faces[nx + f], "sub", swap_y[f]))
        for e in range(nx):
            for f in range(ny):
                out.append(lax.ppermute(faces[nx + ny + e * ny + f], ("boxes", "sub"), both(swap_x[e], swap_y[f])))
        return out

    def gathered(own):
        line = own + lax.ppermute(own, "pair", pair_swap)
        sheet = jnp.stack([line] + [lax.ppermute(line, "sub", p) for p in swap_y])
        out = [sheet]
        for p in swap_x:
            out.append(lax.ppermute(sheet, "boxes", p))
        for e, p in enumerate(far_x):
            count = L2X - ox // 4
            at = jnp.where(upward(lax.axis_index("boxes"), e, 2), ox // 4 - count, 0)
            out.append(lax.ppermute(lax.dynamic_slice_in_dim(sheet, at, count, axis=1), "boxes", p))
        return out

    planes, rows = ox + 2 * XH, oy + YH * ny
    planes1, rows1 = planes // 2, rows // 2
    o2x, o2y = ox // 4, oy // 4
    planes2 = o2x + 2 * L2X
    rows2 = o2y * (ny + 1) + (8 if ny == 1 else 0)

    box = spec((ox, oy, oz))
    faces = [spec((XH + GX, oy, oz))] * nx + [spec((2, ox, YH, oz))] * ny + [spec((DC + DG, YH, oz))] * (nx * ny)
    faces = call(lambda *r: send_kernel(nx, ny, *r), faces)(phase, target_mask, deviation)
    got = traded(faces)
    phase, target_mask, deviation, _ = lax.optimization_barrier((phase, target_mask, deviation, faces))
    group = oz // ZW
    c, g, own, c2 = call(
        own_kernel,
        [in_vmem((ox, oy, oz)), in_vmem((ox, oy, oz)), in_vmem((2, ox // group, oy, oz)), spec((o2x, o2y, oz))],
        [(oy, oz), (o2x, o2y, oz)],
        mib=24,
    )(phase, target_mask, deviation)
    padded = (planes, rows, oz)
    cpad, gpad, strip = call(
        lambda *r: extend_kernel(nx, ny, *r),
        [in_vmem(padded), in_vmem(padded), spec((2 * planes // group, rows, oz))],
        mib=24,
    )(held(c), held(g), held(own), *got)
    strip = lax.ppermute(strip, "pair", pair_swap)
    fine = (planes, rows, 2 * oz)
    middle = (planes1, rows1, oz)
    down = call(
        lambda *r: down_kernel(nx, *r),
        [in_vmem(fine)] * 6 + [in_vmem(middle)] * 7 + [spec((o2x, o2y, oz))] + [spec((XH - 1, rows1, oz))] * nx,
        [fine, fine, middle, (8, rows, oz), (o2x, oy // 2, oz)],
        mib=24,
    )(held(cpad), held(gpad), strip, c2)
    kept, f2, sides = down[:13], down[13], down[14:]
    sides = [lax.ppermute(s, "boxes", p) for s, p in zip(sides, swap_x)]
    got = gathered(f2)
    lowest = (planes2, rows2, oz)
    return tuple(call(
        lambda *r: up_kernel(nx, ny, nfar, *r),
        [box, box],
        [fine, fine, middle, middle, middle] + [lowest] * 8 + [(planes1 // 2, 2 * (o2y + 8), oz), (8, rows, oz)],
        mib=24,
    )(*[held(x) for x in kept], *sides, *got))


def solution(mesh):
    where = P(("groups", "boxes"), "sub", "pair")
    return jax.shard_map(
        per_device,
        mesh=mesh,
        in_specs=(where, where, where),
        out_specs=(where, where),
        check_vma=False,
    )
```

```python
import jax
import jax.numpy as jnp
from jax import lax
from jax.experimental import pallas as pl
from jax.experimental.pallas import tpu as pltpu
from jax.sharding import PartitionSpec as P

SWEEPS = 2
BOTTOM_SWEEPS = 8

floor_conduct = 0.1
relax_weight = 0.8

XH = 8
YH = 16
GX = 6
DC, DG = 6, 5
ZW = 16
L2X = 10
F32 = jnp.float32
BF16 = jnp.bfloat16
MIB = 1 << 20


def exchanges(count, step=1):
    swaps = []
    for e in range(2):
        pairs = []
        for i in range(count):
            if (i // step + e) % 2 == 0 and i + step < count:
                pairs += [(i, i + step), (i + step, i)]
        if pairs:
            swaps.append(pairs)
    return swaps


def upward(index, e, step=1):
    return ((index // step) + e) % 2 == 0


def spec(shape):
    return jax.ShapeDtypeStruct(shape, F32)


def in_vmem(shape):
    return pltpu.VMEM(shape, F32)


def held(x):
    return pltpu.with_memory_space_constraint(x, pltpu.VMEM)


def params(mib):
    return pltpu.CompilerParams(vmem_limit_bytes=mib * MIB)


def roll_up(v, axis):
    return pltpu.roll(v, v.shape[axis] - 1, axis)


def roll_down(v, axis):
    return pltpu.roll(v, 1, axis)


def loop(low, high, body, init=None, unroll=1):
    def step(i, carry):
        if init is None:
            body(i)
            return carry
        return body(i, carry)

    carry = 0 if init is None else init
    whole = (high - low) // unroll
    if whole > 1:

        def several(k, carry):
            for j in range(unroll):
                carry = step(low + k * unroll + j, carry)
            return carry

        carry = lax.fori_loop(0, whole, several, carry)
        low += whole * unroll
    for i in range(low, high):
        carry = step(i, carry)
    return carry


def unrolling(ref):
    return UNROLL.get(ref.shape[1] * ref.shape[2] // 1024, 4)


UNROLL = {20: 4, 5: 8}


def coefficients(c, kx, ky, kz, rd, low, high, scale):
    half = 0.5 * scale

    def faces(x):
        cx = c[x]
        fx = half * (cx + c[x + 1])
        fy = half * (cx + roll_up(cx, 0))
        fz = half * (cx + roll_up(cx, 1))
        kx[x] = fx
        ky[x] = fy
        kz[x] = fz
        return cx, fx, fy, fz

    _, first, _, _ = faces(low - 1)

    def body(x, before):
        cx, fx, fy, fz = faces(x)
        diagonal = fx + before + fy + roll_down(fy, 0) + fz + roll_down(fz, 1)
        inside = cx > 0.0
        rd[x] = jnp.where(inside, relax_weight / jnp.where(inside, diagonal, 1.0), 0.0)
        return fx

    loop(low, high, body, first, unrolling(rd))


def operate(v, kx, ky, kz, low, high, use):
    def body(x, before):
        vx = v[x]
        fx = kx[x] * (vx - v[x + 1])
        fy = ky[x] * (vx - roll_up(vx, 0))
        fz = kz[x] * (vx - roll_up(vx, 1))
        use(x, vx, (fx - before) + (fy - roll_down(fy, 0)) + (fz - roll_down(fz, 1)))
        return fx

    loop(low, high, body, kx[low - 1] * (v[low - 1] - v[low]), unrolling(v))


def sweep(v, out, g, kx, ky, kz, rd, low, high):
    def use(x, vx, av):
        out[x] = vx + rd[x] * (g[x] - av)

    operate(v, kx, ky, kz, low, high, use)


def iota2(shape, dim):
    return lax.broadcasted_iota(jnp.int32, shape, dim)


def make(phase, mask, dev, x, rows=slice(None)):
    p = phase[x, rows, :]
    return floor_conduct + (1.0 - floor_conduct) * (p * p * p), mask[x, rows, :].astype(F32) * dev[x, rows, :]


def send_kernel(nx, ny, phase, mask, dev, *outs):
    ox, oy, _ = phase.shape
    bx = lax.axis_index("boxes")
    sy = lax.axis_index("sub")
    place = 0
    rows = [pl.ds(pl.multiple_of(jnp.where(upward(sy, f), oy - YH, 0), 8), YH) for f in range(ny)]
    for e in range(nx):
        up = upward(bx, e)
        face = outs[place]
        place += 1
        for x in range(XH):
            p = phase[jnp.where(up, ox - XH, 0) + x]
            face[x] = floor_conduct + (1.0 - floor_conduct) * (p * p * p)
        for x in range(GX):
            at = jnp.where(up, ox - GX, 0) + x
            face[XH + x] = mask[at].astype(F32) * dev[at]
    for f in range(ny):
        face = outs[place]
        place += 1

        def body(x, face=face, f=f):
            face[0, x], face[1, x] = make(phase, mask, dev, x, rows[f])

        loop(0, ox, body, unroll=8)
    for e in range(nx):
        up = upward(bx, e)
        for f in range(ny):
            face = outs[place]
            place += 1
            for x in range(DC):
                face[x] = make(phase, mask, dev, jnp.where(up, ox - DC, 0) + x, rows[f])[0]
            for x in range(DG):
                face[DC + x] = make(phase, mask, dev, jnp.where(up, ox - DG, 0) + x, rows[f])[1]


def pack(planes, turns, lane):
    total = None
    for b, (plane, turn) in enumerate(zip(planes, turns)):
        moved = pltpu.roll(plane, turn, 1)
        total = moved if total is None else jnp.where(lane >= ZW * b, moved, total)
    return total


def strip_turns(oz, start):
    return [lax.rem(ZW * b + oz - start, oz) for b in range(oz // ZW)]


def split(x):
    high = x.astype(BF16)
    rest = x - high.astype(F32)
    middle = rest.astype(BF16)
    low = (rest - middle.astype(F32)).astype(BF16)
    return jnp.concatenate([high, middle, low], axis=-1)


def times(x, matrix):
    return jnp.dot(split(x), matrix, preferred_element_type=F32)


def thrice(matrix):
    return jnp.concatenate([matrix.astype(BF16)] * 3, axis=0)


def own_kernel(phase, mask, dev, c, g, strip, c2, sums, work):
    ox, oy, oz = phase.shape
    pz = lax.axis_index("pair")

    def body(x):
        c[x], g[x] = make(phase, mask, dev, x)

    loop(0, ox, body, unroll=4)
    quarter = oz // 4
    i, j = iota2((oz, oz), 0), iota2((oz, oz), 1)
    matrix = thrice(jnp.where(j == oz // 2 + pz * quarter + lax.div(i, 4), 1.0 / 64.0, 0.0))
    for x in range(ox // 4):
        sums[...] = (c[4 * x] + c[4 * x + 1]) + (c[4 * x + 2] + c[4 * x + 3])
        part = [sums[pl.ds(k, oy // 4, stride=4), :] for k in range(4)]
        work[x] = (part[0] + part[1]) + (part[2] + part[3])
    c2[...] = times(work[...].reshape(-1, oz), matrix).reshape(c2.shape)
    group = oz // ZW
    turns = strip_turns(oz, jnp.where(pz == 0, oz - ZW, 0))
    lane = iota2((oy, oz), 1)
    for which, source in enumerate((c, g)):
        for a in range(ox // group):
            strip[which, a] = pack([source[group * a + b] for b in range(group)], turns, lane)


def halo_rows(ny, f, oy, up):
    if ny == 1:
        return oy
    return jnp.where(up, oy, oy + YH)


def extend_kernel(nx, ny, c, g, own, *refs):
    count = nx + ny + nx * ny
    got, (c_out, g_out, strip) = refs[:count], refs[count:]
    ox, oy, oz = c.shape
    planes, nrows, _ = c_out.shape
    bx = lax.axis_index("boxes")
    sy = lax.axis_index("sub")
    pz = lax.axis_index("pair")
    for out, source in ((c_out, c), (g_out, g)):
        for low, high in ((0, XH), (XH + ox, planes)):
            out[low:high] = jnp.zeros((high - low, nrows, oz), F32)
        out[XH:XH + ox, 0:oy, :] = source[...]
    place = 0
    row = iota2((YH, oz), 0)

    def trim(values, up):
        if ny > 1:
            return values
        return jnp.where(lax.div(row, 2) == jnp.where(up, YH // 2 - 1, 0), 0.0, values)

    def below(up, planes):
        return jnp.where(up, XH + ox, XH - planes)

    for e in range(nx):
        up = upward(bx, e)
        face = got[place]
        place += 1
        c_out[pl.ds(below(up, XH), XH), 0:oy, :] = face[0:XH]
        g_out[pl.ds(below(up, GX), GX), 0:oy, :] = face[XH:XH + GX]
    for f in range(ny):
        up = upward(sy, f)
        face = got[place]
        place += 1
        rows = pl.ds(pl.multiple_of(halo_rows(ny, f, oy, up), 8), YH)

        def copy(x, face=face, rows=rows, up=up):
            c_out[XH + x, rows, :] = trim(face[0, x], up)
            g_out[XH + x, rows, :] = trim(face[1, x], up)

        loop(0, ox, copy, unroll=8)
    for e in range(nx):
        ux = upward(bx, e)
        for f in range(ny):
            up = upward(sy, f)
            face = got[place]
            place += 1
            rows = pl.ds(pl.multiple_of(halo_rows(ny, f, oy, up), 8), YH)
            for x in range(DC):
                c_out[below(ux, DC) + x, rows, :] = trim(face[x], up)
            for x in range(DG):
                g_out[below(ux, DG) + x, rows, :] = trim(face[DC + x], up)
    group = oz // ZW
    turns = strip_turns(oz, jnp.where(pz == 0, oz - ZW, 0))
    packed = planes // group
    side = XH // group
    for which, source in enumerate((c_out, g_out)):
        for a in range(packed):
            at = which * packed + a
            if side <= a < packed - side:
                strip[at, 0:oy, :] = own[which, a - side]
                rows = slice(oy, nrows)
            else:
                rows = slice(0, nrows)
            lane = iota2((nrows - (rows.start or 0), oz), 1)
            strip[at, rows, :] = pack([source[group * a + b, rows, :] for b in range(group)], turns, lane)


def pool(source, low, high, out, matrix, work, step):
    tiles, rows, width = work.shape

    def body(k):
        sums = []
        for j in range(step):
            at = 2 * (low + step * k + j)
            total = source(at) + source(at + 1)
            parts = []
            for h in range(tiles // step):
                slot = j * (tiles // step) + h
                work[slot] = total[:, width * h:width * h + width]
                parts.append(work[slot, pl.ds(0, rows // 2, stride=2), :] + work[slot, pl.ds(1, rows // 2, stride=2), :])
            sums.append(jnp.concatenate(parts, axis=1))
        done = times(jnp.concatenate(sums, axis=0), matrix)
        out[pl.ds(step * k, step)] = done.reshape(step, rows // 2, done.shape[1])

    loop(0, (high - low) // step, body)


def pool_matrix(size_in, size_out, limit, shift, weight):
    i, j = iota2((size_in, size_out), 0), iota2((size_in, size_out), 1)
    return thrice(jnp.where((i < limit) & (j == shift + lax.div(i, 2)), weight, 0.0))


KEPT = 13
SKIP = XH - 3


def inner(ref, out):
    skip = (ref.shape[0] - out.shape[0]) // 2
    return ref.at[skip:ref.shape[0] - skip]


def down_kernel(nx, cpad, gpad, strip, c2, *refs):
    kept, f2 = refs[:KEPT], refs[KEPT]
    faces = refs[KEPT + 1:KEPT + 1 + nx]
    held_here = refs[KEPT + 1 + nx:2 * KEPT + 1 + nx]
    kx, ky, kz, rd, g, u0, kx1, ky1, kz1, rd1, c1, f1, u1 = held_here
    c, first, v1, work, work1, sems = refs[2 * KEPT + 1 + nx:]
    copies = [pltpu.make_async_copy(inner(a, k), k, sems.at[i]) for i, (a, k) in enumerate(zip(held_here, kept))]
    planes, rows, oz = cpad.shape
    pz = lax.axis_index("pair")
    bx = lax.axis_index("boxes")
    group = oz // ZW
    packed = planes // group
    lane = iota2((rows, oz), 1)
    start = jnp.where(pz == 0, 0, oz - ZW)
    near = (lane >= start) & (lane < start + ZW)

    def unpack(a):
        cs, gs = strip[a], strip[packed + a]
        for b in range(group):
            x = group * a + b
            turn = lax.rem(start + oz - ZW * b, oz)
            c[x, :, 0:oz] = cpad[x]
            g[x, :, 0:oz] = gpad[x]
            c[x, :, oz:] = jnp.where(near, pltpu.roll(cs, turn, 1), 0.0)
            g[x, :, oz:] = jnp.where(near, pltpu.roll(gs, turn, 1), 0.0)

    loop(0, packed, unpack)
    edge = XH - GX
    coefficients(c, kx, ky, kz, rd, edge, planes - edge, 1.0)
    for copy in copies[0:5]:
        copy.start()

    def start_sweep(x):
        first[x] = g[x] * rd[x]

    loop(edge, planes - edge, start_sweep)
    sweep(first, u0, g, kx, ky, kz, rd, edge + 1, planes - edge - 1)
    copies[5].start()
    rest = first

    def use(x, vx, av):
        rest[x] = g[x] - av

    operate(u0, kx, ky, kz, edge + 2, planes - edge - 2, use)
    matrix = pool_matrix(2 * oz, oz, 2 * oz, 0, 0.125)
    planes1 = planes // 2
    pool(lambda x: c[x], 0, planes1, c1, matrix, work, 4)
    f1[...] = jnp.zeros_like(f1)
    low1 = (edge + 2) // 2
    high1 = planes1 - low1
    pool(lambda x: rest[x], low1, high1, f1.at[low1:high1], matrix, work, 4)
    coefficients(c1, kx1, ky1, kz1, rd1, 1, planes1 - 1, 0.25)

    def start_sweep1(x):
        v1[x] = f1[x] * rd1[x]

    loop(low1, high1, start_sweep1)
    u1[...] = jnp.zeros_like(u1)
    sweep(v1, u1, f1, kx1, ky1, kz1, rd1, low1 + 1, high1 - 1)
    for copy in copies[6:]:
        copy.start()
    h1 = XH // 2
    o1 = planes1 - XH

    def use1(x, vx, av):
        v1[x] = f1[x] - av

    operate(u1, kx1, ky1, kz1, h1, planes1 - h1, use1)
    half = oz // 2
    matrix1 = pool_matrix(oz, oz, half, jnp.where(pz == 0, 0, half // 2), 0.125)
    own1 = 2 * f2.shape[1]
    pool(lambda x: v1[x, 0:own1, :], h1 // 2, (planes1 - h1) // 2, f2, matrix1, work1, f2.shape[0])
    f2[...] = f2[...] + c2[...]
    for e in range(nx):
        up = upward(bx, e)
        faces[e][0:h1] = u1[pl.ds(jnp.where(up, o1, h1), h1)]
        faces[e][h1:2 * h1 - 1] = f1[pl.ds(jnp.where(up, o1 + 1, h1), h1 - 1)]
    for copy in copies:
        copy.wait()


def up_kernel(nx, ny, nfar, *refs):
    kept = refs[:KEPT]
    at = KEPT
    faces = refs[at:at + nx]
    at += nx
    pieces = 1 + nx + nfar
    got = refs[at:at + pieces]
    at += pieces
    field, residual = refs[at:at + 2]
    at += 2
    held_here = refs[at:at + KEPT]
    at += KEPT
    kx, ky, kz, rd, g, u0, kx1, ky1, kz1, rd1, c1, f1, u1 = held_here
    ua, ub, v1, w1, c2, f2, kx2, ky2, kz2, rd2, v2, w2, tall, wide, sems = refs[at:]
    copies = [pltpu.make_async_copy(k, inner(a, k), sems.at[i]) for i, (a, k) in enumerate(zip(held_here, kept))]
    for copy in copies[6:] + copies[:6]:
        copy.start()
    planes, rows, lanes = u0.shape
    planes1, rows1, oz = u1.shape
    planes2, rows2, _ = c2.shape
    ox, oy, _ = field.shape
    bx = lax.axis_index("boxes")
    sy = lax.axis_index("sub")
    pz = lax.axis_index("pair")
    o2x, o2y = ox // 4, oy // 4

    c2[...] = jnp.zeros_like(c2)
    f2[...] = jnp.zeros_like(f2)
    lower = iota2((o2y, oz), 1) < oz // 2
    places = [(L2X, o2x)]
    for e in range(nx):
        places.append((jnp.where(upward(bx, e), L2X + o2x, L2X - o2x), o2x))
    for e in range(nfar):
        places.append((jnp.where(upward(bx, e, 2), L2X + 2 * o2x, 0), L2X - o2x))
    for (x0, count), piece in zip(places, got):
        for f in range(ny + 1):
            if f == 0:
                y0 = 0
            else:
                y0 = pl.multiple_of(jnp.where(upward(sy, f - 1), o2y, rows2 - o2y), 8)
            for x in range(count):
                values = piece[f, x]
                f2[x0 + x, pl.ds(y0, o2y), :] = jnp.where(lower, values, 0.0)
                c2[x0 + x, pl.ds(y0, o2y), :] = jnp.where(lower, pltpu.roll(values, oz // 2, 1), 0.0)
    coefficients(c2, kx2, ky2, kz2, rd2, 1, planes2 - 1, 0.0625)

    def start_sweep2(x):
        v2[x] = f2[x] * rd2[x]

    loop(1, planes2 - 1, start_sweep2)
    old, new = v2, w2
    for k in range(2, BOTTOM_SWEEPS + 1):
        sweep(old, new, f2, kx2, ky2, kz2, rd2, k, planes2 - k)
        old, new = new, old

    h1 = XH // 2
    o1 = planes1 - XH
    for copy in copies[6:]:
        copy.wait()
    for e in range(nx):
        up = upward(bx, e)
        u1[pl.ds(jnp.where(up, planes1 - h1, 0), h1)] = faces[e][0:h1]
        f1[pl.ds(jnp.where(up, planes1 - h1, 1), h1 - 1)] = faces[e][h1:2 * h1 - 1]
    i, j = iota2((oz, oz), 0), iota2((oz, oz), 1)
    spread_z = thrice(jnp.where(i == lax.div(lax.rem(pz * (oz // 2) + j, oz), 2), 1.0, 0.0))
    base = L2X - h1 // 2
    count = planes1 // 2
    moved = times(old[base:base + count].reshape(count * rows2, oz), spread_z)
    row = iota2((8, oz), 0)
    for x in range(count):
        t = moved[x * rows2:x * rows2 + rows2]
        if ny == 1:
            halo = jnp.where(upward(sy, 0), t[o2y:o2y + 8], pltpu.roll(t[rows2 - 8:], 4, 0))
        else:
            halo = jnp.where(row < 4, t[o2y:o2y + 8], t[rows2 - 8:])
        t = jnp.concatenate([t[0:o2y], halo], axis=0)
        tall[x, pl.ds(0, o2y + 8, stride=2), :] = t
        tall[x, pl.ds(1, o2y + 8, stride=2), :] = t
        both = tall[x, 0:rows1, :]
        for k in range(2):
            y = 2 * x + k
            v1[y] = jnp.where(c1[y] > 0.0, u1[y] + both, 0.0)

    sweep(v1, w1, f1, kx1, ky1, kz1, rd1, 1, planes1 - 1)
    sweep(w1, v1, f1, kx1, ky1, kz1, rd1, 2, planes1 - 2)

    i, j = iota2((oz, lanes), 0), iota2((oz, lanes), 1)
    spread_z0 = thrice(jnp.where(i == lax.div(j, 2), 1.0, 0.0))
    step = 4
    for copy in copies[:6]:
        copy.wait()

    def spread0(n):
        low = 2 + step * n
        moved = times(v1[pl.ds(low, step)].reshape(step * rows1, oz), spread_z0)
        for m in range(step):
            for h in range(lanes // oz):
                cols = slice(oz * h, oz * h + oz)
                values = moved[m * rows1:m * rows1 + rows1, cols]
                wide[2 * m + h, pl.ds(0, rows1, stride=2), :] = values
                wide[2 * m + h, pl.ds(1, rows1, stride=2), :] = values
                for k in range(2):
                    y = 2 * (low + m) + k
                    ua[y, :, cols] = jnp.where(rd[y, :, cols] > 0.0, u0[y, :, cols] + wide[2 * m + h], 0.0)

    loop(0, (planes1 - 4) // step, spread0)
    sweep(ua, ub, g, kx, ky, kz, rd, XH - 2, planes - XH + 2)
    sweep(ub, ua, g, kx, ky, kz, rd, XH - 1, planes - XH + 1)

    def use(x, vx, av):
        field[x - XH] = vx[0:oy, 0:oz]
        residual[x - XH] = g[x, 0:oy, 0:oz] - av[0:oy, 0:oz]

    operate(ua, kx, ky, kz, XH, planes - XH, use)


def call(kernel, outs, scratch=(), mib=16, raw_in=0, raw_out=0, copies=0):
    where = [pl.BlockSpec(memory_space=pl.ANY)], [pl.BlockSpec(memory_space=pltpu.VMEM)]
    outs = tuple(outs)
    extra = (pltpu.SemaphoreType.DMA((copies,)),) if copies else ()

    def run(*operands):
        return pl.pallas_call(
            kernel,
            in_specs=where[0] * raw_in + where[1] * (len(operands) - raw_in),
            out_specs=tuple(where[0] * raw_out + where[1] * (len(outs) - raw_out)),
            out_shape=outs,
            scratch_shapes=tuple(pltpu.VMEM(s, F32) for s in scratch) + extra,
            compiler_params=params(mib),
        )(*operands)

    return run


def per_device(phase, target_mask, deviation):
    ox, oy, oz = phase.shape
    nbox, nsub = lax.axis_size("boxes"), lax.axis_size("sub")
    swap_x, swap_y, far_x = exchanges(nbox), exchanges(nsub), exchanges(nbox, 2)
    nx, ny, nfar = len(swap_x), len(swap_y), len(far_x)
    pair_swap = [(0, 1), (1, 0)]

    def both(px, py):
        return [(a * nsub + c, b * nsub + d) for a, b in px for c, d in py]

    def traded(faces):
        out = []
        for e in range(nx):
            out.append(lax.ppermute(faces[e], "boxes", swap_x[e]))
        for f in range(ny):
            out.append(lax.ppermute(faces[nx + f], "sub", swap_y[f]))
        for e in range(nx):
            for f in range(ny):
                out.append(lax.ppermute(faces[nx + ny + e * ny + f], ("boxes", "sub"), both(swap_x[e], swap_y[f])))
        return out

    def gathered(own):
        line = own + lax.ppermute(own, "pair", pair_swap)
        sheet = jnp.stack([line] + [lax.ppermute(line, "sub", p) for p in swap_y])
        out = [sheet]
        for p in swap_x:
            out.append(lax.ppermute(sheet, "boxes", p))
        for e, p in enumerate(far_x):
            count = L2X - ox // 4
            at = jnp.where(upward(lax.axis_index("boxes"), e, 2), ox // 4 - count, 0)
            out.append(lax.ppermute(lax.dynamic_slice_in_dim(sheet, at, count, axis=1), "boxes", p))
        return out

    planes, rows = ox + 2 * XH, oy + YH * ny
    planes1, rows1 = planes // 2, rows // 2
    o2x, o2y = ox // 4, oy // 4
    planes2 = o2x + 2 * L2X
    rows2 = o2y * (ny + 1) + (8 if ny == 1 else 0)

    box = spec((ox, oy, oz))
    faces = [spec((XH + GX, oy, oz))] * nx + [spec((2, ox, YH, oz))] * ny + [spec((DC + DG, YH, oz))] * (nx * ny)
    faces = call(lambda *r: send_kernel(nx, ny, *r), faces)(phase, target_mask, deviation)
    got = traded(faces)
    phase, target_mask, deviation, _ = lax.optimization_barrier((phase, target_mask, deviation, faces))
    group = oz // ZW
    c, g, own, c2 = call(
        own_kernel,
        [in_vmem((ox, oy, oz)), in_vmem((ox, oy, oz)), in_vmem((2, ox // group, oy, oz)), spec((o2x, o2y, oz))],
        [(oy, oz), (o2x, o2y, oz)],
        mib=24,
    )(phase, target_mask, deviation)
    padded = (planes, rows, oz)
    cpad, gpad, strip = call(
        lambda *r: extend_kernel(nx, ny, *r),
        [in_vmem(padded), in_vmem(padded), spec((2 * planes // group, rows, oz))],
        mib=24,
    )(held(c), held(g), held(own), *got)
    strip = lax.ppermute(strip, "pair", pair_swap)
    fine = (planes, rows, 2 * oz)
    middle = (planes1, rows1, oz)
    small = (planes - 2 * SKIP, rows, 2 * oz)
    down = call(
        lambda *r: down_kernel(nx, *r),
        [spec(small)] * 6 + [spec(middle)] * 7 + [spec((o2x, o2y, oz))] + [spec((XH - 1, rows1, oz))] * nx,
        [fine] * 6 + [middle] * 7 + [fine, fine, middle, (8, rows, oz), (o2x, oy // 2, oz)],
        mib=48,
        raw_out=KEPT,
        copies=KEPT,
    )(held(cpad), held(gpad), strip, c2)
    kept, f2, sides = down[:KEPT], down[KEPT], down[KEPT + 1:]
    sides = [lax.ppermute(s, "boxes", p) for s, p in zip(sides, swap_x)]
    got = gathered(f2)
    lowest = (planes2, rows2, oz)
    return tuple(call(
        lambda *r: up_kernel(nx, ny, nfar, *r),
        [box, box],
        [fine] * 6 + [middle] * 7 + [fine, fine, middle, middle] + [lowest] * 8
        + [(planes1 // 2, 2 * (o2y + 8), oz), (8, rows, oz)],
        mib=52,
        raw_in=KEPT,
        copies=KEPT,
    )(*kept, *sides, *got))


def solution(mesh):
    where = P(("groups", "boxes"), "sub", "pair")
    return jax.shard_map(
        per_device,
        mesh=mesh,
        in_specs=(where, where, where),
        out_specs=(where, where),
        check_vma=False,
    )
```

```python
import jax
import jax.numpy as jnp
from jax import lax
from jax.experimental import pallas as pl
from jax.experimental.pallas import tpu as pltpu
from jax.sharding import PartitionSpec as P

SWEEPS = 2
BOTTOM_SWEEPS = 8

floor_conduct = 0.1
relax_weight = 0.8

XH = 8
YH = 16
GX = 6
DC, DG = 6, 5
ZW = 16
L2X = 10
F32 = jnp.float32
BF16 = jnp.bfloat16
MIB = 1 << 20


def exchanges(count, step=1):
    swaps = []
    for e in range(2):
        pairs = []
        for i in range(count):
            if (i // step + e) % 2 == 0 and i + step < count:
                pairs += [(i, i + step), (i + step, i)]
        if pairs:
            swaps.append(pairs)
    return swaps


def upward(index, e, step=1):
    return (index // step + e) % 2 == 0


def spec(shape):
    return jax.ShapeDtypeStruct(shape, F32)


def in_vmem(shape):
    return pltpu.VMEM(shape, F32)


def in_hbm(shape):
    return pltpu.HBM(shape, F32)


def held(x):
    return pltpu.with_memory_space_constraint(x, pltpu.VMEM)


def params(mib):
    return pltpu.CompilerParams(vmem_limit_bytes=mib * MIB)


def roll_up(v, axis):
    return pltpu.roll(v, v.shape[axis] - 1, axis)


def roll_down(v, axis):
    return pltpu.roll(v, 1, axis)


def next_z(v):
    half = v.shape[1] // 2
    if half < 128:
        return roll_up(v, 1)
    return jnp.concatenate([v[:, half:], roll_up(v[:, :half], 1)], axis=1)


def previous_z(v):
    half = v.shape[1] // 2
    if half < 128:
        return roll_down(v, 1)
    return jnp.concatenate([roll_down(v[:, half:], 1), v[:, :half]], axis=1)


def pick(v, lanes):
    return jnp.take_along_axis(v, lanes, axis=1)


def parted(v):
    lane = iota2(v.shape, 1)
    even = lax.rem(2 * lane, v.shape[1])
    return jnp.concatenate([pick(v, even), pick(v, even + 1)], axis=1)


def joining(shape):
    lane = iota2(shape, 1)
    return lax.rem(lane, 2) == 0, lax.div(lane, 2)


def joined(v, even, at):
    half = v.shape[1] // 2
    return jnp.where(even, pick(v[:, :half], at), pick(v[:, half:], at))


def loop(low, high, body, init=None, unroll=1):
    def step(i, carry):
        if init is None:
            body(i)
            return carry
        return body(i, carry)

    carry = 0 if init is None else init
    whole = (high - low) // unroll
    if whole > 1:

        def several(k, carry):
            for j in range(unroll):
                carry = step(low + k * unroll + j, carry)
            return carry

        carry = lax.fori_loop(0, whole, several, carry)
        low += whole * unroll
    for i in range(low, high):
        carry = step(i, carry)
    return carry


def unrolling(ref):
    return UNROLL.get(ref.shape[1] * ref.shape[2] // 1024, 4)


UNROLL = {20: 4, 18: 4, 6: 8, 5: 8, 4: 8}


def coefficients(c, kx, ky, kz, rd, low, high, scale):
    half = 0.5 * scale

    def faces(x):
        cx = c[x]
        fx = half * (cx + c[x + 1])
        fy = half * (cx + roll_up(cx, 0))
        fz = half * (cx + next_z(cx))
        kx[x] = fx
        ky[x] = fy
        kz[x] = fz
        return cx, fx, fy, fz

    _, first, _, _ = faces(low - 1)

    def body(x, before):
        cx, fx, fy, fz = faces(x)
        diagonal = fx + before + fy + roll_down(fy, 0) + fz + previous_z(fz)
        inside = cx > 0.0
        rd[x] = jnp.where(inside, relax_weight / jnp.where(inside, diagonal, 1.0), 0.0)
        return fx

    loop(low, high, body, first, unrolling(rd))


def operate(v, kx, ky, kz, low, high, use):
    def body(x, before):
        vx = v[x]
        fx = kx[x] * (vx - v[x + 1])
        fy = ky[x] * (vx - roll_up(vx, 0))
        fz = kz[x] * (vx - next_z(vx))
        use(x, vx, (fx - before) + (fy - roll_down(fy, 0)) + (fz - previous_z(fz)))
        return fx

    loop(low, high, body, kx[low - 1] * (v[low - 1] - v[low]), unrolling(v))


def sweep(v, out, g, kx, ky, kz, rd, low, high):
    def use(x, vx, av):
        out[x] = vx + rd[x] * (g[x] - av)

    operate(v, kx, ky, kz, low, high, use)


def iota2(shape, dim):
    return lax.broadcasted_iota(jnp.int32, shape, dim)


def conductivity(p):
    return floor_conduct + (1.0 - floor_conduct) * (p * p * p)


def send_kernel(nx, ny, phase, mask, dev, *refs):
    count = nx + ny + nx * ny
    outs = refs[:count]
    px, mx, dx, py, my, dy, sems = refs[count:]
    ox, oy, _ = phase.shape
    ups = [upward(lax.axis_index("boxes"), e) for e in range(nx)]
    rows = [pl.multiple_of(jnp.where(upward(lax.axis_index("sub"), f), oy - YH, 0), 8) for f in range(ny)]
    copies = []
    for f in range(ny):
        for source, out in ((phase, py), (mask, my), (dev, dy)):
            copies.append((source.at[:, pl.ds(rows[f], YH), :], out.at[f]))
    for e in range(nx):
        for source, out, width in ((phase, px, XH), (mask, mx, GX), (dev, dx, GX)):
            copies.append((source.at[pl.ds(jnp.where(ups[e], ox - width, 0), width)], out.at[e]))
    copies = [pltpu.make_async_copy(a, b, sems.at[i]) for i, (a, b) in enumerate(copies)]
    for copy in copies:
        copy.start()
    for copy in copies[:3 * ny]:
        copy.wait()
    for f in range(ny):
        face = outs[nx + f]

        def body(x, face=face, f=f):
            face[0, x] = conductivity(py[f, x])
            face[1, x] = my[f, x].astype(F32) * dy[f, x]

        loop(0, ox, body, unroll=8)
        for e in range(nx):
            corner = outs[nx + ny + e * ny + f]
            corner[0:DC] = face[0, pl.ds(jnp.where(ups[e], ox - DC, 0), DC)]
            corner[DC:DC + DG] = face[1, pl.ds(jnp.where(ups[e], ox - DG, 0), DG)]
    for copy in copies[3 * ny:]:
        copy.wait()
    for e in range(nx):
        for x in range(XH):
            outs[e][x] = conductivity(px[e, x])
        for x in range(GX):
            outs[e][XH + x] = mx[e, x].astype(F32) * dx[e, x]


def pack(planes, turns, lane):
    total = None
    for b, (plane, turn) in enumerate(zip(planes, turns)):
        moved = pltpu.roll(plane, turn, 1)
        total = moved if total is None else jnp.where(lane >= ZW * b, moved, total)
    return total


def strip_turns(oz, start):
    return [lax.rem(ZW * b + oz - start, oz) for b in range(oz // ZW)]


def split(x):
    high = x.astype(BF16)
    rest = x - high.astype(F32)
    middle = rest.astype(BF16)
    low = (rest - middle.astype(F32)).astype(BF16)
    return jnp.concatenate([high, middle, low], axis=-1)


def times(x, matrix):
    return jnp.dot(split(x), matrix, preferred_element_type=F32)


def thrice(matrix):
    return jnp.concatenate([matrix.astype(BF16)] * 3, axis=0)


def compact(planes, out):
    rows, lanes = planes[0].shape
    lane = iota2((rows, lanes), 1)
    for q in range(len(planes) // 4):
        total = planes[4 * q]
        for i in range(1, 4):
            moved = pltpu.roll(planes[4 * q + i], lanes // 4 * i, 1)
            total = jnp.where(lane < lanes // 4 * i, total, moved)
        out[q * rows:(q + 1) * rows, :] = total


def own_kernel(phase, mask, dev, c_out, g_out, strip, c2, c, g, sums, work):
    ox, oy, oz = phase.shape
    pz = lax.axis_index("pair")

    def body(x):
        c[x], g[x] = conductivity(phase[x]), mask[x].astype(F32) * dev[x]
        c_out[x] = parted(c[x])
        g_out[x] = parted(g[x])

    loop(0, ox, body, unroll=4)
    i, j = iota2((oz, oz), 0), iota2((oz, oz), 1)
    matrix = thrice(jnp.where(j == lax.div(i, 4), 1.0 / 64.0, 0.0))
    for x in range(ox // 4):
        sums[...] = (c[4 * x] + c[4 * x + 1]) + (c[4 * x + 2] + c[4 * x + 3])
        part = [sums[pl.ds(k, oy // 4, stride=4), :] for k in range(4)]
        work[x] = (part[0] + part[1]) + (part[2] + part[3])
    done = times(work[...].reshape(-1, oz), matrix)
    compact([done[x * oy // 4:(x + 1) * oy // 4] for x in range(ox // 4)], c2)
    group = oz // ZW
    turns = strip_turns(oz, jnp.where(pz == 0, oz - ZW, 0))
    lane = iota2((oy, oz), 1)
    for which, source in enumerate((c, g)):
        for a in range(ox // group):
            strip[which, a] = pack([source[group * a + b] for b in range(group)], turns, lane)


def halo_rows(ny, f, oy, up):
    if ny == 1:
        return oy
    return jnp.where(up, oy, oy + YH)


def place_halos(nx, ny, box, got, put, between=lambda: None):
    ox, oy, oz = box
    bx = lax.axis_index("boxes")
    sy = lax.axis_index("sub")
    place = 0
    row = iota2((YH, oz), 0)

    def trim(values, up):
        if ny > 1:
            return values
        return jnp.where(lax.div(row, 2) == jnp.where(up, YH // 2 - 1, 0), 0.0, values)

    def below(up, planes):
        return jnp.where(up, XH + ox, XH - planes)

    for e in range(nx):
        up = upward(bx, e)
        face = got[place]
        place += 1
        for x in range(XH):
            put(0, below(up, XH) + x, slice(0, oy), face[x])
        for x in range(GX):
            put(1, below(up, GX) + x, slice(0, oy), face[XH + x])
    between()
    for f in range(ny):
        up = upward(sy, f)
        face = got[place]
        place += 1
        rows = pl.ds(pl.multiple_of(halo_rows(ny, f, oy, up), 8), YH)

        def copy(x, face=face, rows=rows, up=up):
            put(0, XH + x, rows, trim(face[0, x], up))
            put(1, XH + x, rows, trim(face[1, x], up))

        loop(0, ox, copy, unroll=8)
    for e in range(nx):
        ux = upward(bx, e)
        for f in range(ny):
            up = upward(sy, f)
            face = got[place]
            place += 1
            rows = pl.ds(pl.multiple_of(halo_rows(ny, f, oy, up), 8), YH)
            for x in range(DC):
                put(0, below(ux, DC) + x, rows, trim(face[x], up))
            for x in range(DG):
                put(1, below(ux, DG) + x, rows, trim(face[DC + x], up))


def strip_kernel(nx, ny, own, *refs):
    count = nx + ny + nx * ny
    got, (strip, c, g) = refs[:count], refs[count:]
    planes, nrows, oz = c.shape
    oy = own.shape[2]
    ox = planes - 2 * XH
    pz = lax.axis_index("pair")
    for out in (c, g):
        for low, high in ((0, XH), (XH + ox, planes)):
            out[low:high, oy:, :] = jnp.zeros((high - low, nrows - oy, oz), F32)
    for low, high in ((0, XH - GX), (XH + ox + GX, planes)):
        g[low:high, 0:oy, :] = jnp.zeros((high - low, oy, oz), F32)

    def put(which, plane, rows, values):
        (c, g)[which][plane, rows, :] = values

    place_halos(nx, ny, (ox, oy, oz), got, put)
    group = oz // ZW
    turns = strip_turns(oz, jnp.where(pz == 0, oz - ZW, 0))
    packed = planes // group
    side = XH // group
    for which, source in enumerate((c, g)):
        for a in range(packed):
            at = which * packed + a
            if side <= a < packed - side:
                strip[at, 0:oy, :] = own[which, a - side]
                rows = slice(oy, nrows)
            else:
                rows = slice(0, nrows)
            lane = iota2((nrows - (rows.start or 0), oz), 1)
            strip[at, rows, :] = pack([source[group * a + b, rows, :] for b in range(group)], turns, lane)


def join_kernel(nx, ny, *refs):
    count = nx + ny + nx * ny
    got, outs, (cx, gx, cy, gy, sems) = refs[:count], refs[count:count + 4], refs[count + 4:]
    copies = [pltpu.make_async_copy(a, b, sems.at[i]) for i, (a, b) in enumerate(zip((cx, gx, cy, gy), outs))]
    planes, nrows, lanes = cy.shape
    ox, oy = planes - 2 * XH, cx.shape[1]
    for low, high in ((0, XH), (XH + ox, planes)):
        for out in (cy, gy):
            out[low:high] = jnp.zeros((high - low, nrows, lanes), F32)
    for low, high in ((0, XH - GX), (XH + GX, 2 * XH)):
        gx[low:high] = jnp.zeros((high - low, oy, lanes), F32)

    def put(which, plane, rows, values):
        if isinstance(rows, slice):
            (cx, gx)[which][jnp.where(plane < XH, plane, plane - ox)] = parted(values)
        else:
            (cy, gy)[which][plane, pl.ds(pl.multiple_of(rows.start - oy, 8), rows.size), :] = parted(values)

    def begin():
        copies[0].start()
        copies[1].start()

    place_halos(nx, ny, (ox, oy, lanes // 2), got, put, begin)
    copies[2].start()
    copies[3].start()
    for copy in copies:
        copy.wait()


def halve(total, work):
    work[...] = total
    return work[pl.ds(0, total.shape[0] // 2, stride=2), :] + work[pl.ds(1, total.shape[0] // 2, stride=2), :]


def pool_wide(source, low, high, out, work):
    step, _, width = work.shape

    def body(k):
        for j in range(step):
            total = source[2 * (low + step * k + j)] + source[2 * (low + step * k + j) + 1]
            out[step * k + j] = 0.125 * halve(total[:, :width] + total[:, width:], work.at[j])

    loop(0, (high - low) // step, body)


def pool(source, low, high, out, matrix, work):
    sums = [halve(source(2 * j) + source(2 * j + 1), work.at[j - low]) for j in range(low, high)]
    out[...] = times(jnp.concatenate(sums, axis=0), matrix).reshape(out.shape)


def pool_matrix(size_in, size_out, limit, shift, weight):
    i, j = iota2((size_in, size_out), 0), iota2((size_in, size_out), 1)
    return thrice(jnp.where((i < limit) & (j == shift + lax.div(i, 2)), weight, 0.0))


KEPT, FINE = 10, 3
SKIP = XH - 3
YN = 8


def near_rows(ny, oy):
    if ny > 1:
        return oy, oy + 2 * YH - YN
    return (pl.multiple_of(jnp.where(upward(lax.axis_index("sub"), 0), oy, oy + YH - YN), 8),)


def inner(ny, ref, out):
    planes = pl.ds(SKIP, out.shape[0])
    oy = out.shape[1] - ny * YN
    parts = [(ref.at[planes, pl.ds(0, oy), :], out.at[:, pl.ds(0, oy), :])]
    for f, start in enumerate(near_rows(ny, oy)):
        parts.append((ref.at[planes, pl.ds(start, YN), :], out.at[:, pl.ds(oy + f * YN, YN), :]))
    return parts


def down_kernel(nx, ny, c_own, g_own, cx, gx, cy, gy, strip, c2, *refs):
    kept, f2 = refs[:KEPT], refs[KEPT]
    faces = refs[KEPT + 1:KEPT + 1 + nx]
    held_here = refs[KEPT + 1 + nx:2 * KEPT + 1 + nx]
    c, g, u0, kx1, ky1, kz1, rd1, c1, f1, u1 = held_here
    kx, ky, kz, rd, first, v1, work, work1, low2, sems, arrivals = refs[2 * KEPT + 1 + nx:]
    pairs = []
    for a, k in zip(held_here[:FINE], kept):
        pairs += inner(ny, a, k)
    pairs += list(zip(held_here[FINE:], kept[FINE:]))
    copies = [pltpu.make_async_copy(a, k, sems.at[i]) for i, (a, k) in enumerate(pairs)]
    planes, rows, lanes = c.shape
    oz = lanes // 2
    oy = cx.shape[1]
    pz = lax.axis_index("pair")
    bx = lax.axis_index("boxes")
    group = oz // ZW
    wide = ZW // 2
    packed = planes // group
    lane = iota2((rows, oz), 1)
    start = jnp.where(pz == 0, oz // 2, oz - wide)
    own = lane < oz // 2
    near = (lane >= start) & (lane < start + wide)
    order = lax.rem(lane, oz // 2)
    order = ZW * lax.div(order, wide) + 2 * lax.rem(order, wide) + lax.div(lane, oz // 2)

    last = packed - 1

    def arriving(a, beside, which):
        out, own_planes, x_planes, y_rows = ((c, c_own, cx, cy), (g, g_own, gx, gy))[which]
        here = pl.ds(a * group, group)
        source = own_planes.at[pl.ds(0, group)]
        if beside:
            source = x_planes.at[pl.ds(a // last * group, group)]
        elif beside is False:
            source = own_planes.at[pl.ds((a - 1) * group, group)]
        return (
            pltpu.make_async_copy(source, out.at[here, pl.ds(0, oy), :], arrivals.at[4 * a + 2 * which]),
            pltpu.make_async_copy(
                y_rows.at[here], out.at[here, pl.ds(oy, rows - oy), :], arrivals.at[4 * a + 2 * which + 1]
            ),
        )

    for a in range(packed):
        for which in range(2):
            for copy in arriving(a, a in (0, last), which):
                copy.start()

    def unpack(a):
        for which, (strips, out) in enumerate(((strip[a], c), (strip[packed + a], g))):
            for copy in arriving(a, None, which):
                copy.wait()
            strips = pick(strips, order)
            for b in range(group):
                x = group * a + b
                for h in range(2):
                    cols = slice(h * oz, h * oz + oz)
                    turn = lax.rem(start + (3 - h) * (oz // 2) + oz // 2 - wide * b, oz)
                    far = jnp.where(near, pltpu.roll(strips, turn, 1), 0.0)
                    out[x, :, cols] = jnp.where(own, out[x, :, cols], far)

    loop(0, packed, unpack)
    parts = 1 + ny
    for copy in copies[:2 * parts]:
        copy.start()
    edge = XH - GX
    coefficients(c, kx, ky, kz, rd, edge, planes - edge, 1.0)

    def start_sweep(x):
        first[x] = g[x] * rd[x]

    loop(edge, planes - edge, start_sweep)
    sweep(first, u0, g, kx, ky, kz, rd, edge + 1, planes - edge - 1)
    for copy in copies[2 * parts:3 * parts]:
        copy.start()
    rest = first

    def use(x, vx, av):
        rest[x] = g[x] - av

    operate(u0, kx, ky, kz, edge + 2, planes - edge - 2, use)
    planes1 = planes // 2
    pool_wide(c, 0, planes1, c1, work)
    f1[...] = jnp.zeros_like(f1)
    low1 = (edge + 2) // 2
    high1 = planes1 - low1
    pool_wide(rest, low1, high1, f1.at[low1:high1], work)
    coefficients(c1, kx1, ky1, kz1, rd1, 1, planes1 - 1, 0.25)

    def start_sweep1(x):
        v1[x] = f1[x] * rd1[x]

    loop(low1, high1, start_sweep1)
    u1[...] = jnp.zeros_like(u1)
    sweep(v1, u1, f1, kx1, ky1, kz1, rd1, low1 + 1, high1 - 1)
    for copy in copies[3 * parts:]:
        copy.start()
    h1 = XH // 2
    o1 = planes1 - XH

    def use1(x, vx, av):
        v1[x] = f1[x] - av

    operate(u1, kx1, ky1, kz1, h1, planes1 - h1, use1)
    half = oz // 2
    matrix1 = pool_matrix(oz, oz, half, 0, 0.125)
    own1 = 2 * low2.shape[1]
    pool(lambda x: v1[x, 0:own1, :], h1 // 2, (planes1 - h1) // 2, low2, matrix1, work1)
    tile = c2.shape[0]
    compact([low2[x] for x in range(low2.shape[0])], f2.at[0:tile])
    f2[tile:] = c2[...]
    for e in range(nx):
        up = upward(bx, e)
        faces[e][0:h1] = u1[pl.ds(jnp.where(up, o1, h1), h1)]
        faces[e][h1:2 * h1 - 1] = f1[pl.ds(jnp.where(up, o1 + 1, h1), h1 - 1)]
    for copy in copies:
        copy.wait()


def bottom_kernel(nx, ny, nfar, c_in, g_in, u_in, *refs):
    pieces = 1 + nx + nfar
    got = refs[:pieces]
    add, c, g, u0, kx, ky, kz, rd = refs[pieces:pieces + 8]
    c2, f2, kx2, ky2, kz2, rd2, v2, w2, tall, sems = refs[pieces + 8:]
    copies = [
        pltpu.make_async_copy(a, b, sems.at[i]) for i, (a, b) in enumerate(((c_in, c), (g_in, g), (u_in, u0)))
    ]
    for copy in copies:
        copy.start()
    planes, rows, lanes = u0.shape
    planes2, rows2, oz = c2.shape
    oy = rows - ny * YN
    o2x, o2y = (planes2 - 2 * L2X), oy // 4
    bx = lax.axis_index("boxes")
    sy = lax.axis_index("sub")
    pz = lax.axis_index("pair")

    lane = iota2((o2y, oz), 1)
    row = iota2((o2y, oz), 0)
    quarter = oz // 4
    nsub = lax.axis_size("sub")
    places = [(L2X, got[0], range(o2x), None)]
    for e in range(nx):
        places.append((jnp.where(upward(bx, e), L2X + o2x, L2X - o2x), got[1 + e], range(o2x), None))
    for e in range(nfar):
        far = upward(bx, e, 2)
        places.append((jnp.where(far, L2X + 2 * o2x, 0), got[1 + nx + e], range(L2X - o2x), far))
    for f in range(ny + 1):
        y0, side, keep = 0, sy, lane < 2 * quarter
        if f > 0:
            up = upward(sy, f - 1)
            y0 = pl.multiple_of(jnp.where(up, o2y, rows2 - o2y), 8)
            side = jnp.where(up, sy + 1, sy - 1)
            keep = keep & (side >= 0) & (side < nsub)
            if ny == 1:
                keep = keep & (row != jnp.where(up, o2y - 1, 0))
        side = 2 * jnp.clip(side, 0, nsub - 1)
        for x0, message, count, far in places:
            for j in count:
                for which, out in enumerate((f2, c2)):
                    if far is None:
                        tiles = [message[side + p, which, j // 4] for p in range(2)]
                        turns = [(quarter * (p - j)) % oz for p in range(2)]
                    else:
                        tiles = [message[side + p, which] for p in range(2)]
                        at = jnp.where(far, j, o2x - (L2X - o2x) + j)
                        turns = [lax.rem(quarter * (p + o2x - at), oz) for p in range(2)]
                    low, high = (pltpu.roll(tile, turn, 1) for tile, turn in zip(tiles, turns))
                    out[x0 + j, pl.ds(y0, o2y), :] = jnp.where(keep, jnp.where(lane < quarter, low, high), 0.0)
    coefficients(c2, kx2, ky2, kz2, rd2, 1, planes2 - 1, 0.0625)

    def start_sweep2(x):
        v2[x] = f2[x] * rd2[x]

    loop(1, planes2 - 1, start_sweep2)
    old, new = v2, w2
    for k in range(2, BOTTOM_SWEEPS + 1):
        sweep(old, new, f2, kx2, ky2, kz2, rd2, k, planes2 - k)
        old, new = new, old

    i, j = iota2((oz, oz), 0), iota2((oz, oz), 1)
    spread_z = thrice(jnp.where(i == lax.div(lax.rem(pz * (oz // 2) + j, oz), 2), 1.0, 0.0))
    count, rows1, _ = add.shape
    base = (planes2 - count) // 2
    moved = times(old[base:base + count].reshape(count * rows2, oz), spread_z)
    row = iota2((8, oz), 0)
    for x in range(count):
        t = moved[x * rows2:x * rows2 + rows2]
        if ny == 1:
            halo = jnp.where(upward(sy, 0), t[o2y:o2y + 8], pltpu.roll(t[rows2 - 8:], 4, 0))
        else:
            halo = jnp.where(row < 4, t[o2y:o2y + 8], t[rows2 - 8:])
        t = jnp.concatenate([t[0:o2y], halo], axis=0)
        tall[x, pl.ds(0, o2y + 8, stride=2), :] = t
        tall[x, pl.ds(1, o2y + 8, stride=2), :] = t
        add[x] = tall[x, 0:rows1, :]

    copies[0].wait()
    row = iota2((YN, lanes), 0)

    def close(x):
        c[x, oy:, :] = jnp.where(row == jnp.where(upward(sy, 0), YN - 1, 0), 0.0, c[x, oy:, :])

    if ny == 1:
        loop(0, planes, close, unroll=2)
    coefficients(c, kx, ky, kz, rd, 1, planes - 1, 1.0)
    for copy in copies[1:]:
        copy.wait()


def up_kernel(nx, ny, add, c, g, u0, kx, ky, kz, rd, *refs):
    faces, (kx1, ky1, kz1, rd1, c1, f1, u1) = refs[:nx], refs[nx:nx + 7]
    field, residual = refs[nx + 7:nx + 9]
    ua, ub, v1, w1, x1, wide = refs[nx + 9:]
    planes, rows, lanes = u0.shape
    planes1, rows1, oz = u1.shape
    oy = field.shape[1]
    bx = lax.axis_index("boxes")

    h1 = XH // 2
    for x in range(planes1):
        v1[x] = jnp.where(c1[x] > 0.0, u1[x] + add[x // 2], 0.0)
        w1[x] = f1[x]
    for e in range(nx):
        up = upward(bx, e)
        for x in range(h1):
            at = jnp.where(up, planes1 - h1, 0) + x
            v1[at] = jnp.where(c1[at] > 0.0, faces[e][x] + add[lax.div(at, 2)], 0.0)
        for x in range(h1 - 1):
            w1[jnp.where(up, planes1 - h1, 1) + x] = faces[e][h1 + x]
    sweep(v1, x1, w1, kx1, ky1, kz1, rd1, 1, planes1 - 1)
    sweep(x1, v1, w1, kx1, ky1, kz1, rd1, 2, planes1 - 2)

    step = wide.shape[0]
    low = (SKIP + 1) // 2

    def spread0(x, m, fine):
        wide[m, pl.ds(0, rows1, stride=2), :] = v1[x]
        wide[m, pl.ds(1, rows1, stride=2), :] = v1[x]
        moved = [wide[m, 0:oy]] + [wide[m, pl.ds(start, YN)] for start in near_rows(ny, oy)]
        moved = jnp.concatenate(moved, axis=0)
        moved = jnp.concatenate([moved, moved], axis=1)
        for y in fine:
            ua[y] = jnp.where(c[y] > 0.0, u0[y] + moved, 0.0)

    def several(n):
        for m in range(step):
            x = low + step * n + m
            spread0(x, m, (2 * x - SKIP, 2 * x + 1 - SKIP))

    loop(0, (planes1 - 2 * low) // step, several)
    spread0(low - 1, 0, (0,))
    spread0(planes1 - low, 1, (planes - 1,))
    sweep(ua, ub, g, kx, ky, kz, rd, 1, planes - 1)
    sweep(ub, ua, g, kx, ky, kz, rd, 2, planes - 2)
    order = joining((oy, oz))

    def use(x, vx, av):
        field[x - 3] = joined(vx[0:oy], *order)
        residual[x - 3] = joined(g[x, 0:oy, :] - av[0:oy], *order)

    operate(ua, kx, ky, kz, 3, planes - 3, use)


def call(kernel, outs, scratch=(), mib=16, raw_in=0, raw_out=0, copies=0, more=0):
    where = [pl.BlockSpec(memory_space=pltpu.HBM)], [pl.BlockSpec(memory_space=pltpu.VMEM)]
    outs = tuple(pltpu.HBM(o.shape, o.dtype) if i < raw_out else o for i, o in enumerate(outs))
    extra = tuple(pltpu.SemaphoreType.DMA((n,)) for n in (copies, more) if n)

    def run(*operands):
        operands = [pltpu.with_memory_space_constraint(x, pltpu.HBM) if i < raw_in else x for i, x in enumerate(operands)]
        return pl.pallas_call(
            kernel,
            in_specs=where[0] * raw_in + where[1] * (len(operands) - raw_in),
            out_specs=tuple(where[0] * raw_out + where[1] * (len(outs) - raw_out)),
            out_shape=outs,
            scratch_shapes=tuple(s if hasattr(s, "memory_space") else pltpu.VMEM(s, F32) for s in scratch) + extra,
            compiler_params=params(mib),
        )(*operands)

    return run


def per_device(phase, target_mask, deviation):
    ox, oy, oz = phase.shape
    nbox, nsub = lax.axis_size("boxes"), lax.axis_size("sub")
    swap_x, swap_y, far_x = exchanges(nbox), exchanges(nsub), exchanges(nbox, 2)
    nx, ny, nfar = len(swap_x), len(swap_y), len(far_x)
    pair_swap = [(0, 1), (1, 0)]

    def both(px, py):
        return [(a * nsub + c, b * nsub + d) for a, b in px for c, d in py]

    def traded(faces):
        out = []
        for e in range(nx):
            out.append(lax.ppermute(faces[e], "boxes", swap_x[e]))
        for f in range(ny):
            out.append(lax.ppermute(faces[nx + f], "sub", swap_y[f]))
        for e in range(nx):
            for f in range(ny):
                out.append(lax.ppermute(faces[nx + ny + e * ny + f], ("boxes", "sub"), both(swap_x[e], swap_y[f])))
        return out

    planes, rows = ox + 2 * XH, oy + YH * ny
    planes1, rows1 = planes // 2, rows // 2
    o2x, o2y = ox // 4, oy // 4
    planes2 = o2x + 2 * L2X
    rows2 = o2y * (ny + 1)

    box = spec((ox, oy, oz))
    faces = [spec((XH + GX, oy, oz))] * nx + [spec((2, ox, YH, oz))] * ny + [spec((DC + DG, YH, oz))] * (nx * ny)
    width, edge = (nx, GX, oy, oz), (ny, ox, YH, oz)
    faces = call(
        lambda *r: send_kernel(nx, ny, *r),
        faces,
        [(nx, XH, oy, oz), pltpu.VMEM(width, jnp.int32), width, edge, pltpu.VMEM(edge, jnp.int32), edge],
        raw_in=3,
        copies=3 * (nx + ny),
    )(phase, target_mask, deviation)
    got = traded(faces)
    phase, target_mask, deviation, _ = lax.optimization_barrier((phase, target_mask, deviation, faces))
    group = oz // ZW
    padded = (planes, rows, oz)
    fine = (planes, rows, 2 * oz)
    parted_box = in_hbm((ox, oy, 2 * oz))
    c, g, own, c2 = call(
        own_kernel,
        [parted_box, parted_box, spec((2, ox // group, oy, oz)), spec((o2x // 4 * o2y, oz))],
        [(ox, oy, oz), (ox, oy, oz), (oy, oz), (o2x, o2y, oz)],
    )(phase, target_mask, deviation)
    (strip,) = call(
        lambda *r: strip_kernel(nx, ny, *r), [spec((2 * planes // group, rows, oz))], [padded, padded]
    )(own, *got)
    strip = lax.ppermute(strip, "pair", pair_swap)
    halos = [(2 * XH, oy, 2 * oz)] * 2 + [(planes, rows - oy, 2 * oz)] * 2
    halos = call(lambda *r: join_kernel(nx, ny, *r), [spec(h) for h in halos], halos, raw_out=4, copies=4)(*got)
    middle = (planes1, rows1, oz)
    small = (planes - 2 * SKIP, oy + ny * YN, 2 * oz)
    down = call(
        lambda *r: down_kernel(nx, ny, *r),
        [spec(small)] * FINE + [spec(middle)] * (KEPT - FINE) + [spec((o2x // 2 * o2y, oz))]
        + [spec((XH - 1, rows1, oz))] * nx,
        [fine] * FINE + [middle] * (KEPT - FINE) + [fine] * 5 + [middle, (4, rows, oz), (o2x, oy // 2, oz), (o2x, o2y, oz)],
        mib=48,
        raw_in=6,
        raw_out=KEPT,
        copies=KEPT + FINE * ny,
        more=4 * planes // group,
    )(c, g, *halos, strip, c2)
    kept, f2, sides = down[:KEPT], down[KEPT], down[KEPT + 1:]
    sheet = lax.all_gather(f2, ("sub", "pair")).reshape(-1, 2, o2x // 4, o2y, oz)
    got = [sheet] + [lax.ppermute(sheet, "boxes", p) for p in swap_x]
    for e, p in enumerate(far_x):
        at = jnp.where(upward(lax.axis_index("boxes"), e, 2), o2x // 4 - 1, 0)
        got.append(lax.ppermute(lax.dynamic_index_in_dim(sheet, at, 2, keepdims=False), "boxes", p))
    got, sides = lax.optimization_barrier((got, sides))
    sides = [lax.ppermute(side, "boxes", p) for side, p in zip(sides, swap_x)]
    lowest = (planes2, rows2, oz)
    add, *fine_up = call(
        lambda *r: bottom_kernel(nx, ny, nfar, *r),
        [in_vmem((planes1 // 2, rows1, oz))] + [in_vmem(small)] * 7,
        [lowest] * 8 + [(planes1 // 2, 2 * (o2y + 8), oz)],
        mib=12,
        raw_in=FINE,
        copies=FINE,
    )(*kept[:FINE], *got)
    return tuple(call(
        lambda *r: up_kernel(nx, ny, *r),
        [box, box],
        [small, small, middle, middle, middle, (3, rows, oz)],
        mib=14,
    )(held(add), *[held(x) for x in fine_up], *sides, *kept[FINE:]))


def solution(mesh):
    where = P(("groups", "boxes"), "sub", "pair")
    return jax.shard_map(
        per_device,
        mesh=mesh,
        in_specs=(where, where, where),
        out_specs=(where, where),
        check_vma=False,
    )
```

```python
import jax
import jax.numpy as jnp
from jax import lax
from jax.experimental import pallas as pl
from jax.experimental.pallas import tpu as pltpu
from jax.sharding import PartitionSpec as P

SWEEPS = 2
BOTTOM_SWEEPS = 8

floor_conduct = 0.1
relax_weight = 0.8

XH = 8
YH = 16
GX = 6
DC, DG = 6, 5
ZW = 16
L2X = 10
F32 = jnp.float32
BF16 = jnp.bfloat16
MIB = 1 << 20


def exchanges(count, step=1):
    swaps = []
    for e in range(2):
        pairs = []
        for i in range(count):
            if (i // step + e) % 2 == 0 and i + step < count:
                pairs += [(i, i + step), (i + step, i)]
        if pairs:
            swaps.append(pairs)
    return swaps


def upward(index, e, step=1):
    return (index // step + e) % 2 == 0


def spec(shape):
    return jax.ShapeDtypeStruct(shape, F32)


def in_vmem(shape):
    return pltpu.VMEM(shape, F32)


def in_hbm(shape):
    return pltpu.HBM(shape, F32)


def held(x):
    return pltpu.with_memory_space_constraint(x, pltpu.VMEM)


def params(mib):
    return pltpu.CompilerParams(vmem_limit_bytes=mib * MIB)


def roll_up(v, axis):
    return pltpu.roll(v, v.shape[axis] - 1, axis)


def roll_down(v, axis):
    return pltpu.roll(v, 1, axis)


def next_z(v):
    half = v.shape[1] // 2
    if half < 128:
        return roll_up(v, 1)
    return jnp.concatenate([v[:, half:], roll_up(v[:, :half], 1)], axis=1)


def previous_z(v):
    half = v.shape[1] // 2
    if half < 128:
        return roll_down(v, 1)
    return jnp.concatenate([roll_down(v[:, half:], 1), v[:, :half]], axis=1)


def pick(v, lanes):
    return jnp.take_along_axis(v, lanes, axis=1)


def parted(v):
    lane = iota2(v.shape, 1)
    even = lax.rem(2 * lane, v.shape[1])
    return jnp.concatenate([pick(v, even), pick(v, even + 1)], axis=1)


def joining(shape):
    lane = iota2(shape, 1)
    return lax.rem(lane, 2) == 0, lax.div(lane, 2)


def joined(v, even, at):
    half = v.shape[1] // 2
    return jnp.where(even, pick(v[:, :half], at), pick(v[:, half:], at))


def loop(low, high, body, init=None, unroll=1):
    def step(i, carry):
        if init is None:
            body(i)
            return carry
        return body(i, carry)

    carry = 0 if init is None else init
    whole = (high - low) // unroll
    if whole > 1:

        def several(k, carry):
            for j in range(unroll):
                carry = step(low + k * unroll + j, carry)
            return carry

        carry = lax.fori_loop(0, whole, several, carry)
        low += whole * unroll
    for i in range(low, high):
        carry = step(i, carry)
    return carry


def unrolling(ref):
    return UNROLL.get(ref.shape[1] * ref.shape[2] // 1024, 4)


UNROLL = {20: 4, 18: 4, 6: 8, 5: 8, 4: 8}


def coefficients(c, kx, ky, kz, rd, low, high, scale, also=lambda x, factor: None):
    half = 0.5 * scale

    def faces(x):
        cx = c[x]
        fx = half * (cx + c[x + 1])
        fy = half * (cx + roll_up(cx, 0))
        fz = half * (cx + next_z(cx))
        kx[x] = fx
        ky[x] = fy
        kz[x] = fz
        return cx, fx, fy, fz

    _, first, _, _ = faces(low - 1)

    def body(x, before):
        cx, fx, fy, fz = faces(x)
        diagonal = fx + before + fy + roll_down(fy, 0) + fz + previous_z(fz)
        inside = cx > 0.0
        factor = jnp.where(inside, relax_weight / jnp.where(inside, diagonal, 1.0), 0.0)
        rd[x] = factor
        also(x, factor)
        return fx

    loop(low, high, body, first, unrolling(rd))


def operate(v, kx, ky, kz, low, high, use):
    def body(x, before):
        vx = v[x]
        fx = kx[x] * (vx - v[x + 1])
        fy = ky[x] * (vx - roll_up(vx, 0))
        fz = kz[x] * (vx - next_z(vx))
        use(x, vx, (fx - before) + (fy - roll_down(fy, 0)) + (fz - previous_z(fz)))
        return fx

    loop(low, high, body, kx[low - 1] * (v[low - 1] - v[low]), unrolling(v))


def sweep(v, out, g, kx, ky, kz, rd, low, high):
    def use(x, vx, av):
        out[x] = vx + rd[x] * (g[x] - av)

    operate(v, kx, ky, kz, low, high, use)


def iota2(shape, dim):
    return lax.broadcasted_iota(jnp.int32, shape, dim)


def conductivity(p):
    return floor_conduct + (1.0 - floor_conduct) * (p * p * p)


def send_kernel(nx, ny, phase, mask, dev, *refs):
    count = nx + ny + nx * ny
    outs = refs[:count]
    px, mx, dx, py, my, dy, sems = refs[count:]
    ox, oy, _ = phase.shape
    ups = [upward(lax.axis_index("boxes"), e) for e in range(nx)]
    rows = [pl.multiple_of(jnp.where(upward(lax.axis_index("sub"), f), oy - YH, 0), 8) for f in range(ny)]
    copies = []
    for f in range(ny):
        for source, out in ((phase, py), (mask, my), (dev, dy)):
            copies.append((source.at[:, pl.ds(rows[f], YH), :], out.at[f]))
    for e in range(nx):
        for source, out, width in ((phase, px, XH), (mask, mx, GX), (dev, dx, GX)):
            copies.append((source.at[pl.ds(jnp.where(ups[e], ox - width, 0), width)], out.at[e]))
    copies = [pltpu.make_async_copy(a, b, sems.at[i]) for i, (a, b) in enumerate(copies)]
    for copy in copies:
        copy.start()
    for copy in copies[:3 * ny]:
        copy.wait()
    for f in range(ny):
        face = outs[nx + f]

        def body(x, face=face, f=f):
            face[0, x] = conductivity(py[f, x])
            face[1, x] = my[f, x].astype(F32) * dy[f, x]

        loop(0, ox, body, unroll=8)
        for e in range(nx):
            corner = outs[nx + ny + e * ny + f]
            corner[0:DC] = face[0, pl.ds(jnp.where(ups[e], ox - DC, 0), DC)]
            corner[DC:DC + DG] = face[1, pl.ds(jnp.where(ups[e], ox - DG, 0), DG)]
    for copy in copies[3 * ny:]:
        copy.wait()
    for e in range(nx):
        for x in range(XH):
            outs[e][x] = conductivity(px[e, x])
        for x in range(GX):
            outs[e][XH + x] = mx[e, x].astype(F32) * dx[e, x]


def pack(planes, turns, lane):
    total = None
    for b, (plane, turn) in enumerate(zip(planes, turns)):
        moved = pltpu.roll(plane, turn, 1)
        total = moved if total is None else jnp.where(lane >= ZW * b, moved, total)
    return total


def strip_turns(oz, start):
    return [lax.rem(ZW * b + oz - start, oz) for b in range(oz // ZW)]


def split(x):
    high = x.astype(BF16)
    rest = x - high.astype(F32)
    middle = rest.astype(BF16)
    low = (rest - middle.astype(F32)).astype(BF16)
    return jnp.concatenate([high, middle, low], axis=-1)


def times(x, matrix):
    return jnp.dot(split(x), matrix, preferred_element_type=F32)


def thrice(matrix):
    return jnp.concatenate([matrix.astype(BF16)] * 3, axis=0)


def compact(planes, out):
    rows, lanes = planes[0].shape
    lane = iota2((rows, lanes), 1)
    for q in range(len(planes) // 4):
        total = planes[4 * q]
        for i in range(1, 4):
            moved = pltpu.roll(planes[4 * q + i], lanes // 4 * i, 1)
            total = jnp.where(lane < lanes // 4 * i, total, moved)
        out[q * rows:(q + 1) * rows, :] = total


def own_kernel(phase, mask, dev, c_out, g_out, strip, c2, c, g, sums, work):
    ox, oy, oz = phase.shape
    pz = lax.axis_index("pair")

    def body(x):
        c[x], g[x] = conductivity(phase[x]), mask[x].astype(F32) * dev[x]
        c_out[x] = parted(c[x])
        g_out[x] = parted(g[x])

    loop(0, ox, body, unroll=4)
    i, j = iota2((oz, oz), 0), iota2((oz, oz), 1)
    matrix = thrice(jnp.where(j == lax.div(i, 4), 1.0 / 64.0, 0.0))
    for x in range(ox // 4):
        sums[...] = (c[4 * x] + c[4 * x + 1]) + (c[4 * x + 2] + c[4 * x + 3])
        part = [sums[pl.ds(k, oy // 4, stride=4), :] for k in range(4)]
        work[x] = (part[0] + part[1]) + (part[2] + part[3])
    done = times(work[...].reshape(-1, oz), matrix)
    compact([done[x * oy // 4:(x + 1) * oy // 4] for x in range(ox // 4)], c2)
    group = oz // ZW
    turns = strip_turns(oz, jnp.where(pz == 0, oz - ZW, 0))
    lane = iota2((oy, oz), 1)
    for which, source in enumerate((c, g)):
        for a in range(ox // group):
            strip[which, a] = pack([source[group * a + b] for b in range(group)], turns, lane)


def halo_rows(ny, f, oy, up):
    if ny == 1:
        return oy
    return jnp.where(up, oy, oy + YH)


def place_halos(nx, ny, box, got, put):
    ox, oy, oz = box
    bx = lax.axis_index("boxes")
    sy = lax.axis_index("sub")
    place = 0
    row = iota2((YH, oz), 0)

    def trim(values, up):
        if ny > 1:
            return values
        return jnp.where(lax.div(row, 2) == jnp.where(up, YH // 2 - 1, 0), 0.0, values)

    def below(up, planes):
        return jnp.where(up, XH + ox, XH - planes)

    for e in range(nx):
        up = upward(bx, e)
        face = got[place]
        place += 1
        for x in range(XH):
            put(0, below(up, XH) + x, slice(0, oy), face[x])
        for x in range(GX):
            put(1, below(up, GX) + x, slice(0, oy), face[XH + x])
    for f in range(ny):
        up = upward(sy, f)
        face = got[place]
        place += 1
        rows = pl.ds(pl.multiple_of(halo_rows(ny, f, oy, up), 8), YH)

        def copy(x, face=face, rows=rows, up=up):
            put(0, XH + x, rows, trim(face[0, x], up))
            put(1, XH + x, rows, trim(face[1, x], up))

        loop(0, ox, copy, unroll=8)
    for e in range(nx):
        ux = upward(bx, e)
        for f in range(ny):
            up = upward(sy, f)
            face = got[place]
            place += 1
            rows = pl.ds(pl.multiple_of(halo_rows(ny, f, oy, up), 8), YH)
            for x in range(DC):
                put(0, below(ux, DC) + x, rows, trim(face[x], up))
            for x in range(DG):
                put(1, below(ux, DG) + x, rows, trim(face[DC + x], up))


def strip_kernel(nx, ny, own, *refs):
    count = nx + ny + nx * ny
    got, (strip, c, g) = refs[:count], refs[count:]
    planes, nrows, oz = c.shape
    oy = own.shape[2]
    ox = planes - 2 * XH
    pz = lax.axis_index("pair")
    for out in (c, g):
        for low, high in ((0, XH), (XH + ox, planes)):
            out[low:high, oy:, :] = jnp.zeros((high - low, nrows - oy, oz), F32)
    for low, high in ((0, XH - GX), (XH + ox + GX, planes)):
        g[low:high, 0:oy, :] = jnp.zeros((high - low, oy, oz), F32)

    def put(which, plane, rows, values):
        (c, g)[which][plane, rows, :] = values

    place_halos(nx, ny, (ox, oy, oz), got, put)
    group = oz // ZW
    turns = strip_turns(oz, jnp.where(pz == 0, oz - ZW, 0))
    packed = planes // group
    side = XH // group
    for which, source in enumerate((c, g)):
        for a in range(packed):
            at = which * packed + a
            if side <= a < packed - side:
                strip[at, 0:oy, :] = own[which, a - side]
                rows = slice(oy, nrows)
            else:
                rows = slice(0, nrows)
            lane = iota2((nrows - (rows.start or 0), oz), 1)
            strip[at, rows, :] = pack([source[group * a + b, rows, :] for b in range(group)], turns, lane)


def join_kernel(nx, ny, *refs):
    count = nx + ny + nx * ny
    got, (cx, gx, cy, gy) = refs[:count], refs[count:]
    planes, nrows, lanes = cy.shape
    ox, oy = planes - 2 * XH, cx.shape[1]
    for low, high in ((0, XH), (XH + ox, planes)):
        for out in (cy, gy):
            out[low:high] = jnp.zeros((high - low, nrows, lanes), F32)
    for low, high in ((0, XH - GX), (XH + GX, 2 * XH)):
        gx[low:high] = jnp.zeros((high - low, oy, lanes), F32)

    def put(which, plane, rows, values):
        if isinstance(rows, slice):
            (cx, gx)[which][jnp.where(plane < XH, plane, plane - ox)] = parted(values)
        else:
            (cy, gy)[which][plane, pl.ds(pl.multiple_of(rows.start - oy, 8), rows.size), :] = parted(values)

    place_halos(nx, ny, (ox, oy, lanes // 2), got, put)


def halve(total, work):
    work[...] = total
    return work[pl.ds(0, total.shape[0] // 2, stride=2), :] + work[pl.ds(1, total.shape[0] // 2, stride=2), :]


def pool_wide(source, low, high, out, work):
    step, _, width = work.shape

    def body(k):
        for j in range(step):
            total = source[2 * (low + step * k + j)] + source[2 * (low + step * k + j) + 1]
            out[step * k + j] = 0.125 * halve(total[:, :width] + total[:, width:], work.at[j])

    loop(0, (high - low) // step, body)


def pool(source, low, high, out, matrix, work):
    sums = [halve(source(2 * j) + source(2 * j + 1), work.at[j - low]) for j in range(low, high)]
    out[...] = times(jnp.concatenate(sums, axis=0), matrix).reshape(out.shape)


def pool_matrix(size_in, size_out, limit, shift, weight):
    i, j = iota2((size_in, size_out), 0), iota2((size_in, size_out), 1)
    return thrice(jnp.where((i < limit) & (j == shift + lax.div(i, 2)), weight, 0.0))


KEPT, FINE = 10, 3
SKIP = XH - 3
YN = 8


def near_rows(ny, oy):
    if ny > 1:
        return oy, oy + 2 * YH - YN
    return (pl.multiple_of(jnp.where(upward(lax.axis_index("sub"), 0), oy, oy + YH - YN), 8),)


def inner(ny, ref, out):
    planes = pl.ds(SKIP, out.shape[0])
    oy = out.shape[1] - ny * YN
    parts = [(ref.at[planes, pl.ds(0, oy), :], out.at[:, pl.ds(0, oy), :])]
    for f, start in enumerate(near_rows(ny, oy)):
        parts.append((ref.at[planes, pl.ds(start, YN), :], out.at[:, pl.ds(oy + f * YN, YN), :]))
    return parts


def down_kernel(nx, ny, c_own, g_own, cx, gx, cy, gy, strip, c2, *refs):
    kept, f2 = refs[:KEPT], refs[KEPT]
    faces = refs[KEPT + 1:KEPT + 1 + nx]
    held_here = refs[KEPT + 1 + nx:2 * KEPT + 1 + nx]
    c, g, u0, kx1, ky1, kz1, rd1, c1, f1, u1 = held_here
    kx, ky, kz, rd, first, v1, work, work1, low2, sems, arrivals = refs[2 * KEPT + 1 + nx:]
    pairs = []
    for a, k in zip(held_here[:FINE], kept):
        pairs += inner(ny, a, k)
    pairs += list(zip(held_here[FINE:], kept[FINE:]))
    copies = [pltpu.make_async_copy(a, k, sems.at[i]) for i, (a, k) in enumerate(pairs)]
    planes, rows, lanes = c.shape
    oz = lanes // 2
    oy = cx.shape[1]
    pz = lax.axis_index("pair")
    bx = lax.axis_index("boxes")
    group = oz // ZW
    wide = ZW // 2
    packed = planes // group
    lane = iota2((rows, oz), 1)
    start = jnp.where(pz == 0, oz // 2, oz - wide)
    own = lane < oz // 2
    near = (lane >= start) & (lane < start + wide)
    order = lax.rem(lane, oz // 2)
    order = ZW * lax.div(order, wide) + 2 * lax.rem(order, wide) + lax.div(lane, oz // 2)

    last = packed - 1

    def arriving(a, beside, which):
        out, own_planes, x_planes, y_rows = ((c, c_own, cx, cy), (g, g_own, gx, gy))[which]
        here = pl.ds(a * group, group)
        source = own_planes.at[pl.ds(0, group)]
        if beside:
            source = x_planes.at[pl.ds(a // last * group, group)]
        elif beside is False:
            source = own_planes.at[pl.ds((a - 1) * group, group)]
        return (
            pltpu.make_async_copy(source, out.at[here, pl.ds(0, oy), :], arrivals.at[4 * a + 2 * which]),
            pltpu.make_async_copy(
                y_rows.at[here], out.at[here, pl.ds(oy, rows - oy), :], arrivals.at[4 * a + 2 * which + 1]
            ),
        )

    for a in range(packed):
        for which in range(2):
            for copy in arriving(a, a in (0, last), which):
                copy.start()

    def unpack(a):
        for which, (strips, out) in enumerate(((strip[a], c), (strip[packed + a], g))):
            for copy in arriving(a, None, which):
                copy.wait()
            strips = pick(strips, order)
            for b in range(group):
                x = group * a + b
                for h in range(2):
                    cols = slice(h * oz, h * oz + oz)
                    turn = lax.rem(start + (3 - h) * (oz // 2) + oz // 2 - wide * b, oz)
                    far = jnp.where(near, pltpu.roll(strips, turn, 1), 0.0)
                    out[x, :, cols] = jnp.where(own, out[x, :, cols], far)

    loop(0, packed, unpack)
    parts = 1 + ny
    for copy in copies[:2 * parts]:
        copy.start()
    edge = XH - GX

    def start_sweep(x, factor):
        first[x] = g[x] * factor

    coefficients(c, kx, ky, kz, rd, edge, planes - edge, 1.0, start_sweep)
    sweep(first, u0, g, kx, ky, kz, rd, edge + 1, planes - edge - 1)
    for copy in copies[2 * parts:3 * parts]:
        copy.start()
    rest = first

    def use(x, vx, av):
        rest[x] = g[x] - av

    operate(u0, kx, ky, kz, edge + 2, planes - edge - 2, use)
    planes1 = planes // 2
    pool_wide(c, 0, planes1, c1, work)
    f1[...] = jnp.zeros_like(f1)
    low1 = (edge + 2) // 2
    high1 = planes1 - low1
    pool_wide(rest, low1, high1, f1.at[low1:high1], work)
    copies[3 * parts + 5].start()
    coefficients(c1, kx1, ky1, kz1, rd1, 1, planes1 - 1, 0.25)
    for copy in copies[3 * parts:3 * parts + 5]:
        copy.start()

    def start_sweep1(x):
        v1[x] = f1[x] * rd1[x]

    loop(low1, high1, start_sweep1)
    u1[...] = jnp.zeros_like(u1)
    sweep(v1, u1, f1, kx1, ky1, kz1, rd1, low1 + 1, high1 - 1)
    copies[3 * parts + 6].start()
    h1 = XH // 2
    o1 = planes1 - XH

    def use1(x, vx, av):
        v1[x] = f1[x] - av

    operate(u1, kx1, ky1, kz1, h1, planes1 - h1, use1)
    half = oz // 2
    matrix1 = pool_matrix(oz, oz, half, 0, 0.125)
    own1 = 2 * low2.shape[1]
    pool(lambda x: v1[x, 0:own1, :], h1 // 2, (planes1 - h1) // 2, low2, matrix1, work1)
    tile = c2.shape[0]
    compact([low2[x] for x in range(low2.shape[0])], f2.at[0:tile])
    f2[tile:] = c2[...]
    for e in range(nx):
        up = upward(bx, e)
        faces[e][0:h1] = u1[pl.ds(jnp.where(up, o1, h1), h1)]
        faces[e][h1:2 * h1 - 1] = f1[pl.ds(jnp.where(up, o1 + 1, h1), h1 - 1)]
    for copy in copies:
        copy.wait()


def face_kernel(ny, c_in, g_in, u_in, c, g, u0, kx, ky, kz, rd, sems):
    copies = [
        pltpu.make_async_copy(a, b, sems.at[i]) for i, (a, b) in enumerate(((c_in, c), (g_in, g), (u_in, u0)))
    ]
    for copy in copies:
        copy.start()
    planes, rows, lanes = u0.shape
    oy = rows - ny * YN
    up = upward(lax.axis_index("sub"), 0)
    copies[0].wait()
    row = iota2((YN, lanes), 0)

    def close(x):
        c[x, oy:, :] = jnp.where(row == jnp.where(up, YN - 1, 0), 0.0, c[x, oy:, :])

    if ny == 1:
        loop(0, planes, close, unroll=2)
    coefficients(c, kx, ky, kz, rd, 1, planes - 1, 1.0)
    for copy in copies[1:]:
        copy.wait()


def bottom_kernel(nx, ny, nfar, *refs):
    pieces = 1 + nx + nfar
    got = refs[:pieces]
    add, c2, f2, kx2, ky2, kz2, rd2, v2, w2, tall = refs[pieces:]
    planes2, rows2, oz = c2.shape
    o2x = planes2 - 2 * L2X
    o2y = rows2 // (ny + 1)
    bx = lax.axis_index("boxes")
    sy = lax.axis_index("sub")
    pz = lax.axis_index("pair")

    lane = iota2((o2y, oz), 1)
    row = iota2((o2y, oz), 0)
    quarter = oz // 4
    nsub = lax.axis_size("sub")
    places = [(L2X, got[0], range(o2x), None)]
    for e in range(nx):
        places.append((jnp.where(upward(bx, e), L2X + o2x, L2X - o2x), got[1 + e], range(o2x), None))
    for e in range(nfar):
        far = upward(bx, e, 2)
        places.append((jnp.where(far, L2X + 2 * o2x, 0), got[1 + nx + e], range(L2X - o2x), far))
    for f in range(ny + 1):
        y0, side, keep = 0, sy, lane < 2 * quarter
        if f > 0:
            up = upward(sy, f - 1)
            y0 = pl.multiple_of(jnp.where(up, o2y, rows2 - o2y), 8)
            side = jnp.where(up, sy + 1, sy - 1)
            keep = keep & (side >= 0) & (side < nsub)
            if ny == 1:
                keep = keep & (row != jnp.where(up, o2y - 1, 0))
        side = 2 * jnp.clip(side, 0, nsub - 1)
        for x0, message, count, far in places:
            for j in count:
                for which, out in enumerate((f2, c2)):
                    if far is None:
                        tiles = [message[side + p, which, j // 4] for p in range(2)]
                        turns = [(quarter * (p - j)) % oz for p in range(2)]
                    else:
                        tiles = [message[side + p, which] for p in range(2)]
                        at = jnp.where(far, j, o2x - (L2X - o2x) + j)
                        turns = [lax.rem(quarter * (p + o2x - at), oz) for p in range(2)]
                    low, high = (pltpu.roll(tile, turn, 1) for tile, turn in zip(tiles, turns))
                    out[x0 + j, pl.ds(y0, o2y), :] = jnp.where(keep, jnp.where(lane < quarter, low, high), 0.0)
    coefficients(c2, kx2, ky2, kz2, rd2, 1, planes2 - 1, 0.0625)

    def start_sweep2(x):
        v2[x] = f2[x] * rd2[x]

    loop(1, planes2 - 1, start_sweep2)
    old, new = v2, w2
    for k in range(2, BOTTOM_SWEEPS + 1):
        sweep(old, new, f2, kx2, ky2, kz2, rd2, k, planes2 - k)
        old, new = new, old

    i, j = iota2((oz, oz), 0), iota2((oz, oz), 1)
    spread_z = thrice(jnp.where(i == lax.div(lax.rem(pz * (oz // 2) + j, oz), 2), 1.0, 0.0))
    count, rows1, _ = add.shape
    base = (planes2 - count) // 2
    moved = times(old[base:base + count].reshape(count * rows2, oz), spread_z)
    row = iota2((8, oz), 0)
    for x in range(count):
        t = moved[x * rows2:x * rows2 + rows2]
        if ny == 1:
            halo = jnp.where(upward(sy, 0), t[o2y:o2y + 8], pltpu.roll(t[rows2 - 8:], 4, 0))
        else:
            halo = jnp.where(row < 4, t[o2y:o2y + 8], t[rows2 - 8:])
        t = jnp.concatenate([t[0:o2y], halo], axis=0)
        tall[x, pl.ds(0, o2y + 8, stride=2), :] = t
        tall[x, pl.ds(1, o2y + 8, stride=2), :] = t
        add[x] = tall[x, 0:rows1, :]


def up_kernel(nx, ny, add, c, g, u0, kx, ky, kz, rd, *refs):
    faces, (kx1, ky1, kz1, rd1, c1, f1, u1) = refs[:nx], refs[nx:nx + 7]
    outs = refs[nx + 7:nx + 9]
    field, residual, ua, ub, v1, w1, x1, wide, sems = refs[nx + 9:]
    planes, rows, lanes = u0.shape
    planes1, rows1, oz = u1.shape
    oy = field.shape[1]
    bx = lax.axis_index("boxes")

    h1 = XH // 2
    for x in range(planes1):
        v1[x] = jnp.where(c1[x] > 0.0, u1[x] + add[x // 2], 0.0)
        w1[x] = f1[x]
    for e in range(nx):
        up = upward(bx, e)
        for x in range(h1):
            at = jnp.where(up, planes1 - h1, 0) + x
            v1[at] = jnp.where(c1[at] > 0.0, faces[e][x] + add[lax.div(at, 2)], 0.0)
        for x in range(h1 - 1):
            w1[jnp.where(up, planes1 - h1, 1) + x] = faces[e][h1 + x]
    sweep(v1, x1, w1, kx1, ky1, kz1, rd1, 1, planes1 - 1)
    sweep(x1, v1, w1, kx1, ky1, kz1, rd1, 2, planes1 - 2)

    step = wide.shape[0]
    low = (SKIP + 1) // 2

    def spread0(x, m, fine):
        wide[m, pl.ds(0, rows1, stride=2), :] = v1[x]
        wide[m, pl.ds(1, rows1, stride=2), :] = v1[x]
        moved = [wide[m, 0:oy]] + [wide[m, pl.ds(start, YN)] for start in near_rows(ny, oy)]
        moved = jnp.concatenate(moved, axis=0)
        moved = jnp.concatenate([moved, moved], axis=1)
        for y in fine:
            ua[y] = jnp.where(c[y] > 0.0, u0[y] + moved, 0.0)

    def several(n):
        for m in range(step):
            x = low + step * n + m
            spread0(x, m, (2 * x - SKIP, 2 * x + 1 - SKIP))

    loop(0, (planes1 - 2 * low) // step, several)
    spread0(low - 1, 0, (0,))
    spread0(planes1 - low, 1, (planes - 1,))
    sweep(ua, ub, g, kx, ky, kz, rd, 1, planes - 1)
    sweep(ub, ua, g, kx, ky, kz, rd, 2, planes - 2)
    order = joining((oy, oz))
    ox, chunk = field.shape[0], XH
    copies = []
    for k in range(ox // chunk):
        base = 3 + k * chunk

        def use(x, vx, av):
            field[x - 3] = joined(vx[0:oy], *order)
            residual[x - 3] = joined(g[x, 0:oy, :] - av[0:oy], *order)

        operate(ua, kx, ky, kz, base, base + chunk, use)
        here = pl.ds(k * chunk, chunk)
        for n, (a, b) in enumerate(zip((field, residual), outs)):
            copies.append(pltpu.make_async_copy(a.at[here], b.at[here], sems.at[2 * k + n]))
            copies[-1].start()
    for copy in copies:
        copy.wait()


def call(kernel, outs, scratch=(), mib=16, raw_in=0, raw_out=0, copies=0, more=0):
    where = [pl.BlockSpec(memory_space=pltpu.HBM)], [pl.BlockSpec(memory_space=pltpu.VMEM)]
    outs = tuple(pltpu.HBM(o.shape, o.dtype) if i < raw_out else o for i, o in enumerate(outs))
    extra = tuple(pltpu.SemaphoreType.DMA((n,)) for n in (copies, more) if n)

    def run(*operands):
        operands = [pltpu.with_memory_space_constraint(x, pltpu.HBM) if i < raw_in else x for i, x in enumerate(operands)]
        return pl.pallas_call(
            kernel,
            in_specs=where[0] * raw_in + where[1] * (len(operands) - raw_in),
            out_specs=tuple(where[0] * raw_out + where[1] * (len(outs) - raw_out)),
            out_shape=outs,
            scratch_shapes=tuple(s if hasattr(s, "memory_space") else pltpu.VMEM(s, F32) for s in scratch) + extra,
            compiler_params=params(mib),
        )(*operands)

    return run


def per_device(phase, target_mask, deviation):
    ox, oy, oz = phase.shape
    nbox, nsub = lax.axis_size("boxes"), lax.axis_size("sub")
    swap_x, swap_y, far_x = exchanges(nbox), exchanges(nsub), exchanges(nbox, 2)
    nx, ny, nfar = len(swap_x), len(swap_y), len(far_x)
    pair_swap = [(0, 1), (1, 0)]

    def both(px, py):
        return [(a * nsub + c, b * nsub + d) for a, b in px for c, d in py]

    def traded(faces):
        out = []
        for e in range(nx):
            out.append(lax.ppermute(faces[e], "boxes", swap_x[e]))
        for f in range(ny):
            out.append(lax.ppermute(faces[nx + f], "sub", swap_y[f]))
        for e in range(nx):
            for f in range(ny):
                out.append(lax.ppermute(faces[nx + ny + e * ny + f], ("boxes", "sub"), both(swap_x[e], swap_y[f])))
        return out

    planes, rows = ox + 2 * XH, oy + YH * ny
    planes1, rows1 = planes // 2, rows // 2
    o2x, o2y = ox // 4, oy // 4
    planes2 = o2x + 2 * L2X
    rows2 = o2y * (ny + 1)

    box = spec((ox, oy, oz))
    faces = [spec((XH + GX, oy, oz))] * nx + [spec((2, ox, YH, oz))] * ny + [spec((DC + DG, YH, oz))] * (nx * ny)
    width, edge = (nx, GX, oy, oz), (ny, ox, YH, oz)
    faces = call(
        lambda *r: send_kernel(nx, ny, *r),
        faces,
        [(nx, XH, oy, oz), pltpu.VMEM(width, jnp.int32), width, edge, pltpu.VMEM(edge, jnp.int32), edge],
        raw_in=3,
        copies=3 * (nx + ny),
    )(phase, target_mask, deviation)
    got = traded(faces)
    phase, target_mask, deviation, _ = lax.optimization_barrier((phase, target_mask, deviation, faces))
    group = oz // ZW
    padded = (planes, rows, oz)
    fine = (planes, rows, 2 * oz)
    parted_box = in_hbm((ox, oy, 2 * oz))
    c, g, own, c2 = call(
        own_kernel,
        [parted_box, parted_box, spec((2, ox // group, oy, oz)), spec((o2x // 4 * o2y, oz))],
        [(ox, oy, oz), (ox, oy, oz), (oy, oz), (o2x, o2y, oz)],
    )(phase, target_mask, deviation)
    (strip,) = call(
        lambda *r: strip_kernel(nx, ny, *r), [spec((2 * planes // group, rows, oz))], [padded, padded]
    )(own, *got)
    strip = lax.ppermute(strip, "pair", pair_swap)
    halos = [(2 * XH, oy, 2 * oz)] * 2 + [(planes, rows - oy, 2 * oz)] * 2
    halos = call(lambda *r: join_kernel(nx, ny, *r), [in_vmem(h) for h in halos], mib=6)(*got)
    middle = (planes1, rows1, oz)
    small = (planes - 2 * SKIP, oy + ny * YN, 2 * oz)
    down = call(
        lambda *r: down_kernel(nx, ny, *r),
        [spec(small)] * FINE + [spec(middle)] * (KEPT - FINE) + [spec((o2x // 2 * o2y, oz))]
        + [spec((XH - 1, rows1, oz))] * nx,
        [fine] * FINE + [middle] * (KEPT - FINE) + [fine] * 5 + [middle, (4, rows, oz), (o2x, oy // 2, oz), (o2x, o2y, oz)],
        mib=48,
        raw_in=2,
        raw_out=KEPT,
        copies=KEPT + FINE * ny,
        more=4 * planes // group,
    )(c, g, *[held(h) for h in halos], strip, c2)
    kept, f2, sides = down[:KEPT], down[KEPT], down[KEPT + 1:]
    sheet = lax.all_gather(f2, ("sub", "pair")).reshape(-1, 2, o2x // 4, o2y, oz)
    first, sheet = lax.optimization_barrier((kept[:FINE], sheet))
    fine_up = call(lambda *r: face_kernel(ny, *r), [in_vmem(small)] * 7, mib=6, raw_in=FINE, copies=FINE)(*first)
    got = [sheet] + [lax.ppermute(sheet, "boxes", p) for p in swap_x]
    for e, p in enumerate(far_x):
        at = jnp.where(upward(lax.axis_index("boxes"), e, 2), o2x // 4 - 1, 0)
        got.append(lax.ppermute(lax.dynamic_index_in_dim(sheet, at, 2, keepdims=False), "boxes", p))
    got, sides, fine_up = lax.optimization_barrier((got, sides, fine_up))
    sides = [lax.ppermute(side, "boxes", p) for side, p in zip(sides, swap_x)]
    lowest = (planes2, rows2, oz)
    (add,) = call(
        lambda *r: bottom_kernel(nx, ny, nfar, *r),
        [in_vmem((planes1 // 2, rows1, oz))],
        [lowest] * 8 + [(planes1 // 2, 2 * (o2y + 8), oz)],
        mib=12,
    )(*got)
    return tuple(call(
        lambda *r: up_kernel(nx, ny, *r),
        [box, box],
        [(ox, oy, oz)] * 2 + [small, small, middle, middle, middle, (3, rows, oz)],
        mib=16,
        raw_out=2,
        copies=2 * (ox // XH),
    )(held(add), *[held(x) for x in fine_up], *sides, *kept[FINE:]))


def solution(mesh):
    where = P(("groups", "boxes"), "sub", "pair")
    return jax.shard_map(
        per_device,
        mesh=mesh,
        in_specs=(where, where, where),
        out_specs=(where, where),
        check_vma=False,
    )
```

```python
import jax
import jax.numpy as jnp
from jax import lax
from jax.experimental import pallas as pl
from jax.experimental.pallas import tpu as pltpu
from jax.sharding import PartitionSpec as P

SWEEPS = 2
BOTTOM_SWEEPS = 8

floor_conduct = 0.1
relax_weight = 0.8

XH = 8
YH = 16
GX = 6
DC, DG = 6, 5
ZW = 16
L2X = 10
F32 = jnp.float32
BF16 = jnp.bfloat16
MIB = 1 << 20


def exchanges(count, step=1):
    swaps = []
    for e in range(2):
        pairs = []
        for i in range(count):
            if (i // step + e) % 2 == 0 and i + step < count:
                pairs += [(i, i + step), (i + step, i)]
        if pairs:
            swaps.append(pairs)
    return swaps


def upward(index, e, step=1):
    return (index // step + e) % 2 == 0


def spec(shape):
    return jax.ShapeDtypeStruct(shape, F32)


def in_vmem(shape):
    return pltpu.VMEM(shape, F32)


def in_hbm(shape):
    return pltpu.HBM(shape, F32)


def held(x):
    return pltpu.with_memory_space_constraint(x, pltpu.VMEM)


def params(mib):
    return pltpu.CompilerParams(vmem_limit_bytes=mib * MIB)


def roll_up(v, axis):
    return pltpu.roll(v, v.shape[axis] - 1, axis)


def roll_down(v, axis):
    return pltpu.roll(v, 1, axis)


def next_z(v):
    half = v.shape[1] // 2
    if half < 128:
        return roll_up(v, 1)
    return jnp.concatenate([v[:, half:], roll_up(v[:, :half], 1)], axis=1)


def previous_z(v):
    half = v.shape[1] // 2
    if half < 128:
        return roll_down(v, 1)
    return jnp.concatenate([roll_down(v[:, half:], 1), v[:, :half]], axis=1)


def pick(v, lanes):
    return jnp.take_along_axis(v, lanes, axis=1)


def parted(v):
    lane = iota2(v.shape, 1)
    even = lax.rem(2 * lane, v.shape[1])
    return jnp.concatenate([pick(v, even), pick(v, even + 1)], axis=1)


def joining(shape):
    lane = iota2(shape, 1)
    return lax.rem(lane, 2) == 0, lax.div(lane, 2)


def joined(v, even, at):
    half = v.shape[1] // 2
    return jnp.where(even, pick(v[:, :half], at), pick(v[:, half:], at))


def loop(low, high, body, init=None, unroll=1):
    def step(i, carry):
        if init is None:
            body(i)
            return carry
        return body(i, carry)

    carry = 0 if init is None else init
    whole = (high - low) // unroll
    if whole > 1:

        def several(k, carry):
            for j in range(unroll):
                carry = step(low + k * unroll + j, carry)
            return carry

        carry = lax.fori_loop(0, whole, several, carry)
        low += whole * unroll
    for i in range(low, high):
        carry = step(i, carry)
    return carry


def unrolling(ref):
    return UNROLL.get(ref.shape[1] * ref.shape[2] // 1024, 4)


UNROLL = {20: 6, 18: 4, 6: 8, 5: 8, 4: 10}


def coefficients(c, kx, ky, kz, rd, low, high, scale, also=lambda x, factor: None):
    half = 0.5 * scale

    def faces(x):
        cx = c[x]
        fx = half * (cx + c[x + 1])
        fy = half * (cx + roll_up(cx, 0))
        fz = half * (cx + next_z(cx))
        kx[x] = fx
        ky[x] = fy
        kz[x] = fz
        return cx, fx, fy, fz

    _, first, _, _ = faces(low - 1)

    def body(x, before):
        cx, fx, fy, fz = faces(x)
        diagonal = fx + before + fy + roll_down(fy, 0) + fz + previous_z(fz)
        inside = cx > 0.0
        factor = jnp.where(inside, relax_weight / jnp.where(inside, diagonal, 1.0), 0.0)
        rd[x] = factor
        also(x, factor)
        return fx

    loop(low, high, body, first, unrolling(rd))


def operate(v, kx, ky, kz, low, high, use):
    def body(x, before):
        vx = v[x]
        fx = kx[x] * (vx - v[x + 1])
        fy = ky[x] * (vx - roll_up(vx, 0))
        fz = kz[x] * (vx - next_z(vx))
        use(x, vx, (fx - before) + (fy - roll_down(fy, 0)) + (fz - previous_z(fz)))
        return fx

    loop(low, high, body, kx[low - 1] * (v[low - 1] - v[low]), unrolling(v))


def sweep(v, out, g, kx, ky, kz, rd, low, high):
    def use(x, vx, av):
        out[x] = vx + rd[x] * (g[x] - av)

    operate(v, kx, ky, kz, low, high, use)


def iota2(shape, dim):
    return lax.broadcasted_iota(jnp.int32, shape, dim)


def conductivity(p):
    return floor_conduct + (1.0 - floor_conduct) * (p * p * p)


def send_kernel(nx, ny, phase, mask, dev, *refs):
    count = nx + ny + nx * ny
    outs = refs[:count]
    px, mx, dx, py, my, dy, sems = refs[count:]
    ox, oy, _ = phase.shape
    ups = [upward(lax.axis_index("boxes"), e) for e in range(nx)]
    rows = [pl.multiple_of(jnp.where(upward(lax.axis_index("sub"), f), oy - YH, 0), 8) for f in range(ny)]
    copies = []
    for f in range(ny):
        for source, out in ((phase, py), (mask, my), (dev, dy)):
            copies.append((source.at[:, pl.ds(rows[f], YH), :], out.at[f]))
    for e in range(nx):
        for source, out, width in ((phase, px, XH), (mask, mx, GX), (dev, dx, GX)):
            copies.append((source.at[pl.ds(jnp.where(ups[e], ox - width, 0), width)], out.at[e]))
    copies = [pltpu.make_async_copy(a, b, sems.at[i]) for i, (a, b) in enumerate(copies)]
    for copy in copies:
        copy.start()
    for copy in copies[:3 * ny]:
        copy.wait()
    for f in range(ny):
        face = outs[nx + f]

        def body(x, face=face, f=f):
            face[0, x] = conductivity(py[f, x])
            face[1, x] = my[f, x].astype(F32) * dy[f, x]

        loop(0, ox, body, unroll=8)
        for e in range(nx):
            corner = outs[nx + ny + e * ny + f]
            corner[0:DC] = face[0, pl.ds(jnp.where(ups[e], ox - DC, 0), DC)]
            corner[DC:DC + DG] = face[1, pl.ds(jnp.where(ups[e], ox - DG, 0), DG)]
    for copy in copies[3 * ny:]:
        copy.wait()
    for e in range(nx):
        for x in range(XH):
            outs[e][x] = conductivity(px[e, x])
        for x in range(GX):
            outs[e][XH + x] = mx[e, x].astype(F32) * dx[e, x]


def pack(planes, turns, lane):
    total = None
    for b, (plane, turn) in enumerate(zip(planes, turns)):
        moved = pltpu.roll(plane, turn, 1)
        total = moved if total is None else jnp.where(lane >= ZW * b, moved, total)
    return total


def strip_turns(oz, start):
    return [lax.rem(ZW * b + oz - start, oz) for b in range(oz // ZW)]


def split(x):
    high = x.astype(BF16)
    rest = x - high.astype(F32)
    middle = rest.astype(BF16)
    low = (rest - middle.astype(F32)).astype(BF16)
    return jnp.concatenate([high, middle, low], axis=-1)


def times(x, matrix):
    return jnp.dot(split(x), matrix, preferred_element_type=F32)


def thrice(matrix):
    return jnp.concatenate([matrix.astype(BF16)] * 3, axis=0)


def compact(planes, out):
    rows, lanes = planes[0].shape
    lane = iota2((rows, lanes), 1)
    for q in range(len(planes) // 4):
        total = planes[4 * q]
        for i in range(1, 4):
            moved = pltpu.roll(planes[4 * q + i], lanes // 4 * i, 1)
            total = jnp.where(lane < lanes // 4 * i, total, moved)
        out[q * rows:(q + 1) * rows, :] = total


def own_kernel(phase, mask, dev, c_out, g_out, strip, c2, c, g, sums, work):
    ox, oy, oz = phase.shape
    pz = lax.axis_index("pair")

    def body(x):
        c[x], g[x] = conductivity(phase[x]), mask[x].astype(F32) * dev[x]
        c_out[x] = parted(c[x])
        g_out[x] = parted(g[x])

    loop(0, ox, body, unroll=4)
    i, j = iota2((oz, oz), 0), iota2((oz, oz), 1)
    matrix = thrice(jnp.where(j == lax.div(i, 4), 1.0 / 64.0, 0.0))
    for x in range(ox // 4):
        sums[...] = (c[4 * x] + c[4 * x + 1]) + (c[4 * x + 2] + c[4 * x + 3])
        part = [sums[pl.ds(k, oy // 4, stride=4), :] for k in range(4)]
        work[x] = (part[0] + part[1]) + (part[2] + part[3])
    done = times(work[...].reshape(-1, oz), matrix)
    compact([done[x * oy // 4:(x + 1) * oy // 4] for x in range(ox // 4)], c2)
    group = oz // ZW
    turns = strip_turns(oz, jnp.where(pz == 0, oz - ZW, 0))
    lane = iota2((oy, oz), 1)
    for which, source in enumerate((c, g)):
        for a in range(ox // group):
            strip[which, a] = pack([source[group * a + b] for b in range(group)], turns, lane)


def halo_rows(ny, f, oy, up):
    if ny == 1:
        return oy
    return jnp.where(up, oy, oy + YH)


def place_halos(nx, ny, box, got, put):
    ox, oy, oz = box
    bx = lax.axis_index("boxes")
    sy = lax.axis_index("sub")
    place = 0
    row = iota2((YH, oz), 0)

    def trim(values, up):
        if ny > 1:
            return values
        return jnp.where(lax.div(row, 2) == jnp.where(up, YH // 2 - 1, 0), 0.0, values)

    def below(up, planes):
        return jnp.where(up, XH + ox, XH - planes)

    for e in range(nx):
        up = upward(bx, e)
        face = got[place]
        place += 1
        for x in range(XH):
            put(0, below(up, XH) + x, slice(0, oy), face[x])
        for x in range(GX):
            put(1, below(up, GX) + x, slice(0, oy), face[XH + x])
    for f in range(ny):
        up = upward(sy, f)
        face = got[place]
        place += 1
        rows = pl.ds(pl.multiple_of(halo_rows(ny, f, oy, up), 8), YH)

        def copy(x, face=face, rows=rows, up=up):
            put(0, XH + x, rows, trim(face[0, x], up))
            put(1, XH + x, rows, trim(face[1, x], up))

        loop(0, ox, copy, unroll=8)
    for e in range(nx):
        ux = upward(bx, e)
        for f in range(ny):
            up = upward(sy, f)
            face = got[place]
            place += 1
            rows = pl.ds(pl.multiple_of(halo_rows(ny, f, oy, up), 8), YH)
            for x in range(DC):
                put(0, below(ux, DC) + x, rows, trim(face[x], up))
            for x in range(DG):
                put(1, below(ux, DG) + x, rows, trim(face[DC + x], up))


def strip_kernel(nx, ny, own, *refs):
    count = nx + ny + nx * ny
    got, (strip, c, g) = refs[:count], refs[count:]
    planes, nrows, oz = c.shape
    oy = own.shape[2]
    ox = planes - 2 * XH
    pz = lax.axis_index("pair")
    for out in (c, g):
        for low, high in ((0, XH), (XH + ox, planes)):
            out[low:high, oy:, :] = jnp.zeros((high - low, nrows - oy, oz), F32)
    for low, high in ((0, XH - GX), (XH + ox + GX, planes)):
        g[low:high, 0:oy, :] = jnp.zeros((high - low, oy, oz), F32)

    def put(which, plane, rows, values):
        (c, g)[which][plane, rows, :] = values

    place_halos(nx, ny, (ox, oy, oz), got, put)
    group = oz // ZW
    turns = strip_turns(oz, jnp.where(pz == 0, oz - ZW, 0))
    packed = planes // group
    side = XH // group
    for which, source in enumerate((c, g)):
        for a in range(packed):
            at = which * packed + a
            if side <= a < packed - side:
                strip[at, 0:oy, :] = own[which, a - side]
                rows = slice(oy, nrows)
            else:
                rows = slice(0, nrows)
            lane = iota2((nrows - (rows.start or 0), oz), 1)
            strip[at, rows, :] = pack([source[group * a + b, rows, :] for b in range(group)], turns, lane)


def join_kernel(nx, ny, *refs):
    count = nx + ny + nx * ny
    got, (cx, gx, cy, gy) = refs[:count], refs[count:]
    planes, nrows, lanes = cy.shape
    ox, oy = planes - 2 * XH, cx.shape[1]
    for low, high in ((0, XH), (XH + ox, planes)):
        for out in (cy, gy):
            out[low:high] = jnp.zeros((high - low, nrows, lanes), F32)
    for low, high in ((0, XH - GX), (XH + GX, 2 * XH)):
        gx[low:high] = jnp.zeros((high - low, oy, lanes), F32)

    def put(which, plane, rows, values):
        if isinstance(rows, slice):
            (cx, gx)[which][jnp.where(plane < XH, plane, plane - ox)] = parted(values)
        else:
            (cy, gy)[which][plane, pl.ds(pl.multiple_of(rows.start - oy, 8), rows.size), :] = parted(values)

    place_halos(nx, ny, (ox, oy, lanes // 2), got, put)


def halve(total, work):
    work[...] = total
    return work[pl.ds(0, total.shape[0] // 2, stride=2), :] + work[pl.ds(1, total.shape[0] // 2, stride=2), :]


def pool_wide(source, low, high, out, work):
    step, _, width = work.shape

    def body(k):
        for j in range(step):
            total = source[2 * (low + step * k + j)] + source[2 * (low + step * k + j) + 1]
            out[step * k + j] = 0.125 * halve(total[:, :width] + total[:, width:], work.at[j])

    loop(0, (high - low) // step, body)


def pool(source, low, high, out, matrix, work):
    sums = [halve(source(2 * j) + source(2 * j + 1), work.at[j - low]) for j in range(low, high)]
    out[...] = times(jnp.concatenate(sums, axis=0), matrix).reshape(out.shape)


def pool_matrix(size_in, size_out, limit, shift, weight):
    i, j = iota2((size_in, size_out), 0), iota2((size_in, size_out), 1)
    return thrice(jnp.where((i < limit) & (j == shift + lax.div(i, 2)), weight, 0.0))


KEPT, FINE = 10, 3
SKIP = XH - 3
YN = 8


def near_rows(ny, oy):
    if ny > 1:
        return oy, oy + 2 * YH - YN
    return (pl.multiple_of(jnp.where(upward(lax.axis_index("sub"), 0), oy, oy + YH - YN), 8),)


def inner(ny, ref, out):
    planes = pl.ds(SKIP, out.shape[0])
    oy = out.shape[1] - ny * YN
    parts = [(ref.at[planes, pl.ds(0, oy), :], out.at[:, pl.ds(0, oy), :])]
    for f, start in enumerate(near_rows(ny, oy)):
        parts.append((ref.at[planes, pl.ds(start, YN), :], out.at[:, pl.ds(oy + f * YN, YN), :]))
    return parts


def down_kernel(nx, ny, c_own, g_own, cx, gx, cy, gy, strip, c2, *refs):
    kept, f2 = refs[:KEPT], refs[KEPT]
    faces = refs[KEPT + 1:KEPT + 1 + nx]
    held_here = refs[KEPT + 1 + nx:2 * KEPT + 1 + nx]
    c, g, u0, kx1, ky1, kz1, rd1, c1, f1, u1 = held_here
    kx, ky, kz, rd, first, v1, work, work1, low2, sems, arrivals = refs[2 * KEPT + 1 + nx:]
    pairs = []
    for a, k in zip(held_here[:FINE], kept):
        pairs += inner(ny, a, k)
    pairs += list(zip(held_here[FINE:], kept[FINE:]))
    copies = [pltpu.make_async_copy(a, k, sems.at[i]) for i, (a, k) in enumerate(pairs)]
    planes, rows, lanes = c.shape
    oz = lanes // 2
    oy = cx.shape[1]
    pz = lax.axis_index("pair")
    bx = lax.axis_index("boxes")
    group = oz // ZW
    wide = ZW // 2
    packed = planes // group
    lane = iota2((rows, oz), 1)
    start = jnp.where(pz == 0, oz // 2, oz - wide)
    own = lane < oz // 2
    near = (lane >= start) & (lane < start + wide)
    order = lax.rem(lane, oz // 2)
    order = ZW * lax.div(order, wide) + 2 * lax.rem(order, wide) + lax.div(lane, oz // 2)

    last = packed - 1

    def arriving(a, beside, which):
        out, own_planes, x_planes, y_rows = ((c, c_own, cx, cy), (g, g_own, gx, gy))[which]
        here = pl.ds(a * group, group)
        source = own_planes.at[pl.ds(0, group)]
        if beside:
            source = x_planes.at[pl.ds(a // last * group, group)]
        elif beside is False:
            source = own_planes.at[pl.ds((a - 1) * group, group)]
        return (
            pltpu.make_async_copy(source, out.at[here, pl.ds(0, oy), :], arrivals.at[4 * a + 2 * which]),
            pltpu.make_async_copy(
                y_rows.at[here], out.at[here, pl.ds(oy, rows - oy), :], arrivals.at[4 * a + 2 * which + 1]
            ),
        )

    for a in range(packed):
        for which in range(2):
            for copy in arriving(a, a in (0, last), which):
                copy.start()

    def unpack(a):
        for which, (strips, out) in enumerate(((strip[a], c), (strip[packed + a], g))):
            for copy in arriving(a, None, which):
                copy.wait()
            strips = pick(strips, order)
            for b in range(group):
                x = group * a + b
                for h in range(2):
                    cols = slice(h * oz, h * oz + oz)
                    turn = lax.rem(start + (3 - h) * (oz // 2) + oz // 2 - wide * b, oz)
                    far = jnp.where(near, pltpu.roll(strips, turn, 1), 0.0)
                    out[x, :, cols] = jnp.where(own, out[x, :, cols], far)

    loop(0, packed, unpack)
    parts = 1 + ny
    for copy in copies[:2 * parts]:
        copy.start()
    edge = XH - GX

    def start_sweep(x, factor):
        first[x] = g[x] * factor

    coefficients(c, kx, ky, kz, rd, edge, planes - edge, 1.0, start_sweep)
    sweep(first, u0, g, kx, ky, kz, rd, edge + 1, planes - edge - 1)
    for copy in copies[2 * parts:3 * parts]:
        copy.start()
    rest = first

    def use(x, vx, av):
        rest[x] = g[x] - av

    operate(u0, kx, ky, kz, edge + 2, planes - edge - 2, use)
    planes1 = planes // 2
    pool_wide(c, 0, planes1, c1, work)
    f1[...] = jnp.zeros_like(f1)
    low1 = (edge + 2) // 2
    high1 = planes1 - low1
    pool_wide(rest, low1, high1, f1.at[low1:high1], work)
    copies[3 * parts + 5].start()
    coefficients(c1, kx1, ky1, kz1, rd1, 1, planes1 - 1, 0.25)
    for copy in copies[3 * parts:3 * parts + 5]:
        copy.start()

    def start_sweep1(x):
        v1[x] = f1[x] * rd1[x]

    loop(low1, high1, start_sweep1)
    u1[...] = jnp.zeros_like(u1)
    sweep(v1, u1, f1, kx1, ky1, kz1, rd1, low1 + 1, high1 - 1)
    copies[3 * parts + 6].start()
    h1 = XH // 2
    o1 = planes1 - XH

    def use1(x, vx, av):
        v1[x] = f1[x] - av

    operate(u1, kx1, ky1, kz1, h1, planes1 - h1, use1)
    half = oz // 2
    matrix1 = pool_matrix(oz, oz, half, 0, 0.125)
    own1 = 2 * low2.shape[1]
    pool(lambda x: v1[x, 0:own1, :], h1 // 2, (planes1 - h1) // 2, low2, matrix1, work1)
    tile = c2.shape[0]
    compact([low2[x] for x in range(low2.shape[0])], f2.at[0:tile])
    f2[tile:] = c2[...]
    for e in range(nx):
        up = upward(bx, e)
        faces[e][0:h1] = u1[pl.ds(jnp.where(up, o1, h1), h1)]
        faces[e][h1:2 * h1 - 1] = f1[pl.ds(jnp.where(up, o1 + 1, h1), h1 - 1)]
    for copy in copies:
        copy.wait()


def face_kernel(ny, c_in, g_in, u_in, c, g, u0, kx, ky, kz, rd, sems):
    copies = [
        pltpu.make_async_copy(a, b, sems.at[i]) for i, (a, b) in enumerate(((c_in, c), (g_in, g), (u_in, u0)))
    ]
    for copy in copies:
        copy.start()
    planes, rows, lanes = u0.shape
    oy = rows - ny * YN
    up = upward(lax.axis_index("sub"), 0)
    copies[0].wait()
    row = iota2((YN, lanes), 0)

    def close(x):
        c[x, oy:, :] = jnp.where(row == jnp.where(up, YN - 1, 0), 0.0, c[x, oy:, :])

    if ny == 1:
        loop(0, planes, close, unroll=2)
    coefficients(c, kx, ky, kz, rd, 1, planes - 1, 1.0)
    for copy in copies[1:]:
        copy.wait()


def bottom_kernel(nx, ny, nfar, *refs):
    pieces = 1 + nx + nfar
    got = refs[:pieces]
    add, c2, f2, kx2, ky2, kz2, rd2, v2, w2, tall = refs[pieces:]
    planes2, rows2, oz = c2.shape
    o2x = planes2 - 2 * L2X
    o2y = rows2 // (ny + 1)
    bx = lax.axis_index("boxes")
    sy = lax.axis_index("sub")
    pz = lax.axis_index("pair")

    lane = iota2((o2y, oz), 1)
    row = iota2((o2y, oz), 0)
    quarter = oz // 4
    nsub = lax.axis_size("sub")
    places = [(L2X, got[0], range(o2x), None)]
    for e in range(nx):
        places.append((jnp.where(upward(bx, e), L2X + o2x, L2X - o2x), got[1 + e], range(o2x), None))
    for e in range(nfar):
        far = upward(bx, e, 2)
        places.append((jnp.where(far, L2X + 2 * o2x, 0), got[1 + nx + e], range(L2X - o2x), far))
    for f in range(ny + 1):
        y0, side, keep = 0, sy, lane < 2 * quarter
        if f > 0:
            up = upward(sy, f - 1)
            y0 = pl.multiple_of(jnp.where(up, o2y, rows2 - o2y), 8)
            side = jnp.where(up, sy + 1, sy - 1)
            keep = keep & (side >= 0) & (side < nsub)
            if ny == 1:
                keep = keep & (row != jnp.where(up, o2y - 1, 0))
        side = 2 * jnp.clip(side, 0, nsub - 1)
        for x0, message, count, far in places:
            for j in count:
                for which, out in enumerate((f2, c2)):
                    if far is None:
                        tiles = [message[side + p, which, j // 4] for p in range(2)]
                        turns = [(quarter * (p - j)) % oz for p in range(2)]
                    else:
                        tiles = [message[side + p, which] for p in range(2)]
                        at = jnp.where(far, j, o2x - (L2X - o2x) + j)
                        turns = [lax.rem(quarter * (p + o2x - at), oz) for p in range(2)]
                    low, high = (pltpu.roll(tile, turn, 1) for tile, turn in zip(tiles, turns))
                    out[x0 + j, pl.ds(y0, o2y), :] = jnp.where(keep, jnp.where(lane < quarter, low, high), 0.0)
    coefficients(c2, kx2, ky2, kz2, rd2, 1, planes2 - 1, 0.0625)

    def start_sweep2(x):
        v2[x] = f2[x] * rd2[x]

    loop(1, planes2 - 1, start_sweep2)
    old, new = v2, w2
    for k in range(2, BOTTOM_SWEEPS + 1):
        sweep(old, new, f2, kx2, ky2, kz2, rd2, k, planes2 - k)
        old, new = new, old

    i, j = iota2((oz, oz), 0), iota2((oz, oz), 1)
    spread_z = thrice(jnp.where(i == lax.div(lax.rem(pz * (oz // 2) + j, oz), 2), 1.0, 0.0))
    count, rows1, _ = add.shape
    base = (planes2 - count) // 2
    moved = times(old[base:base + count].reshape(count * rows2, oz), spread_z)
    row = iota2((8, oz), 0)
    for x in range(count):
        t = moved[x * rows2:x * rows2 + rows2]
        if ny == 1:
            halo = jnp.where(upward(sy, 0), t[o2y:o2y + 8], pltpu.roll(t[rows2 - 8:], 4, 0))
        else:
            halo = jnp.where(row < 4, t[o2y:o2y + 8], t[rows2 - 8:])
        t = jnp.concatenate([t[0:o2y], halo], axis=0)
        tall[x, pl.ds(0, o2y + 8, stride=2), :] = t
        tall[x, pl.ds(1, o2y + 8, stride=2), :] = t
        add[x] = tall[x, 0:rows1, :]


def up_kernel(nx, ny, add, c, g, u0, kx, ky, kz, rd, *refs):
    faces, (kx1, ky1, kz1, rd1, c1, f1, u1) = refs[:nx], refs[nx:nx + 7]
    outs = refs[nx + 7:nx + 9]
    field, residual, ua, ub, v1, w1, x1, wide, sems = refs[nx + 9:]
    planes, rows, lanes = u0.shape
    planes1, rows1, oz = u1.shape
    oy = field.shape[1]
    bx = lax.axis_index("boxes")

    h1 = XH // 2
    for x in range(planes1):
        v1[x] = jnp.where(c1[x] > 0.0, u1[x] + add[x // 2], 0.0)
        w1[x] = f1[x]
    for e in range(nx):
        up = upward(bx, e)
        for x in range(h1):
            at = jnp.where(up, planes1 - h1, 0) + x
            v1[at] = jnp.where(c1[at] > 0.0, faces[e][x] + add[lax.div(at, 2)], 0.0)
        for x in range(h1 - 1):
            w1[jnp.where(up, planes1 - h1, 1) + x] = faces[e][h1 + x]
    sweep(v1, x1, w1, kx1, ky1, kz1, rd1, 1, planes1 - 1)
    sweep(x1, v1, w1, kx1, ky1, kz1, rd1, 2, planes1 - 2)

    step = wide.shape[0]
    low = (SKIP + 1) // 2

    def spread0(x, m, fine):
        wide[m, pl.ds(0, rows1, stride=2), :] = v1[x]
        wide[m, pl.ds(1, rows1, stride=2), :] = v1[x]
        moved = [wide[m, 0:oy]] + [wide[m, pl.ds(start, YN)] for start in near_rows(ny, oy)]
        moved = jnp.concatenate(moved, axis=0)
        moved = jnp.concatenate([moved, moved], axis=1)
        for y in fine:
            ua[y] = jnp.where(c[y] > 0.0, u0[y] + moved, 0.0)

    def several(n):
        for m in range(step):
            x = low + step * n + m
            spread0(x, m, (2 * x - SKIP, 2 * x + 1 - SKIP))

    loop(0, (planes1 - 2 * low) // step, several)
    spread0(low - 1, 0, (0,))
    spread0(planes1 - low, 1, (planes - 1,))
    sweep(ua, ub, g, kx, ky, kz, rd, 1, planes - 1)
    sweep(ub, ua, g, kx, ky, kz, rd, 2, planes - 2)
    order = joining((oy, oz))
    ox, chunk = field.shape[0], XH
    copies = []
    for k in range(ox // chunk):
        base = 3 + k * chunk

        def use(x, vx, av):
            field[x - 3] = joined(vx[0:oy], *order)
            residual[x - 3] = joined(g[x, 0:oy, :] - av[0:oy], *order)

        operate(ua, kx, ky, kz, base, base + chunk, use)
        here = pl.ds(k * chunk, chunk)
        for n, (a, b) in enumerate(zip((field, residual), outs)):
            copies.append(pltpu.make_async_copy(a.at[here], b.at[here], sems.at[2 * k + n]))
            copies[-1].start()
    for copy in copies:
        copy.wait()


def call(kernel, outs, scratch=(), mib=16, raw_in=0, raw_out=0, copies=0, more=0):
    where = [pl.BlockSpec(memory_space=pltpu.HBM)], [pl.BlockSpec(memory_space=pltpu.VMEM)]
    outs = tuple(pltpu.HBM(o.shape, o.dtype) if i < raw_out else o for i, o in enumerate(outs))
    extra = tuple(pltpu.SemaphoreType.DMA((n,)) for n in (copies, more) if n)

    def run(*operands):
        operands = [pltpu.with_memory_space_constraint(x, pltpu.HBM) if i < raw_in else x for i, x in enumerate(operands)]
        return pl.pallas_call(
            kernel,
            in_specs=where[0] * raw_in + where[1] * (len(operands) - raw_in),
            out_specs=tuple(where[0] * raw_out + where[1] * (len(outs) - raw_out)),
            out_shape=outs,
            scratch_shapes=tuple(s if hasattr(s, "memory_space") else pltpu.VMEM(s, F32) for s in scratch) + extra,
            compiler_params=params(mib),
        )(*operands)

    return run


def per_device(phase, target_mask, deviation):
    ox, oy, oz = phase.shape
    nbox, nsub = lax.axis_size("boxes"), lax.axis_size("sub")
    swap_x, swap_y, far_x = exchanges(nbox), exchanges(nsub), exchanges(nbox, 2)
    nx, ny, nfar = len(swap_x), len(swap_y), len(far_x)
    pair_swap = [(0, 1), (1, 0)]

    def both(px, py):
        return [(a * nsub + c, b * nsub + d) for a, b in px for c, d in py]

    def traded(faces):
        out = []
        for e in range(nx):
            out.append(lax.ppermute(faces[e], "boxes", swap_x[e]))
        for f in range(ny):
            out.append(lax.ppermute(faces[nx + f], "sub", swap_y[f]))
        for e in range(nx):
            for f in range(ny):
                out.append(lax.ppermute(faces[nx + ny + e * ny + f], ("boxes", "sub"), both(swap_x[e], swap_y[f])))
        return out

    planes, rows = ox + 2 * XH, oy + YH * ny
    planes1, rows1 = planes // 2, rows // 2
    o2x, o2y = ox // 4, oy // 4
    planes2 = o2x + 2 * L2X
    rows2 = o2y * (ny + 1)

    box = spec((ox, oy, oz))
    faces = [spec((XH + GX, oy, oz))] * nx + [spec((2, ox, YH, oz))] * ny + [spec((DC + DG, YH, oz))] * (nx * ny)
    width, edge = (nx, GX, oy, oz), (ny, ox, YH, oz)
    faces = call(
        lambda *r: send_kernel(nx, ny, *r),
        faces,
        [(nx, XH, oy, oz), pltpu.VMEM(width, jnp.int32), width, edge, pltpu.VMEM(edge, jnp.int32), edge],
        raw_in=3,
        copies=3 * (nx + ny),
    )(phase, target_mask, deviation)
    got = traded(faces)
    phase, target_mask, deviation, _ = lax.optimization_barrier((phase, target_mask, deviation, faces))
    group = oz // ZW
    padded = (planes, rows, oz)
    fine = (planes, rows, 2 * oz)
    parted_box = in_hbm((ox, oy, 2 * oz))
    c, g, own, c2 = call(
        own_kernel,
        [parted_box, parted_box, spec((2, ox // group, oy, oz)), spec((o2x // 4 * o2y, oz))],
        [(ox, oy, oz), (ox, oy, oz), (oy, oz), (o2x, o2y, oz)],
    )(phase, target_mask, deviation)
    (strip,) = call(
        lambda *r: strip_kernel(nx, ny, *r), [spec((2 * planes // group, rows, oz))], [padded, padded]
    )(own, *got)
    strip = lax.ppermute(strip, "pair", pair_swap)
    halos = [(2 * XH, oy, 2 * oz)] * 2 + [(planes, rows - oy, 2 * oz)] * 2
    halos = call(lambda *r: join_kernel(nx, ny, *r), [in_vmem(h) for h in halos], mib=6)(*got)
    middle = (planes1, rows1, oz)
    small = (planes - 2 * SKIP, oy + ny * YN, 2 * oz)
    down = call(
        lambda *r: down_kernel(nx, ny, *r),
        [spec(small)] * FINE + [spec(middle)] * (KEPT - FINE) + [spec((o2x // 2 * o2y, oz))]
        + [spec((XH - 1, rows1, oz))] * nx,
        [fine] * FINE + [middle] * (KEPT - FINE) + [fine] * 5 + [middle, (4, rows, oz), (o2x, oy // 2, oz), (o2x, o2y, oz)],
        mib=48,
        raw_in=2,
        raw_out=KEPT,
        copies=KEPT + FINE * ny,
        more=4 * planes // group,
    )(c, g, *[held(h) for h in halos], strip, c2)
    kept, f2, sides = down[:KEPT], down[KEPT], down[KEPT + 1:]
    sheet = lax.all_gather(f2, ("sub", "pair")).reshape(-1, 2, o2x // 4, o2y, oz)
    first, sheet = lax.optimization_barrier((kept[:FINE], sheet))
    fine_up = call(lambda *r: face_kernel(ny, *r), [in_vmem(small)] * 7, mib=6, raw_in=FINE, copies=FINE)(*first)
    got = [sheet] + [lax.ppermute(sheet, "boxes", p) for p in swap_x]
    for e, p in enumerate(far_x):
        at = jnp.where(upward(lax.axis_index("boxes"), e, 2), o2x // 4 - 1, 0)
        got.append(lax.ppermute(lax.dynamic_index_in_dim(sheet, at, 2, keepdims=False), "boxes", p))
    got, sides, fine_up = lax.optimization_barrier((got, sides, fine_up))
    sides = [lax.ppermute(side, "boxes", p) for side, p in zip(sides, swap_x)]
    lowest = (planes2, rows2, oz)
    (add,) = call(
        lambda *r: bottom_kernel(nx, ny, nfar, *r),
        [in_vmem((planes1 // 2, rows1, oz))],
        [lowest] * 8 + [(planes1 // 2, 2 * (o2y + 8), oz)],
        mib=12,
    )(*got)
    return tuple(call(
        lambda *r: up_kernel(nx, ny, *r),
        [box, box],
        [(ox, oy, oz)] * 2 + [small, small, middle, middle, middle, (3, rows, oz)],
        mib=16,
        raw_out=2,
        copies=2 * (ox // XH),
    )(held(add), *[held(x) for x in fine_up], *sides, *kept[FINE:]))


def solution(mesh):
    where = P(("groups", "boxes"), "sub", "pair")
    return jax.shard_map(
        per_device,
        mesh=mesh,
        in_specs=(where, where, where),
        out_specs=(where, where),
        check_vma=False,
    )
```
